128 devices in a mesh: dp: 4 (over y), context: 8 (over z, core), tensor: 4 (over x).
Axes of the slice: x: 4, y: 4, z: 4, core: 2. Of those that a mesh axis runs over, the one named last changes fastest.
Arguments:
- tokens: bfloat16 [4, 1024, 2048], P('dp', 'context'), may hold values from -32 to 32
- routes: int32 [4, 1024, 8], P('dp', 'context'), may hold values from 0 to 63, all different within a row; in each aligned block of 128 rows (0 to 127, 128 to 255, ..., all dimensions but the last counted through in order) at most 32 rows name the same one
- attention_gain: bfloat16 [2048], P(('dp', 'context')), may hold values from 0.5 to 1.5
- query_matrix: bfloat16 [2048, 4096], P(('dp', 'context'), 'tensor'), may hold values from -0.125 to 0.125
- key_matrix: bfloat16 [2048, 512], P(('dp', 'context'), 'tensor'), may hold values from -0.125 to 0.125
- value_matrix: bfloat16 [2048, 512], P(('dp', 'context'), 'tensor'), may hold values from -0.125 to 0.125
- query_gain: bfloat16 [128], replicated, may hold values from 0.099609375 to 1.8984375
- key_gain: bfloat16 [128], replicated, may hold values from 0.099609375 to 1.8984375
- output_matrix: bfloat16 [4096, 2048], P('tensor', ('dp', 'context')), may hold values from -0.25 to 0.25
- experts_gain: bfloat16 [2048], P(('dp', 'context')), may hold values from 0.5 to 1.5
- router_matrix: bfloat16 [2048, 64], P(('dp', 'context')), may hold values from -0.0625 to 0.0625
- gate_weight: bfloat16 [64, 768, 2048], P(('dp', 'context'), 'tensor'), may hold values from -0.125 to 0.125
- up_weight: bfloat16 [64, 768, 2048], P(('dp', 'context'), 'tensor'), may hold values from -0.125 to 0.125
- down_weight: bfloat16 [64, 768, 2048], P(('dp', 'context'), 'tensor'), may hold values from -0.4375 to 0.4375
- cotangent: bfloat16 [4, 1024, 2048], P('dp', 'context'), may hold values from -10 to 10
Outputs:
- output: float32 [4, 1024, 2048], P('dp', 'context')
- tokens_grad: float32 [4, 1024, 2048], P('dp', 'context')
- attention_gain_grad: float32 [2048], P(('dp', 'context'))
- query_weight_grad: float32 [2048, 4096], P(('dp', 'context'), 'tensor')
- key_weight_grad: float32 [2048, 512], P(('dp', 'context'), 'tensor')
- value_weight_grad: float32 [2048, 512], P(('dp', 'context'), 'tensor')
- query_gain_grad: float32 [128], P(('dp', 'context'))
- key_gain_grad: float32 [128], P(('dp', 'context'))
- output_weight_grad: float32 [4096, 2048], P('tensor', ('dp', 'context'))
- experts_gain_grad: float32 [2048], P(('dp', 'context'))
- router_grad: float32 [2048, 64], P(('dp', 'context'))
- gate_grad: float32 [64, 768, 2048], P(('dp', 'context'), 'tensor')
- up_grad: float32 [64, 768, 2048], P(('dp', 'context'), 'tensor')
- down_grad: float32 [64, 768, 2048], P(('dp', 'context'), 'tensor')
The draws below stay inside these ranges and needn't reach their ends.
Inputs may be any that keep to these rules, and one draw needn't show every extreme that they name: `routes`: each token names 8 distinct experts. In each aligned block of 128 positions of a sequence no expert is named by more than 32 tokens, and in some block one expert is named by exactly 32.
All inputs are finite; a program needn't handle non-finite values.
Results may differ from the reference program's by a relative error of at most 0.017.
Values may be sent and summed in bfloat16 or wider, within the bound.
A program may use at most 256 MiB of HBM per device.

```python
import math
import jax
import jax.numpy as jnp
import numpy as np
from jax import lax

MODEL_DIMENSION = 2048
HQ = 32
KEY_VALUE_HEADS = 4
HEAD_DIMENSION = 128
FF = 768
TOP = 8
EXPERTS = 64
SEQ_LEN = 1024
SEQUENCES = 4
BLOCK = 128
CAP = 32
N_TENSOR = 4


def draw_tokens(key, part):
    key = jax.random.fold_in(key, 11)
    streams = jax.random.split(key, 3)
    entries = jax.random.truncated_normal(streams[0], -5.0, 5.0, (SEQUENCES, SEQ_LEN, MODEL_DIMENSION), jnp.float32)
    row_scale = jnp.exp(jax.random.uniform(streams[1], (SEQUENCES, SEQ_LEN, 1), jnp.float32, -1.15, 1.15))
    column_scale = jnp.exp(jax.random.uniform(streams[2], (1, 1, MODEL_DIMENSION), jnp.float32, -0.7, 0.7))
    return (entries * row_scale * column_scale).astype(jnp.bfloat16)


def draw_cotangent(key, part):
    key = jax.random.fold_in(key, 23)
    row_count = SEQUENCES * SEQ_LEN
    position = jnp.arange(row_count, dtype=jnp.float32).reshape(SEQUENCES, SEQ_LEN, 1) / max(row_count - 1, 1)
    rising = 0.6 * jnp.exp(position * 1.1)
    entries = jax.random.truncated_normal(key, -5.0, 5.0, (SEQUENCES, SEQ_LEN, MODEL_DIMENSION), jnp.float32)
    return (entries * rising).astype(jnp.bfloat16)


def steps_of(stream_key, extent, cuts, least, top_value):
    level = 1.0
    for dim, parts in cuts:
        steps = jax.random.uniform(jax.random.fold_in(jax.random.fold_in(stream_key, 6), dim), (parts,), jnp.float32, least / len(cuts), top_value / len(cuts))
        level = level * jnp.repeat(jnp.exp(steps), extent[dim] // parts).reshape((-1,) + (1,) * (len(extent) - 1 - dim))
    return level


def routed_block(key, own, number, rows, number_of, top, most, skew):
    order = jax.random.permutation(key, number_of)
    heavy_load, ordinary = shares(number_of, rows * top, most, skew, True), shares(number_of, rows * top, most, skew, False)
    places = jnp.arange(number_of)

    def named(lengths, offset_by):
        used = int((lengths > 0).sum())
        fixed = max(1, used // 4)
        moved = fixed + (places - fixed + offset_by * (used - fixed)) % max(1, number_of - fixed)
        return jnp.zeros((number_of,), jnp.int32).at[order[jnp.where(places < fixed, places, moved)]].set(jnp.asarray(lengths, jnp.int32))

    lengths = jnp.where(number % 4 == 0, named(heavy_load, number // 4), named(ordinary, number - number // 4 - 1))
    mixed = jax.random.permutation(jax.random.fold_in(own, 3), number_of)
    donor, sink = mixed[0:number_of // 2 * 2:2], mixed[1:number_of // 2 * 2:2]
    slack = jnp.minimum(lengths[donor] - 1, most - lengths[sink]) // 2
    slack = jnp.where((donor == order[0]) | (sink == order[0]) | (lengths[sink] == 0), 0, jnp.maximum(slack, 0))
    moved = jax.random.randint(jax.random.fold_in(own, 4), (number_of // 2,), 0, 1 << 20) % (slack + 1)
    lengths = lengths.at[donor].add(-moved).at[sink].add(moved)
    items = jnp.searchsorted(jnp.cumsum(lengths), jnp.arange(rows * top), side="right").astype(jnp.int32)
    table = items.reshape(top, rows).T
    table = table[jax.random.permutation(jax.random.fold_in(own, 1), rows)]
    offset_by = jax.random.randint(jax.random.fold_in(own, 2), (rows, 1), 0, top)
    return jnp.take_along_axis(table, (jnp.arange(top)[None, :] + offset_by) % top, axis=1)


def shares(count, total, bound, slope, full):
    loads = [(1 << 20) // math.isqrt(standing ** slope) + 1 for standing in range(1, count + 1)]
    largest = bound if full else min(bound, max(-(-total // count), total * loads[0] // sum(loads)))
    least = 1 if total - largest >= count - 1 else 0
    given, rest = [largest] + [least] * (count - 1), total - largest - least * (count - 1)
    while rest > 0:
        movable = [i for i in range(1, count) if given[i] < largest] or [i for i in range(1, count) if given[i] < bound]
        mass, left = sum([loads[i] for i in movable]), rest
        for i in movable:
            more = min(bound - given[i], max(1, left * loads[i] // mass), rest)
            given[i] = given[i] + more
            rest = rest - more
    return np.array(given)


def centred(stream_key, dims, spread, most, cuts=(), held_as=jnp.bfloat16):
    level = steps_of(stream_key, dims, cuts, -0.22, 0.18) if cuts else 1.0
    values = jax.random.normal(stream_key, dims, jnp.float32) * spread * level
    return jnp.minimum(jnp.maximum(values, -most), most).astype(held_as)


def setup_inputs(seed: int = 0) -> dict:
    arg_keys = jax.random.split(jax.random.key(seed), 16)
    tokens = draw_tokens(jax.random.fold_in(arg_keys[15], 71), 0)
    routes_keys = jax.random.split(jax.random.fold_in(arg_keys[1], 1), SEQUENCES * SEQ_LEN // BLOCK)
    routes_turns = jax.random.permutation(jax.random.fold_in(arg_keys[1], 3), SEQUENCES * SEQ_LEN // BLOCK)
    routes = jax.vmap(lambda own, number: routed_block(jax.random.fold_in(arg_keys[1], 2), own, number, BLOCK, EXPERTS, TOP, CAP, 2))(routes_keys, routes_turns).reshape((SEQUENCES, SEQ_LEN, TOP))
    attention_gain = jnp.clip(1.0 + 0.1 * jax.random.normal(arg_keys[2], (MODEL_DIMENSION,), jnp.float32), 0.5, 1.5).astype(jnp.bfloat16)
    query_matrix = centred(arg_keys[3], (MODEL_DIMENSION, HQ * HEAD_DIMENSION), MODEL_DIMENSION ** -0.5, 0.125, ((0, 32), (1, 4)))
    key_matrix = centred(arg_keys[4], (MODEL_DIMENSION, KEY_VALUE_HEADS * HEAD_DIMENSION), MODEL_DIMENSION ** -0.5, 0.125, ((0, 32), (1, 4)))
    value_matrix = centred(arg_keys[5], (MODEL_DIMENSION, KEY_VALUE_HEADS * HEAD_DIMENSION), MODEL_DIMENSION ** -0.5, 0.125, ((0, 32), (1, 4)))
    query_gain = jnp.clip(1.0 + 0.18 * jax.random.normal(arg_keys[6], (HEAD_DIMENSION,), jnp.float32), 0.099609375, 1.8984375).astype(jnp.bfloat16)
    key_gain = jnp.clip(1.0 + 0.18 * jax.random.normal(arg_keys[7], (HEAD_DIMENSION,), jnp.float32), 0.099609375, 1.8984375).astype(jnp.bfloat16)
    output_matrix = centred(arg_keys[8], (HQ * HEAD_DIMENSION, MODEL_DIMENSION), (HQ * HEAD_DIMENSION // 8) ** -0.5, 0.25, ((0, 4), (1, 32)))
    experts_gain = jnp.clip(1.0 + 0.1 * jax.random.normal(arg_keys[9], (MODEL_DIMENSION,), jnp.float32), 0.5, 1.5).astype(jnp.bfloat16)
    router_matrix = centred(arg_keys[10], (MODEL_DIMENSION, EXPERTS), (4 * MODEL_DIMENSION) ** -0.5, 0.0625, ((0, 32),))
    gate_weight = centred(arg_keys[11], (EXPERTS, FF, MODEL_DIMENSION), MODEL_DIMENSION ** -0.5, 0.125, ((0, 32), (1, 4)))
    up_weight = centred(arg_keys[12], (EXPERTS, FF, MODEL_DIMENSION), MODEL_DIMENSION ** -0.5, 0.125, ((0, 32), (1, 4)))
    down_weight = centred(arg_keys[13], (EXPERTS, FF, MODEL_DIMENSION), (FF // 4) ** -0.5, 0.4375, ((0, 32), (1, 4)))
    cotangent = draw_cotangent(jax.random.fold_in(arg_keys[15], 71), 0)
    return dict(tokens=tokens, routes=routes, attention_gain=attention_gain, query_matrix=query_matrix, key_matrix=key_matrix, value_matrix=value_matrix, query_gain=query_gain, key_gain=key_gain, output_matrix=output_matrix, experts_gain=experts_gain, router_matrix=router_matrix, gate_weight=gate_weight, up_weight=up_weight, down_weight=down_weight, cotangent=cotangent)


EPSILON = 1e-06
THETA = 1000000.0

@jax.custom_vjp
def low(v):
    return lax.optimization_barrier(v.astype(jnp.bfloat16)).astype(jnp.float32)

@jax.custom_vjp
def low_back(v):
    return v

def low_keep(v):
    return (low(v), None)

def low_pass(kept, grad):
    return (grad,)

def back_keep(v):
    return (v, None)

def back_low(kept, grad):
    return (low(grad),)
low.defvjp(low_keep, low_pass)
low_back.defvjp(back_keep, back_low)

def rms_scale(values, gain_vector):
    mean_square = lax.optimization_barrier(jnp.mean(values * values, axis=-1, keepdims=True))
    return values * lax.rsqrt(mean_square + EPSILON) * gain_vector

def rotary_tables(positions, head_size):
    half_size = head_size // 2
    frequency = jnp.exp(jnp.arange(half_size, dtype=jnp.float32) * (-2.0 * math.log(THETA) / head_size))
    angles = positions[:, None] * frequency[None, :]
    return (jnp.cos(angles)[:, None, :], jnp.sin(angles)[:, None, :])

def rotate(values, cosine_table, sine_table):
    half_size = values.shape[-1] // 2
    first_half = values[..., :half_size]
    second_half = values[..., half_size:]
    return jnp.concatenate([first_half * cosine_table - second_half * sine_table, second_half * cosine_table + first_half * sine_table], axis=-1)

def attend(pieces):
    queries, keys, values = pieces
    length, head_count, head_size = queries.shape
    key_heads = keys.shape[1]
    grouped = queries.reshape(length, key_heads, head_count // key_heads, head_size)
    raw_scores = low_back(jnp.einsum('qkgd,lkd->kgql', grouped, keys, precision=lax.Precision.HIGHEST))
    scores = raw_scores * head_size ** (-0.5)
    positions = jnp.arange(length, dtype=jnp.int32)
    allowed = positions[None, :] <= positions[:, None]
    masked = jnp.where(allowed, scores, -1e+30)
    highest = lax.optimization_barrier(jnp.max(masked, axis=-1, keepdims=True))
    exponent = jnp.exp(masked - highest)
    probabilities = exponent / lax.optimization_barrier(jnp.sum(exponent, axis=-1, keepdims=True))
    attention_mixed = jnp.einsum('kgql,lkd->qkgd', low(probabilities), values, precision=lax.Precision.HIGHEST)
    return attention_mixed.reshape(length, head_count, head_size)

def expert_block(pieces):
    rows, gate_rows, up_rows, down_rows = pieces
    exact_compute = lax.Precision.HIGHEST
    part_size = gate_rows.shape[0] // N_TENSOR
    combined = jnp.zeros(rows.shape, jnp.float32)
    for slice_index in range(N_TENSOR):
        start_row = slice_index * part_size
        inputs = low_back(rows)
        gate_hidden = low_back(jnp.dot(inputs, gate_rows[start_row:start_row + part_size].T, precision=exact_compute, preferred_element_type=jnp.float32))
        up_hidden = low_back(jnp.dot(inputs, up_rows[start_row:start_row + part_size].T, precision=exact_compute, preferred_element_type=jnp.float32))
        inner = low(gate_hidden * jax.nn.sigmoid(gate_hidden) * up_hidden)
        combined = combined + low(low_back(jnp.dot(inner, down_rows[start_row:start_row + part_size], precision=exact_compute, preferred_element_type=jnp.float32)))
    return combined

def slot_tables(routes):
    sequences, length, top_count = routes.shape
    blocks = sequences * (length // BLOCK)
    flat_routes = routes.reshape(blocks, BLOCK * top_count).astype(jnp.int32)
    matches = (flat_routes[:, :, None] == jnp.arange(EXPERTS, dtype=jnp.int32)[None, None, :]).astype(jnp.int32)
    slot_rank = lax.optimization_barrier(jnp.sum((jnp.cumsum(matches, axis=1).astype(jnp.int32) - 1) * matches, axis=-1)).astype(jnp.int32)
    block_index = jnp.arange(blocks, dtype=jnp.int32)[:, None]
    destination = flat_routes * (blocks * CAP) + block_index * CAP + slot_rank
    return (destination.reshape(sequences, length, top_count).astype(jnp.int32), blocks * CAP)

def full_layer(tokens, attention_gain, query_matrix, key_matrix, value_matrix, query_gain, key_gain, output_matrix, experts_gain, router_matrix, gate_weight, up_weight, down_weight, routes):
    exact_compute = lax.Precision.HIGHEST
    sequences, length, model_width = tokens.shape
    head_size = query_gain.shape[0]
    query_heads = query_matrix.shape[1] // head_size
    key_heads = key_matrix.shape[1] // head_size
    normed_input = low(rms_scale(tokens, attention_gain))
    query_unrotated = low_back(jnp.einsum('ypn,ni->ypi', normed_input, query_matrix, precision=exact_compute))
    key_unrotated = low_back(jnp.einsum('ypn,ni->ypi', normed_input, key_matrix, precision=exact_compute))
    value_projected = low_back(jnp.einsum('ypn,ni->ypi', normed_input, value_matrix, precision=exact_compute))
    cosine_table, sine_table = rotary_tables(jnp.arange(length, dtype=jnp.float32), head_size)
    queries = low(rotate(rms_scale(query_unrotated.reshape(sequences, length, query_heads, head_size), query_gain), cosine_table, sine_table))
    keys = low(rotate(rms_scale(key_unrotated.reshape(sequences, length, key_heads, head_size), key_gain), cosine_table, sine_table))
    values = low(value_projected.reshape(sequences, length, key_heads, head_size))
    attention_mixed = lax.map(jax.checkpoint(attend), (queries, keys, values))
    attention_mixed = low_back(low(attention_mixed.reshape(sequences, length, query_heads * head_size)))
    hidden_state = tokens + low_back(jnp.einsum('nto,oh->nth', attention_mixed, output_matrix, precision=exact_compute))
    routed_tokens = low(rms_scale(hidden_state, experts_gain))
    router_logits = low_back(jnp.einsum('cfg,gu->cfu', routed_tokens, router_matrix, precision=exact_compute))
    chosen = jnp.take_along_axis(router_logits, routes, axis=-1)
    top_logit = lax.optimization_barrier(jnp.max(chosen, axis=-1, keepdims=True))
    gate_terms = jnp.exp(chosen - top_logit)
    gate_values = gate_terms / lax.optimization_barrier(jnp.sum(gate_terms, axis=-1, keepdims=True))
    destination, rows_each = slot_tables(routes)
    top_count = routes.shape[2]
    pair_count = sequences * length * top_count
    slot_pair = jnp.full((EXPERTS * rows_each,), pair_count, jnp.int32).at[destination.reshape(-1)].set(jnp.arange(pair_count, dtype=jnp.int32))
    slot_token = jnp.where(slot_pair < pair_count, slot_pair // top_count, sequences * length).astype(jnp.int32)
    padded_rows = jnp.concatenate([routed_tokens.reshape(sequences * length, model_width), jnp.zeros((1, model_width), jnp.float32)], axis=0)
    expert_rows = jnp.take(padded_rows, slot_token, axis=0).reshape(EXPERTS, rows_each, model_width)
    expert_out = lax.map(jax.checkpoint(expert_block), (expert_rows, gate_weight, up_weight, down_weight))
    flat_out = expert_out.reshape(EXPERTS * rows_each, model_width)
    experts_part = jnp.zeros((sequences, length, model_width), jnp.float32)
    for pick_index in range(top_count):
        experts_part = experts_part + gate_values[:, :, pick_index:pick_index + 1] * jnp.take(flat_out, destination[:, :, pick_index], axis=0)
    return hidden_state + experts_part

def reference(tokens, routes, attention_gain, query_matrix, key_matrix, value_matrix, query_gain, key_gain, output_matrix, experts_gain, router_matrix, gate_weight, up_weight, down_weight, cotangent):
    floats = [argument.astype(jnp.float32) for argument in (tokens, attention_gain, query_matrix, key_matrix, value_matrix, query_gain, key_gain, output_matrix, experts_gain, router_matrix, gate_weight, up_weight, down_weight)]

    def forward(*values):
        return full_layer(*values, routes)
    output, pullback = jax.vjp(forward, *floats)
    gradients = pullback(cotangent.astype(jnp.float32))
    return (output, gradients[0], gradients[1], gradients[2], gradients[3], gradients[4], gradients[5], gradients[6], gradients[7], gradients[8], gradients[9], gradients[10], gradients[11], gradients[12])
```

```python
import functools
import math

import jax
import jax.numpy as jnp
from jax import lax
from jax.experimental import pallas as pl
from jax.experimental.pallas import tpu as pltpu
from jax.sharding import PartitionSpec as P

MESH = pl.DeviceIdType.MESH
F32 = jnp.float32
BF16 = jnp.bfloat16
MIB = 1 << 20


class Links:
    def __init__(self, send_sem, recv_sem):
        self.send_sem, self.recv_sem = send_sem, recv_sem
        self.copies = []

    def send(self, source, target, device, arriving):
        index = len(self.copies)
        copy = pltpu.make_async_remote_copy(
            src_ref=source,
            dst_ref=target,
            send_sem=self.send_sem.at[index],
            recv_sem=self.recv_sem.at[index],
            device_id=device,
            device_id_type=MESH,
        )
        copy.start()
        landing = pltpu.make_async_remote_copy(
            src_ref=arriving,
            dst_ref=arriving,
            send_sem=self.send_sem.at[index],
            recv_sem=self.recv_sem.at[index],
            device_id=device,
            device_id_type=MESH,
        )
        self.copies.append(copy)
        return landing

    def finish(self):
        for copy in self.copies:
            copy.wait_send()


def greet(devices):
    barrier = pltpu.get_barrier_semaphore()
    for device in devices:
        pl.semaphore_signal(barrier, inc=1, device_id=device, device_id_type=MESH)
    pl.semaphore_wait(barrier, len(devices))


def plane_place():
    y = lax.axis_index("dp")
    position = lax.axis_index("context")
    z = position // 2
    core = position - 2 * z

    def device(step):
        return {"dp": (y + step[0]) % 4, "context": ((z + step[1]) % 4) * 2 + core}

    def slot(step, other=False):
        at = 1 - core if other else core
        return ((y + step[0]) % 4) * 8 + ((z + step[1]) % 4) * 2 + at

    sibling = {"context": 2 * z + 1 - core}
    return device, slot, sibling


def along(first, second, order):
    return (first, second) if order == 0 else (second, first)


NEAR = ((1, 0), (-1, 0), (0, 1), (0, -1))


def gather_body(count, *refs):
    mine, whole = refs[:count], refs[count : 2 * count]
    send_sem, recv_sem, own_sem = refs[2 * count :]
    device, slot, sibling = plane_place()
    greet([device(step) for step in NEAR] + [sibling])
    links = Links(send_sem, recv_sem)
    jobs = [(a, order) for a in range(count) for order in range(2)]

    def rows_of(a, order, part):
        rows = mine[a].shape[0]
        start, size = order * (rows // 2), rows // 2
        if part == 2:
            return 0, rows
        if part == 1:
            return start + size // 2, size // 2
        if part == 0:
            return start, size // 2
        return start, size

    def region(a, order, place, part, other=False):
        rows = mine[a].shape[0]
        start, size = rows_of(a, order, part)
        base = pl.multiple_of(slot(along(*place, order), other) * rows + start, 16)
        return whole[a].at[pl.ds(base, size)]

    def push(a, order, place, part, axis, sign):
        step = along(sign, 0, order) if axis == 0 else along(0, sign, order)
        source = region(a, order, place, part)
        if place == (0, 0):
            start, size = rows_of(a, order, part)
            source = mine[a].at[pl.ds(start, size)]
        came = (place[0] - sign, place[1]) if axis == 0 else (place[0], place[1] - sign)
        return links.send(
            source, region(a, order, place, part), device(step), region(a, order, came, part)
        )

    beside = []

    def share(a, order, place, part=None):
        source = mine[a] if part == 2 else region(a, order, place, part)
        beside.append(
            links.send(
                source,
                region(a, order, place, part),
                sibling,
                region(a, order, place, part, True),
            )
        )

    own = []
    for a in range(count):
        copy = pltpu.make_async_copy(mine[a], region(a, 0, (0, 0), 2), own_sem.at[a])
        copy.start()
        own.append(copy)
    got = {}
    for a, order in jobs:
        for sign in (1, -1):
            got[a, order, sign] = push(a, order, (0, 0), None, 0, sign)
    for a, order in jobs:
        for sign in (1, -1):
            got[a, order, 0, sign] = push(a, order, (0, 0), None, 1, sign)
    for a in range(count):
        share(a, 0, (0, 0), 2)
    for a, order in jobs:
        for sign in (1, -1):
            got[a, order, sign].wait_recv()
            got[a, order, "far", sign] = push(
                a, order, (-sign, 0), 0 if sign == 1 else 1, 0, sign
            )
        for sign in (1, -1):
            for way in (1, -1):
                got[a, order, -sign, way] = push(a, order, (-sign, 0), None, 1, way)
            share(a, order, (-sign, 0))
    for a, order in jobs:
        for sign in (1, -1):
            got[a, order, "far", sign].wait_recv()
        for way in (1, -1):
            got[a, order, 2, way] = push(a, order, (2, 0), None, 1, way)
        share(a, order, (2, 0))
    for i in (0, 1, -1, 2):
        for a, order in jobs:
            for way in (1, -1):
                got[a, order, i, way].wait_recv()
                got[a, order, i, "far", way] = push(
                    a, order, (i, -way), 0 if way == 1 else 1, 1, way
                )
                share(a, order, (i, -way))
    for i in (0, 1, -1, 2):
        for a, order in jobs:
            for way in (1, -1):
                got[a, order, i, "far", way].wait_recv()
            share(a, order, (i, 2))
    for copy in beside:
        copy.wait_recv()
    for copy in own:
        copy.wait()
    links.finish()


def gather_copies(count):
    return count * (2 * 20 + 1 + 2 * 15)


def plane_gather(arrays, collective_id):
    count = len(arrays)
    copies = gather_copies(count)
    return pl.pallas_call(
        functools.partial(gather_body, count),
        out_shape=[
            jax.ShapeDtypeStruct((32 * a.shape[0],) + a.shape[1:], a.dtype) for a in arrays
        ],
        in_specs=[pl.BlockSpec(memory_space=pl.ANY)] * count,
        out_specs=[pl.BlockSpec(memory_space=pl.ANY)] * count,
        scratch_shapes=[
            pltpu.SemaphoreType.DMA((copies,)),
            pltpu.SemaphoreType.DMA((copies,)),
            pltpu.SemaphoreType.DMA((count,)),
        ],
        compiler_params=pltpu.CompilerParams(
            collective_id=collective_id, has_side_effects=True, vmem_limit_bytes=16 * MIB
        ),
    )(*arrays)


def add_rows(target, sources, offset, size, chunk=16):
    def step(k, carry):
        base = pl.multiple_of(k * chunk, chunk)
        at = pl.ds(offset + base, chunk)
        total = target[at].astype(F32)
        for source, start in sources:
            total = total + source[pl.ds(start + base, chunk)].astype(F32)
        target[at] = total.astype(target.dtype)
        return carry

    lax.fori_loop(0, size // chunk, step, 0)


SLOTS = (
    (2, 2), (1, 2), (2, 1), (-1, 2), (2, -1), (0, 2), (2, 0),
    (1, 1), (1, -1), (-1, 1), (-1, -1), (0, 1), (1, 0), (0, -1), (-1, 0), (0, 0),
)


def scatter_body(rows, part_ref, out_ref, held, near, landed, send_sem, recv_sem, own_sem):
    device, slot, sibling = plane_place()
    greet([device(step) for step in NEAR] + [sibling])
    links = Links(send_sem, recv_sem)
    half, quarter = rows // 2, rows // 4
    index = {place: k for k, place in enumerate(SLOTS)}

    def base(place):
        return index[place] * rows

    loads, shares = {}, {}
    for k, place in enumerate(SLOTS):
        copy = pltpu.make_async_copy(
            part_ref.at[pl.ds(pl.multiple_of(slot(place) * rows, 16), rows)],
            held.at[pl.ds(base(place), rows)],
            own_sem.at[k],
        )
        copy.start()
        loads[place] = copy
        here = near.at[pl.ds(base(place), rows)]
        shares[place] = links.send(
            part_ref.at[pl.ds(pl.multiple_of(slot(place, True) * rows, 16), rows)],
            here,
            sibling,
            here,
        )
    merged = set()

    def ready(order, place):
        place = along(*place, order)
        if place not in merged:
            merged.add(place)
            loads[place].wait()
            shares[place].wait_recv()
            add_rows(held, [(near, base(place))], base(place), rows)
        return base(place) + order * half

    room = [0]

    def push(start, size, order, axis, sign):
        step = along(sign, 0, order) if axis == 0 else along(0, sign, order)
        at = room[0]
        room[0] += size
        here = landed.at[pl.ds(at, size)]
        return links.send(held.at[pl.ds(start, size)], here, device(step), here), at

    got = {}

    def reduce_ring(key, order, axis, places, stage):
        opposite, plus, minus, mine = places
        if stage == 0:
            start = ready(order, opposite)
            got[key, 0] = push(start, quarter, order, axis, 1)
            got[key, 1] = push(start + quarter, quarter, order, axis, -1)
        if stage == 1:
            start = ready(order, plus)
            copy, at = got[key, 0]
            copy.wait_recv()
            add_rows(held, [(landed, at)], start, quarter)
            got[key, 2] = push(start, half, order, axis, 1)
            start = ready(order, minus)
            copy, at = got[key, 1]
            copy.wait_recv()
            add_rows(held, [(landed, at)], start + quarter, quarter)
            got[key, 3] = push(start, half, order, axis, -1)
        if stage == 2:
            start = ready(order, mine)
            sources = []
            for k in (2, 3):
                copy, at = got[key, k]
                copy.wait_recv()
                sources.append((landed, at))
            if axis == 1:
                add_rows(held, sources, start, half)
            else:
                for k in range(half // 16):
                    total = held[pl.ds(start + 16 * k, 16)].astype(F32)
                    for source, at in sources:
                        total = total + source[pl.ds(at + 16 * k, 16)].astype(F32)
                    out_ref[pl.ds(order * half + 16 * k, 16)] = total

    def ring(i, order, stage):
        reduce_ring((order, i), order, 1, [(i, j) for j in (2, 1, -1, 0)], stage)

    def last(order, stage):
        reduce_ring((order, "last"), order, 0, [(i, 0) for i in (2, 1, -1, 0)], stage)

    for i in (2, 1, -1, 0):
        for order in range(2):
            ring(i, order, 0)
    for i in (2, 1, -1, 0):
        for order in range(2):
            ring(i, order, 1)
    for order in range(2):
        ring(2, order, 2)
        last(order, 0)
    for order in range(2):
        ring(1, order, 2)
        ring(-1, order, 2)
        last(order, 1)
    for order in range(2):
        ring(0, order, 2)
        last(order, 2)
    links.finish()


def plane_scatter(part, collective_id):
    rows, columns = part.shape[0] // 32, part.shape[1]
    copies = 16 + 2 * 20
    vmem = (2 * 16 + 15) * rows * columns * 2 + 2 * rows * columns * 4 + 4 * MIB
    return pl.pallas_call(
        functools.partial(scatter_body, rows),
        out_shape=jax.ShapeDtypeStruct((rows, columns), F32),
        in_specs=[pl.BlockSpec(memory_space=pl.ANY)],
        out_specs=pl.BlockSpec(memory_space=pltpu.VMEM),
        scratch_shapes=[
            pltpu.VMEM((16 * rows, columns), BF16),
            pltpu.VMEM((16 * rows, columns), BF16),
            pltpu.VMEM((15 * rows, columns), BF16),
            pltpu.SemaphoreType.DMA((copies,)),
            pltpu.SemaphoreType.DMA((copies,)),
            pltpu.SemaphoreType.DMA((16,)),
        ],
        compiler_params=pltpu.CompilerParams(
            collective_id=collective_id, has_side_effects=True, vmem_limit_bytes=vmem
        ),
    )(part)


def tensor_sum_body(count, *refs):
    parts, outs = refs[:count], refs[count : 2 * count]
    held, landed = refs[2 * count : 3 * count], refs[3 * count : 4 * count]
    send_sem, recv_sem = refs[4 * count :]
    x = lax.axis_index("tensor")

    def device(step):
        return {"tensor": (x + step) % 4}

    greet([device(1), device(-1)])
    links = Links(send_sem, recv_sem)
    got = {}

    def rows(a, step, start, size):
        quarter = parts[a].shape[0] // 4
        return pl.ds(pl.multiple_of(((x + step) % 4) * quarter + start, 16), size)

    def push(a, source, sign, at, size):
        here = landed[a].at[pl.ds(at, size)]
        return links.send(source, here, device(sign), here)

    for a in range(count):
        held[a][...] = parts[a][...].astype(BF16)
        quarter = parts[a].shape[0] // 4
        eighth = quarter // 2
        got[a, 0] = push(a, held[a].at[rows(a, 2, 0, eighth)], 1, 0, eighth)
        got[a, 1] = push(a, held[a].at[rows(a, 2, eighth, eighth)], -1, eighth, eighth)
    for a in range(count):
        quarter = parts[a].shape[0] // 4
        eighth = quarter // 2
        for k, sign in enumerate((1, -1)):
            got[a, k].wait_recv()
            at = rows(a, sign, k * eighth, eighth)
            total = parts[a][at].astype(F32) + landed[a][k * eighth : (k + 1) * eighth].astype(F32)
            held[a][at] = total.astype(BF16)
            got[a, 2 + k] = push(
                a, held[a].at[rows(a, sign, 0, quarter)], sign, (k + 1) * quarter, quarter
            )
    for a in range(count):
        quarter = parts[a].shape[0] // 4
        got[a, 2].wait_recv()
        got[a, 3].wait_recv()
        mine = rows(a, 0, 0, quarter)
        total = parts[a][mine].astype(F32)
        total = total + landed[a][quarter : 2 * quarter].astype(F32)
        total = total + landed[a][2 * quarter : 3 * quarter].astype(F32)
        outs[a][mine] = total.astype(BF16)
        for k, sign in enumerate((1, -1)):
            got[a, 4 + k] = links.send(
                outs[a].at[mine], outs[a].at[mine], device(sign),
                outs[a].at[rows(a, -sign, 0, quarter)],
            )
    for a in range(count):
        quarter = parts[a].shape[0] // 4
        eighth = quarter // 2
        for k, sign in enumerate((1, -1)):
            got[a, 4 + k].wait_recv()
            at = rows(a, -sign, k * eighth, eighth)
            got[a, 6 + k] = links.send(
                outs[a].at[at], outs[a].at[at], device(sign),
                outs[a].at[rows(a, 2, k * eighth, eighth)],
            )
    for a in range(count):
        got[a, 6].wait_recv()
        got[a, 7].wait_recv()
    links.finish()


def tensor_sum(arrays, collective_id):
    count = len(arrays)
    spec = pl.BlockSpec(memory_space=pltpu.VMEM)
    return pl.pallas_call(
        functools.partial(tensor_sum_body, count),
        out_shape=[jax.ShapeDtypeStruct(a.shape, BF16) for a in arrays],
        in_specs=[spec] * count,
        out_specs=[spec] * count,
        scratch_shapes=[pltpu.VMEM(a.shape, BF16) for a in arrays]
        + [pltpu.VMEM((a.shape[0] * 3 // 4, a.shape[1]), BF16) for a in arrays]
        + [pltpu.SemaphoreType.DMA((8 * count,)), pltpu.SemaphoreType.DMA((8 * count,))],
        compiler_params=pltpu.CompilerParams(
            collective_id=collective_id, has_side_effects=True, vmem_limit_bytes=32 * MIB
        ),
    )(*arrays)


def context_place():
    position = lax.axis_index("context")

    def device(step):
        return {"context": (position + step) % 8}

    return position, device


def context_gather_body(mine, whole, send_sem, recv_sem, own_sem):
    position, device = context_place()
    rows = mine.shape[0]
    greet([device(step) for step in range(1, 8)])
    links = Links(send_sem, recv_sem)

    def region(step):
        return whole.at[pl.ds(pl.multiple_of(((position + step) % 8) * rows, 16), rows)]

    own = pltpu.make_async_copy(mine, region(0), own_sem)
    own.start()
    got = [links.send(mine, region(0), device(step), region(-step)) for step in range(1, 8)]
    for copy in got:
        copy.wait_recv()
    own.wait()
    links.finish()


def context_gather(array, collective_id):
    spec = pl.BlockSpec(memory_space=pltpu.VMEM)
    return pl.pallas_call(
        context_gather_body,
        out_shape=jax.ShapeDtypeStruct((8 * array.shape[0],) + array.shape[1:], array.dtype),
        in_specs=[spec],
        out_specs=spec,
        scratch_shapes=[
            pltpu.SemaphoreType.DMA((7,)),
            pltpu.SemaphoreType.DMA((7,)),
            pltpu.SemaphoreType.DMA,
        ],
        compiler_params=pltpu.CompilerParams(collective_id=collective_id, has_side_effects=True),
    )(array)


def context_scatter_body(part, out, landed, send_sem, recv_sem):
    position, device = context_place()
    rows = out.shape[0]
    greet([device(step) for step in range(1, 8)])
    links = Links(send_sem, recv_sem)

    def region(step):
        return pl.ds(pl.multiple_of(((position + step) % 8) * rows, 16), rows)

    got = []
    for step in range(1, 8):
        here = landed.at[pl.ds((step - 1) * rows, rows)]
        got.append(links.send(part.at[region(step)], here, device(step), here))
    total = part[region(0)].astype(F32)
    for k, copy in enumerate(got):
        copy.wait_recv()
        total = total + landed[k * rows : (k + 1) * rows].astype(F32)
    out[...] = total
    links.finish()


def context_scatter(part, collective_id):
    rows, columns = part.shape[0] // 8, part.shape[1]
    spec = pl.BlockSpec(memory_space=pltpu.VMEM)
    return pl.pallas_call(
        context_scatter_body,
        out_shape=jax.ShapeDtypeStruct((rows, columns), F32),
        in_specs=[spec],
        out_specs=spec,
        scratch_shapes=[
            pltpu.VMEM((7 * rows, columns), part.dtype),
            pltpu.SemaphoreType.DMA((7,)),
            pltpu.SemaphoreType.DMA((7,)),
        ],
        compiler_params=pltpu.CompilerParams(
            collective_id=collective_id, has_side_effects=True, vmem_limit_bytes=24 * MIB
        ),
    )(part)


def dot(a, b, contract):
    return lax.dot_general(a, b, (contract, ((), ())), preferred_element_type=F32)


PAIR = 256
STEP = 512
CAPACITY = 32


def experts_body(
    steps, width, x_ref, c_ref, row_ref, column_ref, gate_ref, lane_ref, wg_ref, wu_ref, wd_ref,
    out_ref, back_ref, gg_ref, gu_ref, gd_ref, rows, pairs, inner, slope_g, slope_u,
):
    step = pl.program_id(0)
    local = wg_ref.shape[0]
    per_pair = 2 * CAPACITY
    pair_count = STEP // PAIR
    per_step = pair_count * per_pair

    @pl.when(step < steps)
    def _():
        base = pl.multiple_of(step * per_step, per_step)
        weights = [[None] * pair_count for _ in range(local)]
        for p in range(pair_count):
            tokens = pl.ds(p * PAIR, PAIR)
            picks = []
            slots = lax.broadcasted_iota(jnp.int32, (per_pair, PAIR), 0)
            for e in range(local):
                match = slots == row_ref[e : e + 1, tokens]
                weights[e][p] = jnp.sum(
                    jnp.where(match, gate_ref[e : e + 1, tokens], 0.0), axis=1, keepdims=True
                )
                picks.append(jnp.where(match, 1.0, 0.0).astype(BF16))
            pick = jnp.concatenate(picks, axis=0)
            taken = dot(pick, x_ref[tokens, :width], ((1,), (0,))).astype(BF16)
            given = dot(pick, c_ref[tokens, :width], ((1,), (0,)))
            for e in range(local):
                at = pl.ds(base + p * per_pair, per_pair)
                mine = slice(e * per_pair, (e + 1) * per_pair)
                rows[e, at] = taken[mine]
                pairs[e, at] = (weights[e][p] * given[mine]).astype(BF16)
        sent, returned = [], []
        for e in range(local):
            at = pl.ds(base, per_step)
            weight = jnp.concatenate(weights[e], axis=0)
            taken, given = rows[e, at], pairs[e, at]
            gate = dot(taken, wg_ref[e], ((1,), (1,)))
            up = dot(taken, wu_ref[e], ((1,), (1,)))
            grad_inner = dot(given, wd_ref[e], ((1,), (1,)))
            sigmoid = jax.nn.sigmoid(gate)
            active = gate * sigmoid
            hidden = (active * up).astype(BF16)
            inner[e, at] = hidden
            sent.append((dot(hidden, wd_ref[e], ((1,), (0,))) * weight).astype(BF16))
            share = jnp.sum(hidden.astype(F32) * grad_inner, axis=1, keepdims=True)
            grad_gate = (grad_inner * up * sigmoid * (1.0 + gate * (1.0 - sigmoid))).astype(BF16)
            grad_up = (grad_inner * active).astype(BF16)
            slope_g[e, at] = grad_gate
            slope_u[e, at] = grad_up
            grad = dot(grad_gate, wg_ref[e], ((1,), (0,)))
            grad = grad + dot(grad_up, wu_ref[e], ((1,), (0,)))
            high = share.astype(BF16).astype(F32)
            lanes = high * lane_ref[2 * e : 2 * e + 1] + (share - high) * lane_ref[2 * e + 1 : 2 * e + 2]
            returned.append((grad.astype(BF16), lanes.astype(BF16)))
        lane_slots = lax.broadcasted_iota(jnp.int32, (PAIR, per_pair), 1)
        for p in range(pair_count):
            tokens = pl.ds(p * PAIR, PAIR)
            mine = slice(p * per_pair, (p + 1) * per_pair)
            places = [
                jnp.where(lane_slots == column_ref[tokens, e : e + 1], 1.0, 0.0).astype(BF16)
                for e in range(local)
            ]
            place = jnp.concatenate(places, axis=1)
            out_rows = jnp.concatenate([s[mine] for s in sent], axis=0)
            out_ref[tokens] = dot(place, out_rows, ((1,), (0,))).astype(BF16)
            back_rows = jnp.concatenate([r[0][mine] for r in returned], axis=0)
            back_ref[tokens, :width] = dot(place, back_rows, ((1,), (0,))).astype(BF16)
            lane_rows = jnp.concatenate([r[1][mine] for r in returned], axis=0)
            back_ref[tokens, width:] = dot(place, lane_rows, ((1,), (0,))).astype(BF16)

    @pl.when(step >= steps)
    def _():
        e = step - steps
        gd_ref[0] = dot(inner[e], pairs[e], ((0,), (0,)))
        gg_ref[0] = dot(slope_g[e], rows[e], ((0,), (0,)))
        gu_ref[0] = dot(slope_u[e], rows[e], ((0,), (0,)))


def experts(x, c, row, column, gate, lanes, wg, wu, wd):
    count, local, units, width = x.shape[0], wg.shape[0], wg.shape[1], wg.shape[2]
    steps = count // STEP
    slots = count // 128 * CAPACITY

    def tokens(s):
        return (jnp.minimum(s, steps - 1), 0)

    def lanes_of(s):
        return (0, jnp.minimum(s, steps - 1))

    def fixed(*shape):
        return pl.BlockSpec(
            shape, lambda s: (0,) * len(shape), pipeline_mode=pl.Buffered(buffer_count=1)
        )

    def weight_out(s):
        return (jnp.maximum(s - steps, 0), 0, 0)

    flops = 2 * (9 * local * slots * units * width + 4 * local * slots * PAIR * width)
    return pl.pallas_call(
        functools.partial(experts_body, steps, width),
        grid=(steps + local,),
        out_shape=[
            jax.ShapeDtypeStruct((count, width), BF16),
            jax.ShapeDtypeStruct((count, width + 128), BF16),
        ]
        + [jax.ShapeDtypeStruct((local, units, width), F32)] * 3,
        in_specs=[
            pl.BlockSpec((STEP, x.shape[1]), tokens),
            pl.BlockSpec((STEP, c.shape[1]), tokens),
            pl.BlockSpec((local, STEP), lanes_of),
            pl.BlockSpec((STEP, local), tokens),
            pl.BlockSpec((local, STEP), lanes_of),
            fixed(2 * local, 128),
            fixed(local, units, width),
            fixed(local, units, width),
            fixed(local, units, width),
        ],
        out_specs=[
            pl.BlockSpec((STEP, width), tokens),
            pl.BlockSpec((STEP, width + 128), tokens),
        ]
        + [pl.BlockSpec((1, units, width), weight_out)] * 3,
        scratch_shapes=[
            pltpu.VMEM((local, slots, width), BF16),
            pltpu.VMEM((local, slots, width), BF16),
            pltpu.VMEM((local, slots, units), BF16),
            pltpu.VMEM((local, slots, units), BF16),
            pltpu.VMEM((local, slots, units), BF16),
        ],
        compiler_params=pltpu.CompilerParams(vmem_limit_bytes=63 * MIB),
        cost_estimate=pl.CostEstimate(
            flops=flops, bytes_accessed=80 * MIB, transcendentals=2 * slots * units
        ),
    )(x, c, row, column, gate, lanes, wg, wu, wd)


EPSILON = 1e-06
THETA = 1000000.0
PLANE = ("dp", "context")


def rms_parts(values, gain_vector):
    inverse = lax.rsqrt(jnp.mean(values * values, axis=-1, keepdims=True) + EPSILON)
    return (values * inverse * gain_vector, inverse)


def rms_back(values, inverse, gain_vector, grad_out):
    scaled = grad_out * gain_vector
    inner_mean = jnp.mean(scaled * values, axis=-1, keepdims=True)
    grad_in = inverse * scaled - values * (inverse * inverse * inverse) * inner_mean
    leading = tuple(range(values.ndim - 1))
    grad_gain = jnp.sum(grad_out * values * inverse, axis=leading)
    return (grad_in, grad_gain)


def rotary_tables(positions, head_size):
    half_size = head_size // 2
    frequency = jnp.exp(jnp.arange(half_size, dtype=F32) * (-2.0 * math.log(THETA) / head_size))
    angles = positions[:, None] * frequency[None, :]
    return (jnp.cos(angles)[:, None, :], jnp.sin(angles)[:, None, :])


def rotate(values, cosine_table, sine_table):
    half_size = values.shape[-1] // 2
    first_half = values[..., :half_size]
    second_half = values[..., half_size:]
    return jnp.concatenate(
        [
            first_half * cosine_table - second_half * sine_table,
            second_half * cosine_table + first_half * sine_table,
        ],
        axis=-1,
    )


def rotate_back(grad_out, cosine_table, sine_table):
    return rotate(grad_out, cosine_table, -sine_table)


def matmul(a, b, contract=((1,), (0,))):
    return lax.dot_general(a, b, (contract, ((), ())), preferred_element_type=F32)


def split_high(values):
    high = values.astype(BF16)
    return high, (values - high.astype(F32)).astype(BF16)


def per_device(
    tokens, routes, attention_gain, query_matrix, key_matrix, value_matrix, query_gain, key_gain,
    output_matrix, experts_gain, router_matrix, gate_weight, up_weight, down_weight, cotangent,
):
    tokens, routes, cotangent = tokens[0], routes[0], cotangent[0]
    rows, width = tokens.shape
    expert_count = router_matrix.shape[1]
    local = gate_weight.shape[0]
    head = query_gain.shape[0]
    query_columns, key_columns = query_matrix.shape[1], key_matrix.shape[1]
    heads = query_columns // head
    owners = 32
    shard = width // owners
    length = rows * 8
    scale = head ** (-0.5)
    qkv_columns = query_columns + 2 * key_columns

    packed = jnp.concatenate(
        [
            query_matrix,
            key_matrix,
            value_matrix,
            output_matrix.T,
            router_matrix,
            attention_gain[:, None],
            experts_gain[:, None],
            jnp.zeros((shard, 128 - expert_count - 2), BF16),
        ],
        axis=1,
    )
    (weights,) = plane_gather([packed], 0)
    qkv_matrix = weights[:, :qkv_columns]
    output_turned = weights[:, qkv_columns : qkv_columns + query_columns]
    rest = weights[:, qkv_columns + query_columns :]
    router = rest[:, :expert_count]
    first_gain = rest[:, expert_count].astype(F32)
    second_gain = rest[:, expert_count + 1].astype(F32)

    expert_ids = jnp.arange(expert_count, dtype=jnp.int32)
    mask = jnp.any(routes[:, :, None] == expert_ids, axis=1)
    sent_mask = jnp.pad(mask.astype(BF16), ((0, 0), (0, 128 - expert_count)))
    (all_grads,) = plane_gather([jnp.concatenate([cotangent, sent_mask], axis=1)], 1)

    residual = tokens.astype(F32)
    normed_input, first_inverse = rms_parts(residual, first_gain)
    normed_low = normed_input.astype(BF16)
    qkv = matmul(normed_low, qkv_matrix)
    query_unrotated = qkv[:, :query_columns].reshape(rows, heads, head)
    key_unrotated = qkv[:, query_columns : query_columns + key_columns].reshape(rows, 1, head)
    value_low = qkv[:, query_columns + key_columns :].astype(BF16)
    positions = lax.axis_index("context") * rows + jnp.arange(rows, dtype=jnp.int32)
    cosine_table, sine_table = rotary_tables(positions.astype(F32), head)
    query_gain_wide, key_gain_wide = query_gain.astype(F32), key_gain.astype(F32)
    query_normed, query_inverse = rms_parts(query_unrotated, query_gain_wide)
    query_low = rotate(query_normed, cosine_table, sine_table).astype(BF16)
    key_normed, key_inverse = rms_parts(key_unrotated, key_gain_wide)
    key_low = rotate(key_normed, cosine_table, sine_table).astype(BF16).reshape(rows, head)
    both = context_gather(jnp.concatenate([key_low, value_low], axis=1), 2)
    all_keys, all_values = both[:, :head], both[:, head:]
    allowed = (jnp.arange(length, dtype=jnp.int32)[None, :] <= positions[:, None])[:, None, :]
    raw_scores = jnp.einsum("bgd,ld->bgl", query_low, all_keys, preferred_element_type=F32)
    masked = jnp.where(allowed, raw_scores * scale, -1e30)
    highest = jnp.max(masked, axis=-1, keepdims=True)
    exponent = jnp.exp(masked - highest)
    row_total = jnp.sum(exponent, axis=-1, keepdims=True)
    probabilities = exponent / row_total
    log_total = highest + jnp.log(row_total)
    attended = jnp.einsum(
        "bgl,ld->bgd", probabilities.astype(BF16), all_values, preferred_element_type=F32
    )
    attended_low = attended.astype(BF16).reshape(rows, query_columns)
    attention_part = matmul(attended_low, output_turned, ((1,), (1,)))
    (attention_out,) = tensor_sum([attention_part], 3)
    hidden_state = residual + attention_out.astype(F32)
    routed_tokens, second_inverse = rms_parts(hidden_state, second_gain)
    routed_low = routed_tokens.astype(BF16)
    logits = matmul(routed_low, router)
    chosen = jnp.where(mask, logits, -1e30)
    gate_terms = jnp.where(mask, jnp.exp(chosen - jnp.max(chosen, axis=-1, keepdims=True)), 0.0)
    gates = gate_terms / jnp.sum(gate_terms, axis=-1, keepdims=True)
    gates_high, gates_low = split_high(gates)
    (all_rows,) = plane_gather([jnp.concatenate([routed_low, gates_high, gates_low], axis=1)], 4)

    first_expert = (lax.axis_index("dp") * 8 + lax.axis_index("context")) * local
    here = lax.dynamic_slice(all_grads, (0, width + first_expert), (all_grads.shape[0], local))
    blocks = here.reshape(owners, rows, local)
    before = jnp.tril(jnp.ones((rows, rows), BF16), -1)
    rank = jnp.einsum("ts,bse->bte", before, blocks, preferred_element_type=F32)
    rank = rank + (CAPACITY * (jnp.arange(owners) % 2)).astype(F32)[:, None, None]
    place = jnp.where(blocks > 0, rank, -1.0).astype(jnp.int32).reshape(owners * rows, local)
    gate_here = lax.dynamic_slice(
        all_rows, (0, width + first_expert), (all_rows.shape[0], local)
    ).astype(F32) + lax.dynamic_slice(
        all_rows, (0, width + expert_count + first_expert), (all_rows.shape[0], local)
    ).astype(F32)
    lane = jnp.arange(128, dtype=jnp.int32)[None, :]
    starts = jnp.arange(2 * local, dtype=jnp.int32)
    wanted = first_expert + starts // 2 + expert_count * (starts % 2)
    lanes = (lane == wanted[:, None]).astype(F32)
    out_terms, back_terms, gate_grad, up_grad, down_grad = experts(
        all_rows, all_grads, place.T, place, gate_here.T, lanes, gate_weight, up_weight, down_weight
    )
    back_sum = plane_scatter(back_terms, 5)
    out_sum = plane_scatter(out_terms, 6)
    experts_out, back_total = tensor_sum([out_sum, back_sum], 7)
    output = hidden_state + experts_out.astype(F32)

    grad_out = cotangent.astype(F32)
    shares = back_total[:, width : width + expert_count].astype(F32)
    shares = shares + back_total[:, width + expert_count :].astype(F32)
    grad_logits = (shares - gates * jnp.sum(shares, axis=-1, keepdims=True)).astype(BF16)
    router_grad = matmul(routed_low, grad_logits, ((0,), (0,)))
    grad_routed = back_total[:, :width].astype(F32) + matmul(grad_logits, router, ((1,), (1,)))
    grad_hidden_norm, second_gain_grad = rms_back(
        hidden_state, second_inverse, second_gain, grad_routed
    )
    grad_hidden = grad_out + grad_hidden_norm
    grad_mixed = grad_hidden.astype(BF16)
    output_grad = matmul(grad_mixed, attended_low, ((0,), (0,)))
    grad_attended = matmul(grad_mixed, output_turned).astype(BF16).reshape(rows, heads, head)
    raw_again = jnp.einsum("bgd,ld->bgl", query_low, all_keys, preferred_element_type=F32)
    probabilities = jnp.exp(jnp.where(allowed, raw_again * scale, -1e30) - log_total)
    grad_probs = jnp.einsum("bgd,ld->bgl", grad_attended, all_values, preferred_element_type=F32)
    row_delta = jnp.sum(probabilities * grad_probs, axis=-1, keepdims=True)
    grad_raw = (scale * probabilities * (grad_probs - row_delta)).astype(BF16)
    grad_query = jnp.einsum("bgl,ld->bgd", grad_raw, all_keys, preferred_element_type=F32)
    grad_keys_all = jnp.einsum("bgl,bgd->ld", grad_raw, query_low, preferred_element_type=F32)
    grad_values_all = jnp.einsum(
        "bgl,bgd->ld", probabilities.astype(BF16), grad_attended, preferred_element_type=F32
    )
    grad_both = context_scatter(jnp.concatenate([grad_keys_all, grad_values_all], axis=1), 8)
    grad_keys = grad_both[:, :head].reshape(rows, 1, head)
    grad_values = grad_both[:, head:]
    grad_query_raw, query_gain_part = rms_back(
        query_unrotated,
        query_inverse,
        query_gain_wide,
        rotate_back(grad_query, cosine_table, sine_table),
    )
    grad_key_raw, key_gain_part = rms_back(
        key_unrotated, key_inverse, key_gain_wide, rotate_back(grad_keys, cosine_table, sine_table)
    )
    grad_qkv = jnp.concatenate(
        [
            grad_query_raw.astype(BF16).reshape(rows, query_columns),
            grad_key_raw.astype(BF16).reshape(rows, key_columns),
            grad_values.astype(BF16),
        ],
        axis=1,
    )
    qkv_grad = matmul(normed_low, grad_qkv, ((0,), (0,)))
    grad_normed_part = matmul(grad_qkv, qkv_matrix, ((1,), (1,)))
    gain_parts = jnp.pad(jnp.stack([query_gain_part, key_gain_part]), ((0, rows - 2), (0, 0)))
    (normed_total,) = tensor_sum([jnp.concatenate([grad_normed_part, gain_parts], axis=1)], 9)
    grad_normed = normed_total[:, :width].astype(F32)
    head_gains = normed_total[:2, width:].astype(F32)
    grad_tokens_norm, first_gain_grad = rms_back(residual, first_inverse, first_gain, grad_normed)
    tokens_grad = grad_hidden + grad_tokens_norm

    def spread(vector):
        each = vector.shape[0] // owners
        return jnp.pad(vector.reshape(owners, each), ((0, 0), (0, shard - each))).reshape(-1, 1)

    terms = jnp.concatenate(
        [
            qkv_grad,
            output_grad,
            router_grad,
            first_gain_grad[:, None],
            second_gain_grad[:, None],
            spread(head_gains[0]),
            spread(head_gains[1]),
            jnp.zeros((width, 128 - expert_count - 4), F32),
        ],
        axis=1,
    ).astype(BF16)
    total = plane_scatter(terms, 10)
    after = qkv_columns + query_columns
    few = head // owners
    return (
        output[None],
        tokens_grad[None],
        total[:, after + expert_count],
        total[:, :query_columns],
        total[:, query_columns : query_columns + key_columns],
        total[:, query_columns + key_columns : qkv_columns],
        total[:few, after + expert_count + 2],
        total[:few, after + expert_count + 3],
        total[:, qkv_columns:after].T,
        total[:, after + expert_count + 1],
        total[:, after : after + expert_count],
        gate_grad,
        up_grad,
        down_grad,
    )


def solution(mesh):
    plane_rows = P(PLANE)
    both = P(PLANE, "tensor")
    tokens = P("dp", "context", None)
    expert_rows = P(PLANE, "tensor", None)
    router = P(PLANE, None)
    output_matrix = P("tensor", PLANE)
    return jax.shard_map(
        per_device,
        mesh=mesh,
        in_specs=(
            tokens, tokens, plane_rows, both, both, both, P(), P(), output_matrix, plane_rows,
            router, expert_rows, expert_rows, expert_rows, tokens,
        ),
        out_specs=(
            tokens, tokens, plane_rows, both, both, both, plane_rows, plane_rows, output_matrix,
            plane_rows, router, expert_rows, expert_rows, expert_rows,
        ),
        check_vma=False,
    )
```

```python
import functools
import math

import jax
import jax.numpy as jnp
from jax import lax
from jax.experimental import pallas as pl
from jax.experimental.pallas import tpu as pltpu
from jax.sharding import PartitionSpec as P

MESH = pl.DeviceIdType.MESH
F32 = jnp.float32
BF16 = jnp.bfloat16
MIB = 1 << 20


class Links:
    def __init__(self, send_sem, recv_sem):
        self.send_sem, self.recv_sem = send_sem, recv_sem
        self.copies = []

    def send(self, source, target, device, arriving):
        index = len(self.copies)
        copy = pltpu.make_async_remote_copy(
            src_ref=source,
            dst_ref=target,
            send_sem=self.send_sem.at[index],
            recv_sem=self.recv_sem.at[index],
            device_id=device,
            device_id_type=MESH,
        )
        copy.start()
        landing = pltpu.make_async_remote_copy(
            src_ref=arriving,
            dst_ref=arriving,
            send_sem=self.send_sem.at[index],
            recv_sem=self.recv_sem.at[index],
            device_id=device,
            device_id_type=MESH,
        )
        self.copies.append(copy)
        return landing

    def finish(self):
        for copy in self.copies:
            copy.wait_send()


def greet(devices):
    barrier = pltpu.get_barrier_semaphore()
    for device in devices:
        pl.semaphore_signal(barrier, inc=1, device_id=device, device_id_type=MESH)
    pl.semaphore_wait(barrier, len(devices))


def plane_place():
    y = lax.axis_index("dp")
    position = lax.axis_index("context")
    z = position // 2
    core = position - 2 * z

    def device(step):
        return {"dp": (y + step[0]) % 4, "context": ((z + step[1]) % 4) * 2 + core}

    def slot(step, other=False):
        at = 1 - core if other else core
        return ((y + step[0]) % 4) * 8 + ((z + step[1]) % 4) * 2 + at

    sibling = {"context": 2 * z + 1 - core}
    return device, slot, sibling


def along(first, second, order):
    return (first, second) if order == 0 else (second, first)


NEAR = ((1, 0), (-1, 0), (0, 1), (0, -1))


def gather_steps(links, mine, whole, own_sem):
    device, slot, sibling = plane_place()
    rows = mine.shape[0]

    def rows_of(order, part):
        start, size = order * (rows // 2), rows // 2
        if part == 2:
            return 0, rows
        if part == 1:
            return start + size // 2, size // 2
        if part == 0:
            return start, size // 2
        return start, size

    def region(order, place, part, other=False):
        start, size = rows_of(order, part)
        base = pl.multiple_of(slot(along(*place, order), other) * rows + start, 16)
        return whole.at[pl.ds(base, size)]

    def push(order, place, part, axis, sign):
        step = along(sign, 0, order) if axis == 0 else along(0, sign, order)
        source = region(order, place, part)
        if place == (0, 0):
            start, size = rows_of(order, part)
            source = mine.at[pl.ds(start, size)]
        came = (place[0] - sign, place[1]) if axis == 0 else (place[0], place[1] - sign)
        return links.send(source, region(order, place, part), device(step), region(order, came, part))

    beside = []

    def share(order, place, part=None):
        source = mine if part == 2 else region(order, place, part)
        beside.append(
            links.send(
                source, region(order, place, part), sibling, region(order, place, part, True)
            )
        )

    own = pltpu.make_async_copy(mine, region(0, (0, 0), 2), own_sem)
    own.start()
    got = {}
    for order in range(2):
        for sign in (1, -1):
            got[order, sign] = push(order, (0, 0), None, 0, sign)
    for order in range(2):
        for sign in (1, -1):
            got[order, 0, sign] = push(order, (0, 0), None, 1, sign)
    share(0, (0, 0), 2)
    yield
    for order in range(2):
        for sign in (1, -1):
            got[order, sign].wait_recv()
            got[order, "far", sign] = push(order, (-sign, 0), 0 if sign == 1 else 1, 0, sign)
        for sign in (1, -1):
            for way in (1, -1):
                got[order, -sign, way] = push(order, (-sign, 0), None, 1, way)
            share(order, (-sign, 0))
    yield
    for order in range(2):
        for sign in (1, -1):
            got[order, "far", sign].wait_recv()
        for way in (1, -1):
            got[order, 2, way] = push(order, (2, 0), None, 1, way)
        share(order, (2, 0))
    yield
    for i in (0, 1, -1, 2):
        for order in range(2):
            for way in (1, -1):
                got[order, i, way].wait_recv()
                got[order, i, "far", way] = push(order, (i, -way), 0 if way == 1 else 1, 1, way)
                share(order, (i, -way))
        yield
    for i in (0, 1, -1, 2):
        for order in range(2):
            for way in (1, -1):
                got[order, i, "far", way].wait_recv()
            share(order, (i, 2))
    yield
    for copy in beside:
        copy.wait_recv()
    own.wait()


GATHER_COPIES = 2 * 20 + 1 + 2 * 15


def gather_body(mine, whole, send_sem, recv_sem, own_sem):
    device, slot, sibling = plane_place()
    greet([device(step) for step in NEAR] + [sibling])
    links = Links(send_sem, recv_sem)
    for _ in gather_steps(links, mine, whole, own_sem):
        pass
    links.finish()


def plane_gather(array, collective_id):
    return pl.pallas_call(
        gather_body,
        out_shape=jax.ShapeDtypeStruct((32 * array.shape[0],) + array.shape[1:], array.dtype),
        in_specs=[pl.BlockSpec(memory_space=pl.ANY)],
        out_specs=pl.BlockSpec(memory_space=pl.ANY),
        scratch_shapes=[
            pltpu.SemaphoreType.DMA((GATHER_COPIES,)),
            pltpu.SemaphoreType.DMA((GATHER_COPIES,)),
            pltpu.SemaphoreType.DMA,
        ],
        compiler_params=pltpu.CompilerParams(
            collective_id=collective_id, has_side_effects=True, vmem_limit_bytes=56 * MIB
        ),
    )(array)


def add_rows(target, sources, offset, size, chunk=16):
    def step(k, carry):
        base = pl.multiple_of(k * chunk, chunk)
        at = pl.ds(offset + base, chunk)
        total = target[at].astype(F32)
        for source, start in sources:
            total = total + source[pl.ds(start + base, chunk)].astype(F32)
        target[at] = total.astype(target.dtype)
        return carry

    lax.fori_loop(0, size // chunk, step, 0)


SLOTS = (
    (2, 2), (1, 2), (2, 1), (-1, 2), (2, -1), (0, 2), (2, 0),
    (1, 1), (1, -1), (-1, 1), (-1, -1), (0, 1), (1, 0), (0, -1), (-1, 0), (0, 0),
)


def scatter_body(rows, part_ref, out_ref, held, near, landed, send_sem, recv_sem, own_sem):
    device, slot, sibling = plane_place()
    greet([device(step) for step in NEAR] + [sibling])
    links = Links(send_sem, recv_sem)
    half, quarter = rows // 2, rows // 4
    index = {place: k for k, place in enumerate(SLOTS)}

    def base(place):
        return index[place] * rows

    loads, shares = {}, {}
    for k, place in enumerate(SLOTS):
        copy = pltpu.make_async_copy(
            part_ref.at[pl.ds(pl.multiple_of(slot(place) * rows, 16), rows)],
            held.at[pl.ds(base(place), rows)],
            own_sem.at[k],
        )
        copy.start()
        loads[place] = copy
        here = near.at[pl.ds(base(place), rows)]
        shares[place] = links.send(
            part_ref.at[pl.ds(pl.multiple_of(slot(place, True) * rows, 16), rows)],
            here,
            sibling,
            here,
        )
    merged = set()

    def ready(order, place):
        place = along(*place, order)
        if place not in merged:
            merged.add(place)
            loads[place].wait()
            shares[place].wait_recv()
            add_rows(held, [(near, base(place))], base(place), rows)
        return base(place) + order * half

    room = [0]

    def push(start, size, order, axis, sign):
        step = along(sign, 0, order) if axis == 0 else along(0, sign, order)
        at = room[0]
        room[0] += size
        here = landed.at[pl.ds(at, size)]
        return links.send(held.at[pl.ds(start, size)], here, device(step), here), at

    got = {}

    def reduce_ring(key, order, axis, places, stage):
        opposite, plus, minus, mine = places
        if stage == 0:
            start = ready(order, opposite)
            got[key, 0] = push(start, quarter, order, axis, 1)
            got[key, 1] = push(start + quarter, quarter, order, axis, -1)
        if stage == 1:
            start = ready(order, plus)
            copy, at = got[key, 0]
            copy.wait_recv()
            add_rows(held, [(landed, at)], start, quarter)
            got[key, 2] = push(start, half, order, axis, 1)
            start = ready(order, minus)
            copy, at = got[key, 1]
            copy.wait_recv()
            add_rows(held, [(landed, at)], start + quarter, quarter)
            got[key, 3] = push(start, half, order, axis, -1)
        if stage == 2:
            start = ready(order, mine)
            sources = []
            for k in (2, 3):
                copy, at = got[key, k]
                copy.wait_recv()
                sources.append((landed, at))
            if axis == 1:
                add_rows(held, sources, start, half)
            else:
                for k in range(half // 16):
                    total = held[pl.ds(start + 16 * k, 16)].astype(F32)
                    for source, at in sources:
                        total = total + source[pl.ds(at + 16 * k, 16)].astype(F32)
                    out_ref[pl.ds(order * half + 16 * k, 16)] = total

    def ring(i, order, stage):
        reduce_ring((order, i), order, 1, [(i, j) for j in (2, 1, -1, 0)], stage)

    def last(order, stage):
        reduce_ring((order, "last"), order, 0, [(i, 0) for i in (2, 1, -1, 0)], stage)

    for i in (2, 1, -1, 0):
        for order in range(2):
            ring(i, order, 0)
    for i in (2, 1, -1, 0):
        for order in range(2):
            ring(i, order, 1)
    for order in range(2):
        ring(2, order, 2)
        last(order, 0)
    for order in range(2):
        ring(1, order, 2)
        ring(-1, order, 2)
        last(order, 1)
    for order in range(2):
        ring(0, order, 2)
        last(order, 2)
    links.finish()


def plane_scatter(part, collective_id):
    rows, columns = part.shape[0] // 32, part.shape[1]
    copies = 16 + 2 * 20
    return pl.pallas_call(
        functools.partial(scatter_body, rows),
        out_shape=jax.ShapeDtypeStruct((rows, columns), F32),
        in_specs=[pl.BlockSpec(memory_space=pl.ANY)],
        out_specs=pl.BlockSpec(memory_space=pltpu.VMEM),
        scratch_shapes=[
            pltpu.VMEM((16 * rows, columns), BF16),
            pltpu.VMEM((16 * rows, columns), BF16),
            pltpu.VMEM((15 * rows, columns), BF16),
            pltpu.SemaphoreType.DMA((copies,)),
            pltpu.SemaphoreType.DMA((copies,)),
            pltpu.SemaphoreType.DMA((16,)),
        ],
        compiler_params=pltpu.CompilerParams(
            collective_id=collective_id, has_side_effects=True, vmem_limit_bytes=56 * MIB
        ),
    )(part)


def tensor_sum_body(count, *refs):
    parts, outs = refs[:count], refs[count : 2 * count]
    held, landed = refs[2 * count : 3 * count], refs[3 * count : 4 * count]
    send_sem, recv_sem = refs[4 * count :]
    x = lax.axis_index("tensor")

    def device(step):
        return {"tensor": (x + step) % 4}

    greet([device(1), device(-1)])
    links = Links(send_sem, recv_sem)
    got = {}

    def rows(a, step, start, size):
        quarter = parts[a].shape[0] // 4
        return pl.ds(pl.multiple_of(((x + step) % 4) * quarter + start, 16), size)

    def push(a, source, sign, at, size):
        here = landed[a].at[pl.ds(at, size)]
        return links.send(source, here, device(sign), here)

    for a in range(count):
        held[a][...] = parts[a][...].astype(BF16)
        quarter = parts[a].shape[0] // 4
        eighth = quarter // 2
        got[a, 0] = push(a, held[a].at[rows(a, 2, 0, eighth)], 1, 0, eighth)
        got[a, 1] = push(a, held[a].at[rows(a, 2, eighth, eighth)], -1, eighth, eighth)
    for a in range(count):
        quarter = parts[a].shape[0] // 4
        eighth = quarter // 2
        for k, sign in enumerate((1, -1)):
            got[a, k].wait_recv()
            at = rows(a, sign, k * eighth, eighth)
            total = parts[a][at].astype(F32) + landed[a][k * eighth : (k + 1) * eighth].astype(F32)
            held[a][at] = total.astype(BF16)
            got[a, 2 + k] = push(
                a, held[a].at[rows(a, sign, 0, quarter)], sign, (k + 1) * quarter, quarter
            )
    for a in range(count):
        quarter = parts[a].shape[0] // 4
        got[a, 2].wait_recv()
        got[a, 3].wait_recv()
        mine = rows(a, 0, 0, quarter)
        total = parts[a][mine].astype(F32)
        total = total + landed[a][quarter : 2 * quarter].astype(F32)
        total = total + landed[a][2 * quarter : 3 * quarter].astype(F32)
        outs[a][mine] = total.astype(BF16)
        for k, sign in enumerate((1, -1)):
            got[a, 4 + k] = links.send(
                outs[a].at[mine], outs[a].at[mine], device(sign),
                outs[a].at[rows(a, -sign, 0, quarter)],
            )
    for a in range(count):
        quarter = parts[a].shape[0] // 4
        eighth = quarter // 2
        for k, sign in enumerate((1, -1)):
            got[a, 4 + k].wait_recv()
            at = rows(a, -sign, k * eighth, eighth)
            got[a, 6 + k] = links.send(
                outs[a].at[at], outs[a].at[at], device(sign),
                outs[a].at[rows(a, 2, k * eighth, eighth)],
            )
    for a in range(count):
        got[a, 6].wait_recv()
        got[a, 7].wait_recv()
    links.finish()


def tensor_sum(arrays, collective_id):
    count = len(arrays)
    spec = pl.BlockSpec(memory_space=pltpu.VMEM)
    return pl.pallas_call(
        functools.partial(tensor_sum_body, count),
        out_shape=[jax.ShapeDtypeStruct(a.shape, BF16) for a in arrays],
        in_specs=[spec] * count,
        out_specs=[spec] * count,
        scratch_shapes=[pltpu.VMEM(a.shape, BF16) for a in arrays]
        + [pltpu.VMEM((a.shape[0] * 3 // 4, a.shape[1]), BF16) for a in arrays]
        + [pltpu.SemaphoreType.DMA((8 * count,)), pltpu.SemaphoreType.DMA((8 * count,))],
        compiler_params=pltpu.CompilerParams(
            collective_id=collective_id, has_side_effects=True, vmem_limit_bytes=32 * MIB
        ),
    )(*arrays)


def context_place():
    position = lax.axis_index("context")

    def device(step):
        return {"context": (position + step) % 8}

    return position, device


def context_gather_body(mine, whole, send_sem, recv_sem, own_sem):
    position, device = context_place()
    rows = mine.shape[0]
    greet([device(step) for step in range(1, 8)])
    links = Links(send_sem, recv_sem)

    def region(step):
        return whole.at[pl.ds(pl.multiple_of(((position + step) % 8) * rows, 16), rows)]

    own = pltpu.make_async_copy(mine, region(0), own_sem)
    own.start()
    got = [links.send(mine, region(0), device(step), region(-step)) for step in range(1, 8)]
    for copy in got:
        copy.wait_recv()
    own.wait()
    links.finish()


def context_gather(array, collective_id):
    spec = pl.BlockSpec(memory_space=pltpu.VMEM)
    return pl.pallas_call(
        context_gather_body,
        out_shape=jax.ShapeDtypeStruct((8 * array.shape[0],) + array.shape[1:], array.dtype),
        in_specs=[spec],
        out_specs=spec,
        scratch_shapes=[
            pltpu.SemaphoreType.DMA((7,)),
            pltpu.SemaphoreType.DMA((7,)),
            pltpu.SemaphoreType.DMA,
        ],
        compiler_params=pltpu.CompilerParams(collective_id=collective_id, has_side_effects=True),
    )(array)


def context_scatter_body(part, out, landed, send_sem, recv_sem):
    position, device = context_place()
    rows = out.shape[0]
    greet([device(step) for step in range(1, 8)])
    links = Links(send_sem, recv_sem)

    def region(step):
        return pl.ds(pl.multiple_of(((position + step) % 8) * rows, 16), rows)

    got = []
    for step in range(1, 8):
        here = landed.at[pl.ds((step - 1) * rows, rows)]
        got.append(links.send(part.at[region(step)], here, device(step), here))
    total = part[region(0)].astype(F32)
    for k, copy in enumerate(got):
        copy.wait_recv()
        total = total + landed[k * rows : (k + 1) * rows].astype(F32)
    out[...] = total
    links.finish()


def context_scatter(part, collective_id):
    rows, columns = part.shape[0] // 8, part.shape[1]
    spec = pl.BlockSpec(memory_space=pltpu.VMEM)
    return pl.pallas_call(
        context_scatter_body,
        out_shape=jax.ShapeDtypeStruct((rows, columns), F32),
        in_specs=[spec],
        out_specs=spec,
        scratch_shapes=[
            pltpu.VMEM((7 * rows, columns), part.dtype),
            pltpu.SemaphoreType.DMA((7,)),
            pltpu.SemaphoreType.DMA((7,)),
        ],
        compiler_params=pltpu.CompilerParams(
            collective_id=collective_id, has_side_effects=True, vmem_limit_bytes=24 * MIB
        ),
    )(part)


EPSILON = 1e-06
THETA = 1000000.0
PLANE = ("dp", "context")


def dot(a, b, contract):
    return lax.dot_general(a, b, (contract, ((), ())), preferred_element_type=F32)


PAIR = 256
STEP = 512
CAPACITY = 32


def experts_body(
    steps, width, x_ref, c_ref, row_ref, column_ref, gate_ref, lane_ref, wg_ref, wu_ref, wd_ref,
    out_ref, back_ref, gg_ref, gu_ref, gd_ref, rows, pairs, inner, slope_g, slope_u,
):
    step = pl.program_id(0)
    local = wg_ref.shape[0]
    per_pair = 2 * CAPACITY
    pair_count = STEP // PAIR
    per_step = pair_count * per_pair

    @pl.when(step < steps)
    def _():
        base = pl.multiple_of(step * per_step, per_step)
        weights = [[None] * pair_count for _ in range(local)]
        for p in range(pair_count):
            tokens = pl.ds(p * PAIR, PAIR)
            picks = []
            slots = lax.broadcasted_iota(jnp.int32, (per_pair, PAIR), 0)
            for e in range(local):
                match = slots == row_ref[e : e + 1, tokens]
                weights[e][p] = jnp.sum(
                    jnp.where(match, gate_ref[e : e + 1, tokens], 0.0), axis=1, keepdims=True
                )
                picks.append(jnp.where(match, 1.0, 0.0).astype(BF16))
            pick = jnp.concatenate(picks, axis=0)
            taken = dot(pick, x_ref[tokens, :width], ((1,), (0,))).astype(BF16)
            given = dot(pick, c_ref[tokens, :width], ((1,), (0,)))
            for e in range(local):
                at = pl.ds(base + p * per_pair, per_pair)
                mine = slice(e * per_pair, (e + 1) * per_pair)
                rows[e, at] = taken[mine]
                pairs[e, at] = (weights[e][p] * given[mine]).astype(BF16)
        sent, returned = [], []
        for e in range(local):
            at = pl.ds(base, per_step)
            weight = jnp.concatenate(weights[e], axis=0)
            taken, given = rows[e, at], pairs[e, at]
            gate = dot(taken, wg_ref[e], ((1,), (1,)))
            up = dot(taken, wu_ref[e], ((1,), (1,)))
            grad_inner = dot(given, wd_ref[e], ((1,), (1,)))
            sigmoid = jax.nn.sigmoid(gate)
            active = gate * sigmoid
            hidden = (active * up).astype(BF16)
            inner[e, at] = hidden
            sent.append((dot(hidden, wd_ref[e], ((1,), (0,))) * weight).astype(BF16))
            share = jnp.sum(hidden.astype(F32) * grad_inner, axis=1, keepdims=True)
            grad_gate = (grad_inner * up * sigmoid * (1.0 + gate * (1.0 - sigmoid))).astype(BF16)
            grad_up = (grad_inner * active).astype(BF16)
            slope_g[e, at] = grad_gate
            slope_u[e, at] = grad_up
            grad = dot(grad_gate, wg_ref[e], ((1,), (0,)))
            grad = grad + dot(grad_up, wu_ref[e], ((1,), (0,)))
            high = share.astype(BF16).astype(F32)
            lanes = high * lane_ref[2 * e : 2 * e + 1] + (share - high) * lane_ref[2 * e + 1 : 2 * e + 2]
            returned.append((grad.astype(BF16), lanes.astype(BF16)))
        lane_slots = lax.broadcasted_iota(jnp.int32, (PAIR, per_pair), 1)
        for p in range(pair_count):
            tokens = pl.ds(p * PAIR, PAIR)
            mine = slice(p * per_pair, (p + 1) * per_pair)
            places = [
                jnp.where(lane_slots == column_ref[tokens, e : e + 1], 1.0, 0.0).astype(BF16)
                for e in range(local)
            ]
            place = jnp.concatenate(places, axis=1)
            out_rows = jnp.concatenate([s[mine] for s in sent], axis=0)
            out_ref[tokens] = dot(place, out_rows, ((1,), (0,))).astype(BF16)
            back_rows = jnp.concatenate([r[0][mine] for r in returned], axis=0)
            back_ref[tokens, :width] = dot(place, back_rows, ((1,), (0,))).astype(BF16)
            lane_rows = jnp.concatenate([r[1][mine] for r in returned], axis=0)
            back_ref[tokens, width:] = dot(place, lane_rows, ((1,), (0,))).astype(BF16)

    @pl.when(step >= steps)
    def _():
        e = step - steps
        gd_ref[0] = dot(inner[e], pairs[e], ((0,), (0,)))
        gg_ref[0] = dot(slope_g[e], rows[e], ((0,), (0,)))
        gu_ref[0] = dot(slope_u[e], rows[e], ((0,), (0,)))


def experts(x, c, row, column, gate, lanes, wg, wu, wd):
    count, local, units, width = x.shape[0], wg.shape[0], wg.shape[1], wg.shape[2]
    steps = count // STEP
    slots = count // 128 * CAPACITY

    def tokens(s):
        return (jnp.minimum(s, steps - 1), 0)

    def lanes_of(s):
        return (0, jnp.minimum(s, steps - 1))

    def fixed(*shape):
        return pl.BlockSpec(
            shape, lambda s: (0,) * len(shape), pipeline_mode=pl.Buffered(buffer_count=1)
        )

    def weight_out(s):
        return (jnp.maximum(s - steps, 0), 0, 0)

    flops = 2 * (9 * local * slots * units * width + 4 * local * slots * PAIR * width)
    return pl.pallas_call(
        functools.partial(experts_body, steps, width),
        grid=(steps + local,),
        out_shape=[
            jax.ShapeDtypeStruct((count, width), BF16),
            jax.ShapeDtypeStruct((count, width + 128), BF16),
        ]
        + [jax.ShapeDtypeStruct((local, units, width), F32)] * 3,
        in_specs=[
            pl.BlockSpec((STEP, x.shape[1]), tokens),
            pl.BlockSpec((STEP, c.shape[1]), tokens),
            pl.BlockSpec((local, STEP), lanes_of),
            pl.BlockSpec((STEP, local), tokens),
            pl.BlockSpec((local, STEP), lanes_of),
            fixed(2 * local, 128),
            fixed(local, units, width),
            fixed(local, units, width),
            fixed(local, units, width),
        ],
        out_specs=[
            pl.BlockSpec((STEP, width), tokens),
            pl.BlockSpec((STEP, width + 128), tokens),
        ]
        + [pl.BlockSpec((1, units, width), weight_out)] * 3,
        scratch_shapes=[
            pltpu.VMEM((local, slots, width), BF16),
            pltpu.VMEM((local, slots, width), BF16),
            pltpu.VMEM((local, slots, units), BF16),
            pltpu.VMEM((local, slots, units), BF16),
            pltpu.VMEM((local, slots, units), BF16),
        ],
        compiler_params=pltpu.CompilerParams(vmem_limit_bytes=63 * MIB),
        cost_estimate=pl.CostEstimate(
            flops=flops, bytes_accessed=80 * MIB, transcendentals=2 * slots * units
        ),
    )(x, c, row, column, gate, lanes, wg, wu, wd)


def weight_terms_body(normed, grad_qkv, mixed, attended, few, out):
    first, second = grad_qkv.shape[1], attended.shape[1]
    out[:, :first] = dot(normed[...], grad_qkv[...], ((0,), (0,))).astype(BF16)
    out[:, first : first + second] = dot(mixed[...], attended[...], ((0,), (0,))).astype(BF16)
    out[:, first + second :] = few[...].astype(F32).T.astype(BF16)


def weight_terms(normed, grad_qkv, mixed, attended, few):
    width = normed.shape[1]
    columns = grad_qkv.shape[1] + attended.shape[1] + few.shape[0]
    block = 256

    def part(a):
        return pl.BlockSpec((a.shape[0], block), lambda i: (0, i))

    def whole(a):
        return pl.BlockSpec(a.shape, lambda i: (0, 0))

    return pl.pallas_call(
        weight_terms_body,
        grid=(width // block,),
        out_shape=jax.ShapeDtypeStruct((width, columns), BF16),
        in_specs=[part(normed), whole(grad_qkv), part(mixed), whole(attended), part(few)],
        out_specs=pl.BlockSpec((block, columns), lambda i: (i, 0)),
        compiler_params=pltpu.CompilerParams(vmem_limit_bytes=32 * MIB),
    )(normed, grad_qkv, mixed, attended, few)


def direct_exchange(links, held, landed, x, device):
    quarter = held.shape[0] // 4
    got = []
    for step in (1, 3, 2):
        source = held.at[pl.ds(pl.multiple_of(((x + step) % 4) * quarter, 16), quarter)]
        here = landed.at[pl.ds((step - 1) * quarter, quarter)]
        got.append(links.send(source, here, device(step), here))
    return got


def front_body(
    head, packed_ref, cot_ref, x_ref, cos_ref, sin_ref, qg_ref, kg_ref,
    weights_out, cot_out, raw_out, normed_out, query_out, both_out, attended_out, mixed_out,
    weights, part, held, landed, keys, send_sem, recv_sem, own_sem,
):
    rows, width = x_ref.shape
    query_columns = attended_out.shape[1]
    heads = query_columns // head
    scale = head ** (-0.5)
    x = lax.axis_index("tensor")
    place, slot, sibling = plane_place()
    position = lax.axis_index("context")

    def tensor_device(step):
        return {"tensor": (x + step) % 4}

    def context_device(step):
        return {"context": (position + step) % 8}

    greet(
        [place(step) for step in NEAR[:2]]
        + [context_device(step) for step in range(1, 8)]
        + [tensor_device(step) for step in range(1, 4)]
    )
    links = Links(send_sem, recv_sem)
    first = gather_steps(links, packed_ref, weights, own_sem.at[0])
    second = gather_steps(links, cot_ref, cot_out, own_sem.at[1])
    next(first)
    values = x_ref[...].astype(F32)
    inverse = lax.rsqrt(jnp.mean(values * values, axis=-1, keepdims=True) + EPSILON)
    next(first)
    next(first)
    next(second)
    for _ in first:
        pass
    store = pltpu.make_async_copy(weights, weights_out, own_sem.at[2])
    store.start()
    last = query_columns * 2 + 2 * head
    take = jnp.where(
        lax.broadcasted_iota(jnp.int32, (8, 128), 1) == 64, 1.0, 0.0
    ).astype(BF16)
    gain = dot(take, weights[:, last : last + 128], ((1,), (1,)))[0:1]
    normed_out[...] = (x_ref[...].astype(F32) * inverse * gain).astype(BF16)

    def turn(values, gain_row):
        inverse = lax.rsqrt(jnp.mean(values * values, axis=-1, keepdims=True) + EPSILON)
        normed = values * inverse * gain_row
        return normed * cos_ref[...] + pltpu.roll(normed, head // 2, 1) * sin_ref[...]

    normed = normed_out[...]
    raw = dot(normed, weights[:, query_columns : query_columns + 2 * head], ((1,), (0,)))
    raw_out[:, query_columns:] = raw[:, :head]
    keys[:, :head] = turn(raw[:, :head], kg_ref[...]).astype(BF16)
    keys[:, head:] = raw[:, head:].astype(BF16)

    def context_rows(step):
        return both_out.at[pl.ds(pl.multiple_of(((position + step) % 8) * rows, 16), rows)]

    own = pltpu.make_async_copy(keys, context_rows(0), own_sem.at[3])
    own.start()
    got = [
        links.send(keys, context_rows(0), context_device(step), context_rows(-step))
        for step in range(1, 8)
    ]
    next(second)
    for part_index in range(4):
        columns = slice(part_index * query_columns // 4, (part_index + 1) * query_columns // 4)
        raw_out[:, columns] = dot(normed, weights[:, columns], ((1,), (0,)))
    for h in range(heads):
        columns = slice(h * head, (h + 1) * head)
        query_out[:, columns] = turn(raw_out[:, columns], qg_ref[...]).astype(BF16)
    own.wait()
    for copy in got:
        copy.wait_recv()
    next(second)
    length = 8 * rows
    key_positions = lax.broadcasted_iota(jnp.int32, (rows, length), 1)
    query_positions = lax.broadcasted_iota(jnp.int32, (rows, length), 0) + position * rows
    allowed = key_positions <= query_positions
    for h in range(heads):
        columns = slice(h * head, (h + 1) * head)
        scores = dot(query_out[:, columns], both_out[:, :head], ((1,), (1,))) * scale
        scores = jnp.where(allowed, scores, -1e30)
        terms = jnp.exp(scores - jnp.max(scores, axis=-1, keepdims=True))
        probabilities = (terms * (1.0 / jnp.sum(terms, axis=-1, keepdims=True))).astype(BF16)
        attended_out[:, columns] = dot(probabilities, both_out[:, head:], ((1,), (0,))).astype(BF16)
    next(second)
    matrix = slice(query_columns + 2 * head, last)
    for block in range(4):
        columns = slice(block * width // 4, (block + 1) * width // 4)
        product = dot(attended_out[...], weights[columns, matrix], ((1,), (1,)))
        part[:, columns] = product
        held[:, columns] = product.astype(BF16)
    got = direct_exchange(links, held, landed, x, tensor_device)
    next(second)
    quarter = rows // 4
    mine = pl.ds(pl.multiple_of(x * quarter, 16), quarter)
    for copy in got:
        copy.wait_recv()
    total = part[mine]
    for k in range(3):
        total = total + landed[k * quarter : (k + 1) * quarter].astype(F32)
    mixed_out[mine] = total.astype(BF16)

    def mixed_rows(step):
        return mixed_out.at[pl.ds(pl.multiple_of(((x + step) % 4) * quarter, 16), quarter)]

    got = [
        links.send(mixed_rows(0), mixed_rows(0), tensor_device(step), mixed_rows(-step))
        for step in (1, 3, 2)
    ]
    for _ in second:
        pass
    for copy in got:
        copy.wait_recv()
    store.wait()
    links.finish()


def front(packed, cotangent, tokens, cosines, sines, query_gain, key_gain, query_columns, collective_id):
    rows, width = tokens.shape
    head = query_gain.shape[1]
    copies = 2 * GATHER_COPIES + 7 + 6
    vmem = pl.BlockSpec(memory_space=pltpu.VMEM)
    hbm = pl.BlockSpec(memory_space=pl.ANY)
    return pl.pallas_call(
        functools.partial(front_body, head),
        out_shape=[
            jax.ShapeDtypeStruct((32 * packed.shape[0], packed.shape[1]), BF16),
            jax.ShapeDtypeStruct((32 * cotangent.shape[0], cotangent.shape[1]), BF16),
            jax.ShapeDtypeStruct((rows, query_columns + head), F32),
            jax.ShapeDtypeStruct((rows, width), BF16),
            jax.ShapeDtypeStruct((rows, query_columns), BF16),
            jax.ShapeDtypeStruct((8 * rows, 2 * head), BF16),
            jax.ShapeDtypeStruct((rows, query_columns), BF16),
            jax.ShapeDtypeStruct((rows, width), BF16),
        ],
        in_specs=[hbm, hbm] + [vmem] * 5,
        out_specs=[hbm, hbm] + [vmem] * 6,
        scratch_shapes=[
            pltpu.VMEM((32 * packed.shape[0], packed.shape[1]), BF16),
            pltpu.VMEM((rows, width), F32),
            pltpu.VMEM((rows, width), BF16),
            pltpu.VMEM((rows * 3 // 4, width), BF16),
            pltpu.VMEM((rows, 2 * head), BF16),
            pltpu.SemaphoreType.DMA((copies,)),
            pltpu.SemaphoreType.DMA((copies,)),
            pltpu.SemaphoreType.DMA((4,)),
        ],
        compiler_params=pltpu.CompilerParams(
            collective_id=collective_id, has_side_effects=True, vmem_limit_bytes=56 * MIB
        ),
    )(packed, cotangent, tokens, cosines, sines, query_gain, key_gain)


def rms_parts(values, gain_vector):
    inverse = lax.rsqrt(jnp.mean(values * values, axis=-1, keepdims=True) + EPSILON)
    return (values * inverse * gain_vector, inverse)


def rms_back(values, inverse, gain_vector, grad_out):
    scaled = grad_out * gain_vector
    inner_mean = jnp.mean(scaled * values, axis=-1, keepdims=True)
    grad_in = inverse * scaled - values * (inverse * inverse * inverse) * inner_mean
    leading = tuple(range(values.ndim - 1))
    grad_gain = jnp.sum(grad_out * values * inverse, axis=leading)
    return (grad_in, grad_gain)


def rotary_tables(positions, head_size):
    half_size = head_size // 2
    frequency = jnp.exp(jnp.arange(half_size, dtype=F32) * (-2.0 * math.log(THETA) / head_size))
    angles = positions[:, None] * frequency[None, :]
    return (jnp.cos(angles)[:, None, :], jnp.sin(angles)[:, None, :])


def rotate(values, cosine_table, sine_table):
    half_size = values.shape[-1] // 2
    first_half = values[..., :half_size]
    second_half = values[..., half_size:]
    return jnp.concatenate(
        [
            first_half * cosine_table - second_half * sine_table,
            second_half * cosine_table + first_half * sine_table,
        ],
        axis=-1,
    )


def rotate_back(grad_out, cosine_table, sine_table):
    return rotate(grad_out, cosine_table, -sine_table)


def matmul(a, b, contract=((1,), (0,))):
    return lax.dot_general(a, b, (contract, ((), ())), preferred_element_type=F32)


def split_high(values):
    high = values.astype(BF16)
    return high, (values - high.astype(F32)).astype(BF16)


def per_device(
    tokens, routes, attention_gain, query_matrix, key_matrix, value_matrix, query_gain, key_gain,
    output_matrix, experts_gain, router_matrix, gate_weight, up_weight, down_weight, cotangent,
):
    tokens, routes, cotangent = tokens[0], routes[0], cotangent[0]
    rows, width = tokens.shape
    expert_count = router_matrix.shape[1]
    local = gate_weight.shape[0]
    head = query_gain.shape[0]
    query_columns, key_columns = query_matrix.shape[1], key_matrix.shape[1]
    heads = query_columns // head
    owners = 32
    shard = width // owners
    length = rows * 8
    scale = head ** (-0.5)
    qkv_columns = query_columns + 2 * key_columns

    packed = jnp.concatenate(
        [
            query_matrix,
            key_matrix,
            value_matrix,
            output_matrix.T,
            router_matrix,
            attention_gain[:, None],
            experts_gain[:, None],
            jnp.zeros((shard, 128 - expert_count - 2), BF16),
        ],
        axis=1,
    )
    expert_ids = jnp.arange(expert_count, dtype=jnp.int32)
    mask = jnp.any(routes[:, :, None] == expert_ids, axis=1)
    sent_mask = jnp.pad(mask.astype(BF16), ((0, 0), (0, 128 - expert_count)))
    positions = lax.axis_index("context") * rows + jnp.arange(rows, dtype=jnp.int32)
    cosine_table, sine_table = rotary_tables(positions.astype(F32), head)
    query_gain_wide, key_gain_wide = query_gain.astype(F32), key_gain.astype(F32)
    weights, all_grads, raw, normed_low, query_flat, both, attended_low, attention_out = front(
        packed,
        jnp.concatenate([cotangent, sent_mask], axis=1),
        tokens,
        jnp.concatenate([cosine_table[:, 0], cosine_table[:, 0]], axis=1),
        jnp.concatenate([-sine_table[:, 0], sine_table[:, 0]], axis=1),
        query_gain_wide[None],
        key_gain_wide[None],
        query_columns,
        0,
    )
    qkv_matrix = weights[:, :qkv_columns]
    output_turned = weights[:, qkv_columns : qkv_columns + query_columns]
    rest = weights[:, qkv_columns + query_columns :]
    router = rest[:, :expert_count]
    first_gain = rest[:, expert_count].astype(F32)
    second_gain = rest[:, expert_count + 1].astype(F32)

    residual = tokens.astype(F32)
    first_inverse = rms_parts(residual, first_gain)[1]
    query_unrotated = raw[:, :query_columns].reshape(rows, heads, head)
    key_unrotated = raw[:, query_columns:].reshape(rows, 1, head)
    query_inverse = rms_parts(query_unrotated, query_gain_wide)[1]
    key_inverse = rms_parts(key_unrotated, key_gain_wide)[1]
    query_low = query_flat.reshape(rows, heads, head)
    all_keys, all_values = both[:, :head], both[:, head:]
    allowed = (jnp.arange(length, dtype=jnp.int32)[None, :] <= positions[:, None])[:, None, :]
    hidden_state = residual + attention_out.astype(F32)
    routed_tokens, second_inverse = rms_parts(hidden_state, second_gain)
    routed_low = routed_tokens.astype(BF16)
    logits = matmul(routed_low, router)
    chosen = jnp.where(mask, logits, -1e30)
    gate_terms = jnp.where(mask, jnp.exp(chosen - jnp.max(chosen, axis=-1, keepdims=True)), 0.0)
    gates = gate_terms / jnp.sum(gate_terms, axis=-1, keepdims=True)
    gates_high, gates_low = split_high(gates)
    all_rows = plane_gather(jnp.concatenate([routed_low, gates_high, gates_low], axis=1), 4)

    first_expert = (lax.axis_index("dp") * 8 + lax.axis_index("context")) * local
    here = lax.dynamic_slice(all_grads, (0, width + first_expert), (all_grads.shape[0], local))
    blocks = here.reshape(owners, rows, local)
    before = jnp.tril(jnp.ones((rows, rows), BF16), -1)
    rank = jnp.einsum("ts,bse->bte", before, blocks, preferred_element_type=F32)
    rank = rank + (CAPACITY * (jnp.arange(owners) % 2)).astype(F32)[:, None, None]
    place = jnp.where(blocks > 0, rank, -1.0).astype(jnp.int32).reshape(owners * rows, local)
    gate_here = lax.dynamic_slice(
        all_rows, (0, width + first_expert), (all_rows.shape[0], local)
    ).astype(F32) + lax.dynamic_slice(
        all_rows, (0, width + expert_count + first_expert), (all_rows.shape[0], local)
    ).astype(F32)
    lane = jnp.arange(128, dtype=jnp.int32)[None, :]
    starts = jnp.arange(2 * local, dtype=jnp.int32)
    wanted = first_expert + starts // 2 + expert_count * (starts % 2)
    lanes = (lane == wanted[:, None]).astype(F32)
    out_terms, back_terms, gate_grad, up_grad, down_grad = experts(
        all_rows, all_grads, place.T, place, gate_here.T, lanes, gate_weight, up_weight, down_weight
    )
    back_sum = plane_scatter(back_terms, 5)
    out_sum = plane_scatter(out_terms, 6)
    experts_out, back_total = tensor_sum([out_sum, back_sum], 7)
    output = hidden_state + experts_out.astype(F32)

    grad_out = cotangent.astype(F32)
    shares = back_total[:, width : width + expert_count].astype(F32)
    shares = shares + back_total[:, width + expert_count :].astype(F32)
    grad_logits = (shares - gates * jnp.sum(shares, axis=-1, keepdims=True)).astype(BF16)
    grad_routed = back_total[:, :width].astype(F32) + matmul(grad_logits, router, ((1,), (1,)))
    grad_hidden_norm, second_gain_grad = rms_back(
        hidden_state, second_inverse, second_gain, grad_routed
    )
    grad_hidden = grad_out + grad_hidden_norm
    grad_mixed = grad_hidden.astype(BF16)
    grad_attended = matmul(grad_mixed, output_turned).astype(BF16).reshape(rows, heads, head)
    raw_again = jnp.einsum("bgd,ld->bgl", query_low, all_keys, preferred_element_type=F32)
    masked = jnp.where(allowed, raw_again * scale, -1e30)
    exponent = jnp.exp(masked - jnp.max(masked, axis=-1, keepdims=True))
    probabilities = exponent / jnp.sum(exponent, axis=-1, keepdims=True)
    grad_probs = jnp.einsum("bgd,ld->bgl", grad_attended, all_values, preferred_element_type=F32)
    row_delta = jnp.sum(probabilities * grad_probs, axis=-1, keepdims=True)
    grad_raw = (scale * probabilities * (grad_probs - row_delta)).astype(BF16)
    grad_query = jnp.einsum("bgl,ld->bgd", grad_raw, all_keys, preferred_element_type=F32)
    grad_keys_all = jnp.einsum("bgl,bgd->ld", grad_raw, query_low, preferred_element_type=F32)
    grad_values_all = jnp.einsum(
        "bgl,bgd->ld", probabilities.astype(BF16), grad_attended, preferred_element_type=F32
    )
    grad_both = context_scatter(jnp.concatenate([grad_keys_all, grad_values_all], axis=1), 8)
    grad_keys = grad_both[:, :head].reshape(rows, 1, head)
    grad_values = grad_both[:, head:]
    grad_query_raw, query_gain_part = rms_back(
        query_unrotated,
        query_inverse,
        query_gain_wide,
        rotate_back(grad_query, cosine_table, sine_table),
    )
    grad_key_raw, key_gain_part = rms_back(
        key_unrotated, key_inverse, key_gain_wide, rotate_back(grad_keys, cosine_table, sine_table)
    )
    grad_qkv = jnp.concatenate(
        [
            grad_query_raw.astype(BF16).reshape(rows, query_columns),
            grad_key_raw.astype(BF16).reshape(rows, key_columns),
            grad_values.astype(BF16),
        ],
        axis=1,
    )
    grad_normed_part = matmul(grad_qkv, qkv_matrix, ((1,), (1,)))
    gain_parts = jnp.pad(jnp.stack([query_gain_part, key_gain_part]), ((0, rows - 2), (0, 0)))
    (normed_total,) = tensor_sum([jnp.concatenate([grad_normed_part, gain_parts], axis=1)], 9)
    grad_normed = normed_total[:, :width].astype(F32)
    head_gains = normed_total[:2, width:].astype(F32)
    grad_tokens_norm, first_gain_grad = rms_back(residual, first_inverse, first_gain, grad_normed)
    tokens_grad = grad_hidden + grad_tokens_norm

    def spread(vector):
        each = vector.shape[0] // owners
        return jnp.pad(vector.reshape(owners, each), ((0, 0), (0, shard - each))).reshape(1, -1)

    few_rows = jnp.concatenate(
        [
            matmul(grad_logits, routed_low, ((0,), (0,))),
            first_gain_grad[None],
            second_gain_grad[None],
            spread(head_gains[0]),
            spread(head_gains[1]),
            jnp.zeros((128 - expert_count - 4, width), F32),
        ],
        axis=0,
    ).astype(BF16)
    terms = weight_terms(normed_low, grad_qkv, grad_mixed, attended_low, few_rows)
    total = plane_scatter(terms, 10)
    after = qkv_columns + query_columns
    few = head // owners
    return (
        output[None],
        tokens_grad[None],
        total[:, after + expert_count],
        total[:, :query_columns],
        total[:, query_columns : query_columns + key_columns],
        total[:, query_columns + key_columns : qkv_columns],
        total[:few, after + expert_count + 2],
        total[:few, after + expert_count + 3],
        total[:, qkv_columns:after].T,
        total[:, after + expert_count + 1],
        total[:, after : after + expert_count],
        gate_grad,
        up_grad,
        down_grad,
    )


def solution(mesh):
    plane_rows = P(PLANE)
    both = P(PLANE, "tensor")
    tokens = P("dp", "context", None)
    expert_rows = P(PLANE, "tensor", None)
    router = P(PLANE, None)
    output_matrix = P("tensor", PLANE)
    return jax.shard_map(
        per_device,
        mesh=mesh,
        in_specs=(
            tokens, tokens, plane_rows, both, both, both, P(), P(), output_matrix, plane_rows,
            router, expert_rows, expert_rows, expert_rows, tokens,
        ),
        out_specs=(
            tokens, tokens, plane_rows, both, both, both, plane_rows, plane_rows, output_matrix,
            plane_rows, router, expert_rows, expert_rows, expert_rows,
        ),
        check_vma=False,
    )
```

```python
import functools
import math

import jax
import jax.numpy as jnp
from jax import lax
from jax.experimental import pallas as pl
from jax.experimental.pallas import tpu as pltpu
from jax.sharding import PartitionSpec as P

MESH = pl.DeviceIdType.MESH
F32 = jnp.float32
BF16 = jnp.bfloat16
MIB = 1 << 20


def rows_at(ref, start, size):
    return ref.at[pl.ds(start, size)]


class Arrival:
    def __init__(self, make):
        self.make = make

    def wait_recv(self):
        self.make().wait_recv()


class Links:
    def __init__(self, send_sem, recv_sem):
        self.send_sem, self.recv_sem = send_sem, recv_sem
        self.copies = []

    def send(self, source, target, device, arriving):
        index = len(self.copies)

        def copy(start, end):
            return pltpu.make_async_remote_copy(
                src_ref=start(),
                dst_ref=end(),
                send_sem=self.send_sem.at[index],
                recv_sem=self.recv_sem.at[index],
                device_id=device,
                device_id_type=MESH,
            )

        copy(source, target).start()
        self.copies.append(lambda: copy(source, target))
        return Arrival(lambda: copy(arriving, arriving))

    def finish(self):
        for copy in self.copies:
            copy().wait_send()


def greet(devices):
    barrier = pltpu.get_barrier_semaphore()
    for device in devices:
        pl.semaphore_signal(barrier, inc=1, device_id=device, device_id_type=MESH)
    pl.semaphore_wait(barrier, len(devices))


def plane_place():
    y = lax.axis_index("dp")
    position = lax.axis_index("context")
    z = position // 2
    core = position - 2 * z
    ys = [lax.rem(y + step, 4) for step in range(4)]
    zs = [lax.rem(z + step, 4) for step in range(4)]
    near = {(a, b): {"dp": ys[a], "context": zs[b] * 2 + core} for a in range(4) for b in range(4)}
    slots = {
        (a, b, other): ys[a] * 8 + zs[b] * 2 + (1 - core if other else core)
        for a in range(4)
        for b in range(4)
        for other in (False, True)
    }

    def device(step):
        return near[step[0] % 4, step[1] % 4]

    def slot(step, other=False):
        return slots[step[0] % 4, step[1] % 4, other]

    sibling = {"context": 2 * z + 1 - core}
    return device, slot, sibling


def along(first, second, order):
    return (first, second) if order == 0 else (second, first)


NEAR = ((1, 0), (-1, 0), (0, 1), (0, -1))


class Gather:
    def __init__(self, links, mine, whole, own_sem):
        self.links, self.mine, self.whole, self.own_sem = links, mine, whole, own_sem
        self.device, self.slot, self.sibling = plane_place()
        self.rows = mine.shape[0]
        self.beside = {}

    def rows_of(self, order, part):
        start, size = order * (self.rows // 2), self.rows // 2
        if part == 2:
            return 0, self.rows
        if part == 1:
            return start + size // 2, size // 2
        if part == 0:
            return start, size // 2
        return start, size

    def region(self, order, place, part, other=False):
        def make():
            start, size = self.rows_of(order, part)
            base = self.slot(along(*place, order), other) * self.rows + start
            return self.whole.at[pl.ds(pl.multiple_of(base, 16), size)]

        return make

    def push(self, order, place, part, axis, sign):
        step = along(sign, 0, order) if axis == 0 else along(0, sign, order)
        source = self.region(order, place, part)
        if place == (0, 0):
            start, size = self.rows_of(order, part)

            def source():
                return self.mine.at[pl.ds(start, size)]

        came = (place[0] - sign, place[1]) if axis == 0 else (place[0], place[1] - sign)
        return self.links.send(
            source,
            self.region(order, place, part),
            self.device(step),
            self.region(order, came, part),
        )

    def share(self, order, place, part=None):
        source = self.region(order, place, part)
        if part == 2:

            def source():
                return self.mine

        self.beside[order, along(*place, order)] = self.links.send(
            source,
            self.region(order, place, part),
            self.sibling,
            self.region(order, place, part, True),
        )

    def own(self):
        return pltpu.make_async_copy(self.mine, self.region(0, (0, 0), 2)(), self.own_sem)

    def wait_beside(self, places=None):
        for key in list(self.beside):
            if places is None or key[1] in places:
                self.beside.pop(key).wait_recv()

    def steps(self):
        got = {}
        self.own().start()
        for order in range(2):
            for sign in (1, -1):
                got[order, sign] = self.push(order, (0, 0), None, 0, sign)
        for order in range(2):
            for sign in (1, -1):
                got[order, 0, sign] = self.push(order, (0, 0), None, 1, sign)
        self.share(0, (0, 0), 2)
        yield
        for order in range(2):
            for sign in (1, -1):
                got[order, sign].wait_recv()
                got[order, "far", sign] = self.push(
                    order, (-sign, 0), 0 if sign == 1 else 1, 0, sign
                )
            for sign in (1, -1):
                for way in (1, -1):
                    got[order, -sign, way] = self.push(order, (-sign, 0), None, 1, way)
                self.share(order, (-sign, 0))

        def near(i):
            for order in range(2):
                for way in (1, -1):
                    got[order, i, way].wait_recv()
                    got[order, i, "far", way] = self.push(
                        order, (i, -way), 0 if way == 1 else 1, 1, way
                    )
                    self.share(order, (i, -way))

        def far(i):
            for order in range(2):
                for way in (1, -1):
                    got[order, i, "far", way].wait_recv()
                self.share(order, (i, 2))

        yield
        near(0)
        yield
        for order in range(2):
            for sign in (1, -1):
                got[order, "far", sign].wait_recv()
            for way in (1, -1):
                got[order, 2, way] = self.push(order, (2, 0), None, 1, way)
            self.share(order, (2, 0))
        yield
        near(1)
        yield
        near(-1)
        yield
        far(0)
        yield
        near(2)
        far(1)
        yield
        far(-1)
        yield
        far(2)


def finish_gather(gather, steps, own=True):
    for _ in steps:
        pass
    gather.wait_beside()
    if own:
        gather.own().wait()


GATHER_COPIES = 2 * 20 + 1 + 2 * 15


def gather_body(mine, whole, send_sem, recv_sem, own_sem):
    device, slot, sibling = plane_place()
    greet([device(step) for step in NEAR] + [sibling])
    links = Links(send_sem, recv_sem)
    gather = Gather(links, mine, whole, own_sem)
    finish_gather(gather, gather.steps())
    links.finish()


def plane_gather(array, collective_id):
    return pl.pallas_call(
        gather_body,
        out_shape=jax.ShapeDtypeStruct((32 * array.shape[0],) + array.shape[1:], array.dtype),
        in_specs=[pl.BlockSpec(memory_space=pl.ANY)],
        out_specs=pl.BlockSpec(memory_space=pl.ANY),
        scratch_shapes=[
            pltpu.SemaphoreType.DMA((GATHER_COPIES,)),
            pltpu.SemaphoreType.DMA((GATHER_COPIES,)),
            pltpu.SemaphoreType.DMA,
        ],
        compiler_params=pltpu.CompilerParams(
            collective_id=collective_id, has_side_effects=True, vmem_limit_bytes=56 * MIB
        ),
    )(array)


def add_rows(target, sources, offset, size, chunk=16):
    def step(k, carry):
        base = pl.multiple_of(k * chunk, chunk)
        at = pl.ds(offset + base, chunk)
        total = target[at].astype(F32)
        for source, start in sources:
            total = total + source[pl.ds(start + base, chunk)].astype(F32)
        target[at] = total.astype(target.dtype)
        return carry

    lax.fori_loop(0, size // chunk, step, 0)


SLOTS = (
    (2, 2), (1, 2), (2, 1), (-1, 2), (2, -1), (0, 2), (2, 0),
    (1, 1), (1, -1), (-1, 1), (-1, -1), (0, 1), (1, 0), (0, -1), (-1, 0), (0, 0),
)


def scatter_steps(links, rows, part_ref, out_ref, held, near, landed, own_sem):
    device, slot, sibling = plane_place()
    half, quarter = rows // 2, rows // 4
    index = {place: k for k, place in enumerate(SLOTS)}

    def base(place):
        return index[place] * rows

    def slot_rows(place, other):
        return rows_at(part_ref, pl.multiple_of(slot(place, other) * rows, 16), rows)

    loads, shares = {}, {}
    for k, place in enumerate(SLOTS):
        copy = pltpu.make_async_copy(
            slot_rows(place, False), held.at[pl.ds(base(place), rows)], own_sem.at[k]
        )
        copy.start()
        loads[place] = copy
        here = functools.partial(rows_at, near, base(place), rows)
        there = functools.partial(slot_rows, place, True)
        shares[place] = links.send(there, here, sibling, here)
    merged = set()

    def ready(order, place):
        place = along(*place, order)
        if place not in merged:
            merged.add(place)
            loads[place].wait()
            shares[place].wait_recv()
            add_rows(held, [(near, base(place))], base(place), rows)
        return base(place) + order * half

    room = [0]

    def push(start, size, order, axis, sign):
        step = along(sign, 0, order) if axis == 0 else along(0, sign, order)
        at = room[0]
        room[0] += size
        here = functools.partial(rows_at, landed, at, size)
        source = functools.partial(rows_at, held, start, size)
        return links.send(source, here, device(step), here), at

    got = {}

    def reduce_ring(key, order, axis, places, stage):
        opposite, plus, minus, mine = places
        if stage == 0:
            start = ready(order, opposite)
            got[key, 0] = push(start, quarter, order, axis, 1)
            got[key, 1] = push(start + quarter, quarter, order, axis, -1)
        if stage == 1:
            start = ready(order, plus)
            copy, at = got[key, 0]
            copy.wait_recv()
            add_rows(held, [(landed, at)], start, quarter)
            got[key, 2] = push(start, half, order, axis, 1)
            start = ready(order, minus)
            copy, at = got[key, 1]
            copy.wait_recv()
            add_rows(held, [(landed, at)], start + quarter, quarter)
            got[key, 3] = push(start, half, order, axis, -1)
        if stage == 2:
            start = ready(order, mine)
            sources = []
            for k in (2, 3):
                copy, at = got[key, k]
                copy.wait_recv()
                sources.append((landed, at))
            if axis == 1:
                add_rows(held, sources, start, half)
            else:
                for k in range(half // 16):
                    total = held[pl.ds(start + 16 * k, 16)].astype(F32)
                    for source, at in sources:
                        total = total + source[pl.ds(at + 16 * k, 16)].astype(F32)
                    out_ref[pl.ds(order * half + 16 * k, 16)] = total

    def ring(i, order, stage):
        reduce_ring((order, i), order, 1, [(i, j) for j in (2, 1, -1, 0)], stage)

    def last(order, stage):
        reduce_ring((order, "last"), order, 0, [(i, 0) for i in (2, 1, -1, 0)], stage)

    yield
    for i in (2, 1, -1, 0):
        for order in range(2):
            ring(i, order, 0)
    for i in (2, 1, -1, 0):
        yield
        for order in range(2):
            ring(i, order, 1)
    yield
    for order in range(2):
        ring(2, order, 2)
        last(order, 0)
    yield
    for order in range(2):
        ring(1, order, 2)
        ring(-1, order, 2)
        last(order, 1)
    yield
    for order in range(2):
        ring(0, order, 2)
        last(order, 2)


SCATTER_COPIES = 16 + 2 * 20


def scatter_scratch(rows, columns):
    return [
        pltpu.VMEM((16 * rows, columns), BF16),
        pltpu.VMEM((16 * rows, columns), BF16),
        pltpu.VMEM((15 * rows, columns), BF16),
        pltpu.SemaphoreType.DMA((16,)),
    ]


def scatter_body(rows, part_ref, out_ref, held, near, landed, own_sem, send_sem, recv_sem):
    device, slot, sibling = plane_place()
    greet([device(step) for step in NEAR] + [sibling])
    links = Links(send_sem, recv_sem)
    for _ in scatter_steps(links, rows, part_ref, out_ref, held, near, landed, own_sem):
        pass
    links.finish()


def plane_scatter(part, collective_id):
    rows, columns = part.shape[0] // 32, part.shape[1]
    return pl.pallas_call(
        functools.partial(scatter_body, rows),
        out_shape=jax.ShapeDtypeStruct((rows, columns), F32),
        in_specs=[pl.BlockSpec(memory_space=pl.ANY)],
        out_specs=pl.BlockSpec(memory_space=pltpu.VMEM),
        scratch_shapes=scatter_scratch(rows, columns)
        + [pltpu.SemaphoreType.DMA((SCATTER_COPIES,)), pltpu.SemaphoreType.DMA((SCATTER_COPIES,))],
        compiler_params=pltpu.CompilerParams(
            collective_id=collective_id, has_side_effects=True, vmem_limit_bytes=56 * MIB
        ),
    )(part)


class TensorSum:
    def __init__(self, links, held, landed, out):
        self.links, self.held, self.landed, self.out = links, held, landed, out
        self.x = lax.axis_index("tensor")
        self.quarter = held.shape[0] // 4

    def device(self, step):
        return {"tensor": (self.x + step) % 4}

    def rows(self, step):
        return pl.ds(pl.multiple_of(((self.x + step) % 4) * self.quarter, 16), self.quarter)

    def part(self, ref, step):
        return ref.at[self.rows(step)]

    def send(self):
        self.got = []
        for step in (1, 3, 2):
            here = functools.partial(
                rows_at, self.landed, (step - 1) * self.quarter, self.quarter
            )
            source = functools.partial(self.part, self.held, step)
            self.got.append(self.links.send(source, here, self.device(step), here))

    def add(self, exact):
        for copy in self.got:
            copy.wait_recv()
        mine = self.rows(0)
        total = exact[mine].astype(F32)
        for k in range(3):
            total = total + self.landed[k * self.quarter : (k + 1) * self.quarter].astype(F32)
        self.out[mine] = total.astype(BF16)
        here = functools.partial(self.part, self.out, 0)
        self.got = [
            self.links.send(
                here, here, self.device(step), functools.partial(self.part, self.out, -step)
            )
            for step in (1, 3, 2)
        ]

    def wait(self):
        for copy in self.got:
            copy.wait_recv()


TENSOR_COPIES = 6


def tensor_scratch(rows, columns):
    return [pltpu.VMEM((rows, columns), BF16), pltpu.VMEM((rows * 3 // 4, columns), BF16)]


def greet_all(context):
    device, slot, sibling = plane_place()
    x, position = lax.axis_index("tensor"), lax.axis_index("context")
    others = [{"tensor": (x + step) % 4} for step in range(1, 4)]
    if context:
        others += [device(step) for step in NEAR[:2]]
        others += [{"context": (position + step) % 8} for step in range(1, 8)]
    else:
        others += [device(step) for step in NEAR] + [sibling]
    greet(others)


def scatter_sum_body(rows, part_ref, out, held, near, landed, own_sem, exact, low, came, send_sem, recv_sem):
    greet_all(False)
    links = Links(send_sem, recv_sem)
    for _ in scatter_steps(links, rows, part_ref, exact, held, near, landed, own_sem):
        pass
    total = TensorSum(links, low, came, out)
    low[...] = exact[...].astype(BF16)
    total.send()
    total.add(exact)
    total.wait()
    links.finish()


def scatter_sum(part, collective_id):
    rows, columns = part.shape[0] // 32, part.shape[1]
    copies = SCATTER_COPIES + TENSOR_COPIES
    return pl.pallas_call(
        functools.partial(scatter_sum_body, rows),
        out_shape=jax.ShapeDtypeStruct((rows, columns), BF16),
        in_specs=[pl.BlockSpec(memory_space=pl.ANY)],
        out_specs=pl.BlockSpec(memory_space=pltpu.VMEM),
        scratch_shapes=scatter_scratch(rows, columns)
        + [pltpu.VMEM((rows, columns), F32)]
        + tensor_scratch(rows, columns)
        + [pltpu.SemaphoreType.DMA((copies,)), pltpu.SemaphoreType.DMA((copies,))],
        compiler_params=pltpu.CompilerParams(
            collective_id=collective_id, has_side_effects=True, vmem_limit_bytes=56 * MIB
        ),
    )(part)


EPSILON = 1e-06
THETA = 1000000.0
PLANE = ("dp", "context")


def dot(a, b, contract):
    return lax.dot_general(a, b, (contract, ((), ())), preferred_element_type=F32)


PAIR = 256
CAPACITY = 32


def weight_terms_body(normed, grad_qkv, mixed, attended, few, out):
    first, second = grad_qkv.shape[1], attended.shape[1]
    out[:, :first] = dot(normed[...], grad_qkv[...], ((0,), (0,))).astype(BF16)
    out[:, first : first + second] = dot(mixed[...], attended[...], ((0,), (0,))).astype(BF16)
    out[:, first + second :] = few[...].astype(F32).T.astype(BF16)


def weight_terms(normed, grad_qkv, mixed, attended, few):
    width = normed.shape[1]
    columns = grad_qkv.shape[1] + attended.shape[1] + few.shape[0]
    block = 256

    def part(a):
        return pl.BlockSpec((a.shape[0], block), lambda i: (0, i))

    def whole(a):
        return pl.BlockSpec(a.shape, lambda i: (0, 0))

    return pl.pallas_call(
        weight_terms_body,
        grid=(width // block,),
        out_shape=jax.ShapeDtypeStruct((width, columns), BF16),
        in_specs=[part(normed), whole(grad_qkv), part(mixed), whole(attended), part(few)],
        out_specs=pl.BlockSpec((block, columns), lambda i: (i, 0)),
        compiler_params=pltpu.CompilerParams(vmem_limit_bytes=32 * MIB),
    )(normed, grad_qkv, mixed, attended, few)


def rotate(values, cosines, sines):
    return values * cosines + pltpu.roll(values, values.shape[1] // 2, 1) * sines


def front_body(
    head, packed_ref, cot_ref, x_ref, cos_ref, sin_ref, qg_ref, kg_ref,
    weights_out, cot_out, raw_out, normed_out, query_out, both_out, attended_out, mixed_out,
    weights, part, held, landed, keys, send_sem, recv_sem, own_sem,
):
    rows, width = x_ref.shape
    query_columns = attended_out.shape[1]
    heads = query_columns // head
    scale = head ** (-0.5)
    position = lax.axis_index("context")

    def context_device(step):
        return {"context": (position + step) % 8}

    greet_all(True)
    links = Links(send_sem, recv_sem)
    weight_gather = Gather(links, packed_ref, weights, own_sem.at[0])
    cot_gather = Gather(links, cot_ref, cot_out, own_sem.at[1])
    first, second = weight_gather.steps(), cot_gather.steps()
    next(first, None)
    values = x_ref[...].astype(F32)
    inverse = lax.rsqrt(jnp.mean(values * values, axis=-1, keepdims=True) + EPSILON)
    next(first, None)
    next(first, None)
    next(first, None)
    next(second, None)
    next(first, None)
    next(first, None)
    next(second, None)
    finish_gather(weight_gather, first)
    store = pltpu.make_async_copy(weights, weights_out, own_sem.at[2])
    store.start()
    last = query_columns * 2 + 2 * head
    take = jnp.where(
        lax.broadcasted_iota(jnp.int32, (8, 128), 1) == 64, 1.0, 0.0
    ).astype(BF16)
    gain = dot(take, weights[:, last : last + 128], ((1,), (1,)))[0:1]
    normed_out[...] = (x_ref[...].astype(F32) * inverse * gain).astype(BF16)

    def turn(values, gain_row):
        inverse = lax.rsqrt(jnp.mean(values * values, axis=-1, keepdims=True) + EPSILON)
        return rotate(values * inverse * gain_row, cos_ref[...], sin_ref[...])

    normed = normed_out[...]
    raw = dot(normed, weights[:, query_columns : query_columns + 2 * head], ((1,), (0,)))
    raw_out[:, query_columns:] = raw[:, :head]
    keys[:, :head] = turn(raw[:, :head], kg_ref[...]).astype(BF16)
    keys[:, head:] = raw[:, head:].astype(BF16)

    def context_rows(step):
        return both_out.at[pl.ds(pl.multiple_of(((position + step) % 8) * rows, 16), rows)]

    own = pltpu.make_async_copy(keys, context_rows(0), own_sem.at[3])
    own.start()
    got = [
        links.send(
            lambda: keys,
            functools.partial(context_rows, 0),
            context_device(step),
            functools.partial(context_rows, -step),
        )
        for step in range(1, 8)
    ]
    next(second, None)
    for part_index in range(4):
        columns = slice(part_index * query_columns // 4, (part_index + 1) * query_columns // 4)
        raw_out[:, columns] = dot(normed, weights[:, columns], ((1,), (0,)))
    for h in range(heads):
        columns = slice(h * head, (h + 1) * head)
        query_out[:, columns] = turn(raw_out[:, columns], qg_ref[...]).astype(BF16)
    own.wait()
    for copy in got:
        copy.wait_recv()
    next(second, None)
    length = 8 * rows
    key_positions = lax.broadcasted_iota(jnp.int32, (rows, length), 1)
    query_positions = lax.broadcasted_iota(jnp.int32, (rows, length), 0) + position * rows
    allowed = key_positions <= query_positions
    for h in range(heads):
        columns = slice(h * head, (h + 1) * head)
        scores = dot(query_out[:, columns], both_out[:, :head], ((1,), (1,))) * scale
        scores = jnp.where(allowed, scores, -1e30)
        terms = jnp.exp(scores - jnp.max(scores, axis=-1, keepdims=True))
        probabilities = (terms * (1.0 / jnp.sum(terms, axis=-1, keepdims=True))).astype(BF16)
        attended_out[:, columns] = dot(probabilities, both_out[:, head:], ((1,), (0,))).astype(BF16)
    next(second, None)
    matrix = slice(query_columns + 2 * head, last)
    for block in range(4):
        columns = slice(block * width // 4, (block + 1) * width // 4)
        product = dot(attended_out[...], weights[columns, matrix], ((1,), (1,)))
        part[:, columns] = product
        held[:, columns] = product.astype(BF16)
    total = TensorSum(links, held, landed, mixed_out)
    total.send()
    next(second, None)
    next(second, None)
    next(second, None)
    total.add(part)
    finish_gather(cot_gather, second)
    total.wait()
    store.wait()
    links.finish()


def front(packed, cotangent, tokens, cosines, sines, query_gain, key_gain, query_columns, collective_id):
    rows, width = tokens.shape
    head = query_gain.shape[1]
    copies = 2 * GATHER_COPIES + 7 + TENSOR_COPIES
    vmem = pl.BlockSpec(memory_space=pltpu.VMEM)
    hbm = pl.BlockSpec(memory_space=pl.ANY)
    return pl.pallas_call(
        functools.partial(front_body, head),
        out_shape=[
            jax.ShapeDtypeStruct((32 * packed.shape[0], packed.shape[1]), BF16),
            jax.ShapeDtypeStruct((32 * cotangent.shape[0], cotangent.shape[1]), BF16),
            jax.ShapeDtypeStruct((rows, query_columns + head), F32),
            jax.ShapeDtypeStruct((rows, width), BF16),
            jax.ShapeDtypeStruct((rows, query_columns), BF16),
            jax.ShapeDtypeStruct((8 * rows, 2 * head), BF16),
            jax.ShapeDtypeStruct((rows, query_columns), BF16),
            jax.ShapeDtypeStruct((rows, width), BF16),
        ],
        in_specs=[hbm, hbm] + [vmem] * 5,
        out_specs=[hbm, hbm] + [vmem] * 6,
        scratch_shapes=[
            pltpu.VMEM((32 * packed.shape[0], packed.shape[1]), BF16),
            pltpu.VMEM((rows, width), F32),
            pltpu.VMEM((rows, width), BF16),
            pltpu.VMEM((rows * 3 // 4, width), BF16),
            pltpu.VMEM((rows, 2 * head), BF16),
            pltpu.SemaphoreType.DMA((copies,)),
            pltpu.SemaphoreType.DMA((copies,)),
            pltpu.SemaphoreType.DMA((4,)),
        ],
        compiler_params=pltpu.CompilerParams(
            collective_id=collective_id, has_side_effects=True, vmem_limit_bytes=56 * MIB
        ),
    )(packed, cotangent, tokens, cosines, sines, query_gain, key_gain)


def back_body(
    head, part_ref, weights_ref, mixed_ref, query_ref, both_ref, raw_ref, cos_ref, sin_ref, qg_ref, kg_ref,
    out_ref, grad_out, normed_out,
    held, near, landed, own_sem, exact, low, came,
    weights, stacked, grads, chances, slopes, key_terms, key_came, normed, normed_low, normed_came,
    send_sem, recv_sem, load_sem,
):
    rows, width = mixed_ref.shape
    query_columns = query_ref.shape[1]
    heads = query_columns // head
    scale = head ** (-0.5)
    position = lax.axis_index("context")

    def context_device(step):
        return {"context": (position + step) % 8}

    load = pltpu.make_async_copy(weights_ref, weights, load_sem)
    load.start()
    greet_all(True)
    links = Links(send_sem, recv_sem)
    sums = scatter_steps(links, rows, part_ref, exact, held, near, landed, own_sem)
    next(sums, None)
    load.wait()
    matrix = slice(query_columns + 2 * head, 2 * query_columns + 2 * head)
    attended = dot(mixed_ref[...], weights[:, matrix], ((1,), (0,))).astype(BF16)
    for h in range(heads):
        columns, here = slice(h * head, (h + 1) * head), slice(h * rows, (h + 1) * rows)
        stacked[here] = query_ref[:, columns]
        grads[here] = attended[:, columns]
    next(sums, None)
    length = 8 * rows
    key_positions = lax.broadcasted_iota(jnp.int32, (rows, length), 1)
    query_positions = lax.broadcasted_iota(jnp.int32, (rows, length), 0) + position * rows
    allowed = key_positions <= query_positions
    for h in range(heads):
        here = slice(h * rows, (h + 1) * rows)
        scores = dot(stacked[here], both_ref[:, :head], ((1,), (1,))) * scale
        scores = jnp.where(allowed, scores, -1e30)
        terms = jnp.exp(scores - jnp.max(scores, axis=-1, keepdims=True))
        probabilities = terms * (1.0 / jnp.sum(terms, axis=-1, keepdims=True))
        chances[here] = probabilities.astype(BF16)
        grad = dot(grads[here], both_ref[:, head:], ((1,), (1,)))
        delta = jnp.sum(probabilities * grad, axis=-1, keepdims=True)
        slopes[here] = (scale * probabilities * (grad - delta)).astype(BF16)
    key_terms[:, :head] = dot(slopes[...], stacked[...], ((0,), (0,))).astype(BF16)
    key_terms[:, head:] = dot(chances[...], grads[...], ((0,), (0,))).astype(BF16)
    got = []
    for step in range(1, 8):
        source = functools.partial(
            rows_at, key_terms, pl.multiple_of(((position + step) % 8) * rows, 16), rows
        )
        target = functools.partial(rows_at, key_came, (step - 1) * rows, rows)
        got.append(links.send(source, target, context_device(step), target))
    next(sums, None)

    def turn_back(values, grad, gain_row):
        grad = rotate(grad, cos_ref[...], -sin_ref[...])
        inverse = lax.rsqrt(jnp.mean(values * values, axis=-1, keepdims=True) + EPSILON)
        scaled = grad * gain_row
        mean = jnp.mean(scaled * values, axis=-1, keepdims=True)
        grad_gain = jnp.sum(grad * values * inverse, axis=0, keepdims=True)
        return inverse * scaled - values * (inverse * inverse * inverse) * mean, grad_gain

    query_gain = jnp.zeros((1, head), F32)
    for h in range(heads):
        columns, here = slice(h * head, (h + 1) * head), slice(h * rows, (h + 1) * rows)
        grad = dot(slopes[here], both_ref[:, :head], ((1,), (0,)))
        grad, gain = turn_back(raw_ref[:, columns], grad, qg_ref[...])
        grad_out[:, columns] = grad.astype(BF16)
        query_gain = query_gain + gain
    for copy in got:
        copy.wait_recv()
    mine = key_terms[pl.ds(pl.multiple_of(position * rows, 16), rows)].astype(F32)
    for k in range(7):
        mine = mine + key_came[k * rows : (k + 1) * rows].astype(F32)
    grad, key_gain = turn_back(raw_ref[:, query_columns:], mine[:, :head], kg_ref[...])
    grad_out[:, query_columns : query_columns + head] = grad.astype(BF16)
    grad_out[:, query_columns + head :] = mine[:, head:].astype(BF16)
    next(sums, None)
    for block in range(4):
        columns = slice(block * width // 4, (block + 1) * width // 4)
        product = dot(grad_out[...], weights[columns, : query_columns + 2 * head], ((1,), (1,)))
        normed[:, columns] = product
        normed_low[:, columns] = product.astype(BF16)
    row = lax.broadcasted_iota(jnp.int32, (rows, head), 0)
    gains = jnp.where(row == 0, query_gain, jnp.where(row == 1, key_gain, 0.0))
    normed[:, width:] = gains
    normed_low[:, width:] = gains.astype(BF16)
    total = TensorSum(links, normed_low, normed_came, normed_out)
    total.send()
    next(sums, None)
    total.add(normed)
    for _ in sums:
        pass
    output = TensorSum(links, low, came, out_ref)
    low[...] = exact[...].astype(BF16)
    output.send()
    total.wait()
    output.add(exact)
    output.wait()
    links.finish()


def back(part, weights, mixed, query_low, both, raw, cosines, sines, query_gain, key_gain, collective_id):
    rows, width = mixed.shape
    head = query_gain.shape[1]
    query_columns = query_low.shape[1]
    stacked = rows * (query_columns // head)
    copies = SCATTER_COPIES + 2 * TENSOR_COPIES + 7
    vmem = pl.BlockSpec(memory_space=pltpu.VMEM)
    hbm = pl.BlockSpec(memory_space=pl.ANY)
    return pl.pallas_call(
        functools.partial(back_body, head),
        out_shape=[
            jax.ShapeDtypeStruct((rows, width), BF16),
            jax.ShapeDtypeStruct((rows, query_columns + 2 * head), BF16),
            jax.ShapeDtypeStruct((rows, width + head), BF16),
        ],
        in_specs=[hbm, hbm] + [vmem] * 8,
        out_specs=[vmem] * 3,
        scratch_shapes=scatter_scratch(rows, width)
        + [pltpu.VMEM((rows, width), F32)]
        + tensor_scratch(rows, width)
        + [
            pltpu.VMEM(weights.shape, BF16),
            pltpu.VMEM((stacked, head), BF16),
            pltpu.VMEM((stacked, head), BF16),
            pltpu.VMEM((stacked, 8 * rows), BF16),
            pltpu.VMEM((stacked, 8 * rows), BF16),
            pltpu.VMEM((8 * rows, 2 * head), BF16),
            pltpu.VMEM((7 * rows, 2 * head), BF16),
            pltpu.VMEM((rows, width + head), F32),
        ]
        + tensor_scratch(rows, width + head)
        + [
            pltpu.SemaphoreType.DMA((copies,)),
            pltpu.SemaphoreType.DMA((copies,)),
            pltpu.SemaphoreType.DMA,
        ],
        compiler_params=pltpu.CompilerParams(
            collective_id=collective_id, has_side_effects=True, vmem_limit_bytes=60 * MIB
        ),
    )(part, weights, mixed, query_low, both, raw, cosines, sines, query_gain, key_gain)


WORK = (
    (0, 0), (1, 0), (-1, 0), (0, 1), (0, -1), (1, 1), (1, -1), (-1, 1),
    (-1, -1), (0, 2), (2, 0), (1, 2), (2, 1), (-1, 2), (2, -1), (2, 2),
)
PUMP = (2, 1, 1, 1, 1, 1, 1, 1)


def pack_work(axis, which):
    code = 0
    for step in range(len(WORK) // 2):
        code += (WORK[2 * step + which][axis] % 4) * 4**step
    return code


def middle_body(
    mine_ref, grads_ref, lane_ref, low_lane_ref, wg_ref, wu_ref, wd_ref,
    out_ref, back_ref, gg_ref, gu_ref, gd_ref,
    whole, given_ref, out_held, back_held, rows, pairs, inner, slope_g, slope_u, gg, gu, gd,
    send_sem, recv_sem, own_sem, load_sem, store_sem, weight_sem,
):
    local, units, width = wg_ref.shape
    per_pair = 2 * CAPACITY
    per_step = 2 * per_pair
    steps = len(WORK) // 2
    half = steps // 2
    device, slot, sibling = plane_place()
    y = lax.axis_index("dp")
    z = lax.axis_index("context") // 2
    greet([device(step) for step in NEAR] + [sibling])
    links = Links(send_sem, recv_sem)
    gather = Gather(links, mine_ref, whole, own_sem)
    pump = gather.steps()
    next(pump, None)

    def base_of(code_y, code_z):
        return pl.multiple_of((((y + code_y % 4) % 4) * 4 + (z + code_z % 4) % 4) * PAIR, PAIR)

    def load(bases):
        return [
            pltpu.make_async_copy(
                grads_ref.at[pl.ds(base, PAIR)], given_ref.at[pl.ds(k * PAIR, PAIR)], load_sem.at[k]
            )
            for k, base in enumerate(bases)
        ]

    def store(bases):
        copies = []
        for k, base in enumerate(bases):
            here = pl.ds(k * PAIR, PAIR)
            copies.append(
                pltpu.make_async_copy(out_held.at[here], out_ref.at[pl.ds(base, PAIR)], store_sem.at[k])
            )
            copies.append(
                pltpu.make_async_copy(
                    back_held.at[here], back_ref.at[pl.ds(base, PAIR)], store_sem.at[2 + k]
                )
            )
        return copies

    codes = [(pack_work(0, k), pack_work(1, k)) for k in range(2)]
    for copy in load([base_of(*code) for code in codes]):
        copy.start()
    row = lax.broadcasted_iota(jnp.int32, (128, 128), 0)
    column = lax.broadcasted_iota(jnp.int32, (128, 128), 1)
    before = jnp.where(column < row, 1.0, 0.0).astype(BF16)
    after = jnp.where(row < column, 1.0, 0.0).astype(BF16)

    def weight_grads(first):
        for e in range(local):
            for total, left, right in ((gd, inner, pairs), (gg, slope_g, rows), (gu, slope_u, rows)):
                for block in range(4):
                    columns = slice(block * width // 4, (block + 1) * width // 4)
                    product = dot(left[e], right[e, :, columns], ((0,), (0,)))
                    if not first:
                        product = product + total[e, :, columns]
                    total[e, :, columns] = product

    def work(step, carry):
        codes = [(carry[0], carry[1]), (carry[2], carry[3])]
        bases = [base_of(*code) for code in codes]
        for at in range(steps):

            @pl.when(step == at)
            def _():
                for _ in range(PUMP[at]):
                    next(pump, None)
                gather.wait_beside(WORK[2 * at : 2 * at + 2])
                if at == 0:
                    gather.own().wait()

        for copy in load(bases):
            copy.wait()
        at = pl.ds(pl.multiple_of((step % half) * per_step, per_step), per_step)
        places, weights = [], [[None, None] for _ in range(local)]
        slots = lax.broadcasted_iota(jnp.int32, (per_pair, PAIR), 0).astype(F32)
        lane_slots = lax.broadcasted_iota(jnp.int32, (PAIR, per_pair), 1).astype(F32)
        taken_parts, given_parts = [], []
        for p in range(2):
            tokens = slice(p * PAIR, (p + 1) * PAIR)
            marks = given_ref[tokens, width:]
            named = dot(low_lane_ref[...], marks, ((1,), (1,)))
            picks, spots = [], []
            ranks_across = [
                dot(named[:, k * 128 : (k + 1) * 128].astype(BF16), after, ((1,), (0,)))
                + float(CAPACITY * k)
                for k in range(2)
            ]
            ranks_down = [
                dot(before, marks[k * 128 : (k + 1) * 128], ((1,), (0,))) + float(CAPACITY * k)
                for k in range(2)
            ]
            across = jnp.where(named > 0.5, jnp.concatenate(ranks_across, axis=1), -1.0)
            down = jnp.where(marks.astype(F32) > 0.5, jnp.concatenate(ranks_down, axis=0), -1.0)
            for e in range(local):
                match = slots == across[e : e + 1]
                picks.append(jnp.where(match, 1.0, 0.0).astype(BF16))
                spot = jnp.sum(
                    jnp.where(lane_ref[2 * e : 2 * e + 1] > 0.5, down, 0.0), axis=1, keepdims=True
                )
                spots.append(jnp.where(lane_slots == spot, 1.0, 0.0).astype(BF16))
            places.append(jnp.concatenate(spots, axis=1))
            pick = jnp.concatenate(picks, axis=0)
            here = pl.ds(bases[p], PAIR)
            gates = dot(pick, whole[here, width:], ((1,), (0,)))
            taken_parts.append(dot(pick, whole[here, :width], ((1,), (0,))).astype(BF16))
            given = dot(pick, given_ref[tokens, :width], ((1,), (0,)))
            scaled = []
            for e in range(local):
                mine = slice(e * per_pair, (e + 1) * per_pair)
                lanes = lane_ref[2 * e : 2 * e + 1] + lane_ref[2 * e + 1 : 2 * e + 2]
                weight = jnp.sum(gates[mine] * lanes, axis=1, keepdims=True)
                weights[e][p] = weight
                scaled.append((weight * given[mine]).astype(BF16))
            given_parts.append(scaled)

        following = [(code[0] // 4, code[1] // 4) for code in codes]

        @pl.when(step < steps - 1)
        def _():
            for copy in load([base_of(*code) for code in following]):
                copy.start()

        sent, returned = [], []
        for e in range(local):
            weight = jnp.concatenate(weights[e], axis=0)
            mine = slice(e * per_pair, (e + 1) * per_pair)
            taken = jnp.concatenate([part[mine] for part in taken_parts], axis=0)
            given = jnp.concatenate([part[e] for part in given_parts], axis=0)
            rows[e, at] = taken
            pairs[e, at] = given
            gate = dot(taken, wg_ref[e], ((1,), (1,)))
            up = dot(taken, wu_ref[e], ((1,), (1,)))
            grad_inner = dot(given, wd_ref[e], ((1,), (1,)))
            sigmoid = jax.nn.sigmoid(gate)
            active = gate * sigmoid
            hidden = (active * up).astype(BF16)
            inner[e, at] = hidden
            sent.append((dot(hidden, wd_ref[e], ((1,), (0,))) * weight).astype(BF16))
            share = jnp.sum(hidden.astype(F32) * grad_inner, axis=1, keepdims=True)
            grad_gate = (grad_inner * up * sigmoid * (1.0 + gate * (1.0 - sigmoid))).astype(BF16)
            grad_up = (grad_inner * active).astype(BF16)
            slope_g[e, at] = grad_gate
            slope_u[e, at] = grad_up
            grad = dot(grad_gate, wg_ref[e], ((1,), (0,)))
            grad = grad + dot(grad_up, wu_ref[e], ((1,), (0,)))
            high = share.astype(BF16).astype(F32)
            lanes = high * lane_ref[2 * e : 2 * e + 1] + (share - high) * lane_ref[2 * e + 1 : 2 * e + 2]
            returned.append((grad.astype(BF16), lanes.astype(BF16)))

        @pl.when(step > 0)
        def _():
            for copy in store(bases):
                copy.wait()

        for p in range(2):
            tokens = slice(p * PAIR, (p + 1) * PAIR)
            mine = slice(p * per_pair, (p + 1) * per_pair)
            out_rows = jnp.concatenate([s[mine] for s in sent], axis=0)
            out_held[tokens] = dot(places[p], out_rows, ((1,), (0,))).astype(BF16)
            back_rows = jnp.concatenate([r[0][mine] for r in returned], axis=0)
            back_held[tokens, :width] = dot(places[p], back_rows, ((1,), (0,))).astype(BF16)
            lane_rows = jnp.concatenate([r[1][mine] for r in returned], axis=0)
            back_held[tokens, width:] = dot(places[p], lane_rows, ((1,), (0,))).astype(BF16)
        for copy in store(bases):
            copy.start()

        @pl.when(step == half - 1)
        def _():
            weight_grads(True)

        return tuple(part for code in following for part in code)

    last = lax.fori_loop(0, steps, work, tuple(part for code in codes for part in code))
    weight_grads(False)
    stores = [
        pltpu.make_async_copy(total, ref, weight_sem.at[k])
        for k, (total, ref) in enumerate(((gg, gg_ref), (gu, gu_ref), (gd, gd_ref)))
    ]
    for copy in stores:
        copy.start()
    for copy in store([pl.multiple_of(k * PAIR, PAIR) for k in range(2)]):
        copy.wait()
    for copy in stores:
        copy.wait()
    finish_gather(gather, pump, False)
    links.finish()


def middle(mine, grads, lanes, low_lanes, wg, wu, wd, collective_id):
    local, units, width = wg.shape
    count = grads.shape[0]
    slots = count // 128 * CAPACITY // 2
    step = 2 * PAIR
    vmem = pl.BlockSpec(memory_space=pltpu.VMEM)
    hbm = pl.BlockSpec(memory_space=pl.ANY)
    return pl.pallas_call(
        middle_body,
        out_shape=[
            jax.ShapeDtypeStruct((count, width), BF16),
            jax.ShapeDtypeStruct((count, width + 128), BF16),
        ]
        + [jax.ShapeDtypeStruct((local, units, width), F32)] * 3,
        in_specs=[hbm, hbm] + [vmem] * 5,
        out_specs=[hbm] * 5,
        scratch_shapes=[
            pltpu.VMEM((count, width + 128), BF16),
            pltpu.VMEM((step, width + 128), BF16),
            pltpu.VMEM((step, width), BF16),
            pltpu.VMEM((step, width + 128), BF16),
            pltpu.VMEM((local, slots, width), BF16),
            pltpu.VMEM((local, slots, width), BF16),
            pltpu.VMEM((local, slots, units), BF16),
            pltpu.VMEM((local, slots, units), BF16),
            pltpu.VMEM((local, slots, units), BF16),
            pltpu.VMEM((local, units, width), F32),
            pltpu.VMEM((local, units, width), F32),
            pltpu.VMEM((local, units, width), F32),
            pltpu.SemaphoreType.DMA((GATHER_COPIES,)),
            pltpu.SemaphoreType.DMA((GATHER_COPIES,)),
            pltpu.SemaphoreType.DMA,
            pltpu.SemaphoreType.DMA((2,)),
            pltpu.SemaphoreType.DMA((4,)),
            pltpu.SemaphoreType.DMA((3,)),
        ],
        compiler_params=pltpu.CompilerParams(
            collective_id=collective_id, has_side_effects=True, vmem_limit_bytes=63 * MIB
        ),
    )(mine, grads, lanes, low_lanes, wg, wu, wd)


def rms_parts(values, gain_vector):
    inverse = lax.rsqrt(jnp.mean(values * values, axis=-1, keepdims=True) + EPSILON)
    return (values * inverse * gain_vector, inverse)


def rms_back(values, inverse, gain_vector, grad_out):
    scaled = grad_out * gain_vector
    inner_mean = jnp.mean(scaled * values, axis=-1, keepdims=True)
    grad_in = inverse * scaled - values * (inverse * inverse * inverse) * inner_mean
    leading = tuple(range(values.ndim - 1))
    grad_gain = jnp.sum(grad_out * values * inverse, axis=leading)
    return (grad_in, grad_gain)


def rotary_tables(positions, head_size):
    half_size = head_size // 2
    frequency = jnp.exp(jnp.arange(half_size, dtype=F32) * (-2.0 * math.log(THETA) / head_size))
    angles = positions[:, None] * frequency[None, :]
    return (jnp.cos(angles)[:, None, :], jnp.sin(angles)[:, None, :])


def matmul(a, b, contract=((1,), (0,))):
    return lax.dot_general(a, b, (contract, ((), ())), preferred_element_type=F32)


def split_high(values):
    high = values.astype(BF16)
    return high, (values - high.astype(F32)).astype(BF16)


def per_device(
    tokens, routes, attention_gain, query_matrix, key_matrix, value_matrix, query_gain, key_gain,
    output_matrix, experts_gain, router_matrix, gate_weight, up_weight, down_weight, cotangent,
):
    tokens, routes, cotangent = tokens[0], routes[0], cotangent[0]
    rows, width = tokens.shape
    expert_count = router_matrix.shape[1]
    local = gate_weight.shape[0]
    head = query_gain.shape[0]
    query_columns, key_columns = query_matrix.shape[1], key_matrix.shape[1]
    heads = query_columns // head
    owners = 32
    shard = width // owners
    length = rows * 8
    scale = head ** (-0.5)
    qkv_columns = query_columns + 2 * key_columns

    packed = jnp.concatenate(
        [
            query_matrix,
            key_matrix,
            value_matrix,
            output_matrix.T,
            router_matrix,
            attention_gain[:, None],
            experts_gain[:, None],
            jnp.zeros((shard, 128 - expert_count - 2), BF16),
        ],
        axis=1,
    )
    expert_ids = jnp.arange(expert_count, dtype=jnp.int32)
    mask = jnp.any(routes[:, :, None] == expert_ids, axis=1)
    sent_mask = jnp.pad(mask.astype(BF16), ((0, 0), (0, 128 - expert_count)))
    positions = lax.axis_index("context") * rows + jnp.arange(rows, dtype=jnp.int32)
    cosine_table, sine_table = rotary_tables(positions.astype(F32), head)
    cosines = jnp.concatenate([cosine_table[:, 0], cosine_table[:, 0]], axis=1)
    sines = jnp.concatenate([-sine_table[:, 0], sine_table[:, 0]], axis=1)
    query_gain_wide, key_gain_wide = query_gain.astype(F32), key_gain.astype(F32)
    weights, all_grads, raw, normed_low, query_flat, both, attended_low, attention_out = front(
        packed,
        jnp.concatenate([cotangent, sent_mask], axis=1),
        tokens,
        cosines,
        sines,
        query_gain_wide[None],
        key_gain_wide[None],
        query_columns,
        0,
    )
    rest = weights[:, qkv_columns + query_columns :]
    router = rest[:, :expert_count]
    first_gain = rest[:, expert_count].astype(F32)
    second_gain = rest[:, expert_count + 1].astype(F32)

    residual = tokens.astype(F32)
    first_inverse = rms_parts(residual, first_gain)[1]
    hidden_state = residual + attention_out.astype(F32)
    routed_tokens, second_inverse = rms_parts(hidden_state, second_gain)
    routed_low = routed_tokens.astype(BF16)
    logits = matmul(routed_low, router)
    chosen = jnp.where(mask, logits, -1e30)
    gate_terms = jnp.where(mask, jnp.exp(chosen - jnp.max(chosen, axis=-1, keepdims=True)), 0.0)
    gates = gate_terms / jnp.sum(gate_terms, axis=-1, keepdims=True)
    gates_high, gates_low = split_high(gates)
    first_expert = (lax.axis_index("dp") * 8 + lax.axis_index("context")) * local
    lane = jnp.arange(128, dtype=jnp.int32)[None, :]
    starts = jnp.arange(2 * local, dtype=jnp.int32)
    wanted = first_expert + starts // 2 + expert_count * (starts % 2)
    lanes = (lane == wanted[:, None]).astype(F32)
    starts = jnp.arange(8, dtype=jnp.int32)
    low_lanes = (lane == jnp.where(starts < local, first_expert + starts, -1)[:, None]).astype(BF16)
    out_terms, back_terms, gate_grad, up_grad, down_grad = middle(
        jnp.concatenate([routed_low, gates_high, gates_low], axis=1), all_grads, lanes, low_lanes,
        gate_weight, up_weight, down_weight, 4,
    )
    back_total = scatter_sum(back_terms, 5)

    grad_out = cotangent.astype(F32)
    shares = back_total[:, width : width + expert_count].astype(F32)
    shares = shares + back_total[:, width + expert_count :].astype(F32)
    grad_logits = (shares - gates * jnp.sum(shares, axis=-1, keepdims=True)).astype(BF16)
    grad_routed = back_total[:, :width].astype(F32) + matmul(grad_logits, router, ((1,), (1,)))
    grad_hidden_norm, second_gain_grad = rms_back(
        hidden_state, second_inverse, second_gain, grad_routed
    )
    grad_hidden = grad_out + grad_hidden_norm
    grad_mixed = grad_hidden.astype(BF16)
    experts_out, grad_qkv, normed_total = back(
        out_terms, weights, grad_mixed, query_flat, both, raw, cosines, sines,
        query_gain_wide[None], key_gain_wide[None], 6,
    )
    output = hidden_state + experts_out.astype(F32)
    grad_normed = normed_total[:, :width].astype(F32)
    head_gains = normed_total[:2, width:].astype(F32)
    grad_tokens_norm, first_gain_grad = rms_back(residual, first_inverse, first_gain, grad_normed)
    tokens_grad = grad_hidden + grad_tokens_norm

    def spread(vector):
        each = vector.shape[0] // owners
        return jnp.pad(vector.reshape(owners, each), ((0, 0), (0, shard - each))).reshape(1, -1)

    few_rows = jnp.concatenate(
        [
            matmul(grad_logits, routed_low, ((0,), (0,))),
            first_gain_grad[None],
            second_gain_grad[None],
            spread(head_gains[0]),
            spread(head_gains[1]),
            jnp.zeros((128 - expert_count - 4, width), F32),
        ],
        axis=0,
    ).astype(BF16)
    terms = weight_terms(normed_low, grad_qkv, grad_mixed, attended_low, few_rows)
    total = plane_scatter(terms, 7)
    after = qkv_columns + query_columns
    few = head // owners
    return (
        output[None],
        tokens_grad[None],
        total[:, after + expert_count],
        total[:, :query_columns],
        total[:, query_columns : query_columns + key_columns],
        total[:, query_columns + key_columns : qkv_columns],
        total[:few, after + expert_count + 2],
        total[:few, after + expert_count + 3],
        total[:, qkv_columns:after].T,
        total[:, after + expert_count + 1],
        total[:, after : after + expert_count],
        gate_grad,
        up_grad,
        down_grad,
    )


def solution(mesh):
    plane_rows = P(PLANE)
    both = P(PLANE, "tensor")
    tokens = P("dp", "context", None)
    expert_rows = P(PLANE, "tensor", None)
    router = P(PLANE, None)
    output_matrix = P("tensor", PLANE)
    return jax.shard_map(
        per_device,
        mesh=mesh,
        in_specs=(
            tokens, tokens, plane_rows, both, both, both, P(), P(), output_matrix, plane_rows,
            router, expert_rows, expert_rows, expert_rows, tokens,
        ),
        out_specs=(
            tokens, tokens, plane_rows, both, both, both, plane_rows, plane_rows, output_matrix,
            plane_rows, router, expert_rows, expert_rows, expert_rows,
        ),
        check_vma=False,
    )
```

```python
import functools
import math

import jax
import jax.numpy as jnp
import numpy as np
from jax import lax
from jax.experimental import pallas as pl
from jax.experimental.pallas import tpu as pltpu
from jax.sharding import PartitionSpec as P

MESH = pl.DeviceIdType.MESH
F32 = jnp.float32
BF16 = jnp.bfloat16
MIB = 1 << 20


def rows_at(ref, start, size):
    return ref.at[pl.ds(start, size)]


class Arrival:
    def __init__(self, links, make):
        self.links, self.make = links, make

    def wait_recv(self):
        self.links.act(lambda: self.make().wait_recv())


class Links:
    def __init__(self, send_sem, recv_sem):
        self.send_sem, self.recv_sem = send_sem, recv_sem
        self.copies = []
        self.planned = None

    def act(self, action):
        if self.planned is None:
            action()
        else:
            self.planned.append(action)

    def plan(self, steps):
        stages, done = [], object()
        while True:
            self.planned = []
            more = next(steps, done)
            stages.append(self.planned)
            if more is done:
                self.planned = None
                return stages

    def send(self, source, target, device, arriving):
        index = len(self.copies)

        def copy(start, end):
            return pltpu.make_async_remote_copy(
                src_ref=start(),
                dst_ref=end(),
                send_sem=self.send_sem.at[index],
                recv_sem=self.recv_sem.at[index],
                device_id=device,
                device_id_type=MESH,
            )

        self.act(lambda: copy(source, target).start())
        self.copies.append(lambda: copy(source, target))
        return Arrival(self, lambda: copy(arriving, arriving))

    def finish(self):
        for copy in self.copies:
            copy().wait_send()


def greet(devices):
    barrier = pltpu.get_barrier_semaphore()
    for device in devices:
        pl.semaphore_signal(barrier, inc=1, device_id=device, device_id_type=MESH)
    pl.semaphore_wait(barrier, len(devices))


def plane_place():
    y = lax.axis_index("dp")
    position = lax.axis_index("context")
    z = position // 2
    core = position - 2 * z
    ys = [lax.rem(y + step, 4) for step in range(4)]
    zs = [lax.rem(z + step, 4) for step in range(4)]
    near = {(a, b): {"dp": ys[a], "context": zs[b] * 2 + core} for a in range(4) for b in range(4)}
    slots = {
        (a, b, other): ys[a] * 8 + zs[b] * 2 + (1 - core if other else core)
        for a in range(4)
        for b in range(4)
        for other in (False, True)
    }

    def device(step):
        return near[step[0] % 4, step[1] % 4]

    def slot(step, other=False):
        return slots[step[0] % 4, step[1] % 4, other]

    sibling = {"context": 2 * z + 1 - core}
    return device, slot, sibling


def along(first, second, order):
    return (first, second) if order == 0 else (second, first)


NEAR = ((1, 0), (-1, 0), (0, 1), (0, -1))


class Gather:
    def __init__(self, links, mine, whole, own_sem):
        self.links, self.mine, self.whole, self.own_sem = links, mine, whole, own_sem
        self.device, self.slot, self.sibling = plane_place()
        self.rows = mine.shape[0]
        self.beside = {}

    def rows_of(self, order, part):
        start, size = order * (self.rows // 2), self.rows // 2
        if part == 2:
            return 0, self.rows
        if part == 1:
            return start + size // 2, size // 2
        if part == 0:
            return start, size // 2
        return start, size

    def region(self, order, place, part, other=False):
        def make():
            start, size = self.rows_of(order, part)
            base = self.slot(along(*place, order), other) * self.rows + start
            return self.whole.at[pl.ds(pl.multiple_of(base, 16), size)]

        return make

    def push(self, order, place, part, axis, sign):
        step = along(sign, 0, order) if axis == 0 else along(0, sign, order)
        source = self.region(order, place, part)
        if place == (0, 0):
            start, size = self.rows_of(order, part)

            def source():
                return self.mine.at[pl.ds(start, size)]

        came = (place[0] - sign, place[1]) if axis == 0 else (place[0], place[1] - sign)
        return self.links.send(
            source,
            self.region(order, place, part),
            self.device(step),
            self.region(order, came, part),
        )

    def share(self, order, place, part=None):
        source = self.region(order, place, part)
        if part == 2:

            def source():
                return self.mine

        self.beside[order, along(*place, order)] = self.links.send(
            source,
            self.region(order, place, part),
            self.sibling,
            self.region(order, place, part, True),
        )

    def own(self):
        return pltpu.make_async_copy(self.mine, self.region(0, (0, 0), 2)(), self.own_sem)

    def wait_beside(self, places=None):
        for key in list(self.beside):
            if places is None or key[1] in places:
                self.beside.pop(key).wait_recv()

    def steps(self):
        got = {}
        self.own().start()
        for order in range(2):
            for sign in (1, -1):
                got[order, sign] = self.push(order, (0, 0), None, 0, sign)
        for order in range(2):
            for sign in (1, -1):
                got[order, 0, sign] = self.push(order, (0, 0), None, 1, sign)
        self.share(0, (0, 0), 2)
        yield
        for order in range(2):
            for sign in (1, -1):
                got[order, sign].wait_recv()
                got[order, "far", sign] = self.push(
                    order, (-sign, 0), 0 if sign == 1 else 1, 0, sign
                )
            for sign in (1, -1):
                for way in (1, -1):
                    got[order, -sign, way] = self.push(order, (-sign, 0), None, 1, way)
                self.share(order, (-sign, 0))

        def near(i):
            for order in range(2):
                for way in (1, -1):
                    got[order, i, way].wait_recv()
                    got[order, i, "far", way] = self.push(
                        order, (i, -way), 0 if way == 1 else 1, 1, way
                    )
                    self.share(order, (i, -way))

        def far(i):
            for order in range(2):
                for way in (1, -1):
                    got[order, i, "far", way].wait_recv()
                self.share(order, (i, 2))

        yield
        near(0)
        yield
        for order in range(2):
            for sign in (1, -1):
                got[order, "far", sign].wait_recv()
            for way in (1, -1):
                got[order, 2, way] = self.push(order, (2, 0), None, 1, way)
            self.share(order, (2, 0))
        yield
        near(1)
        yield
        near(-1)
        yield
        far(0)
        yield
        near(2)
        yield
        far(1)
        yield
        far(-1)
        yield
        far(2)


def finish_gather(gather, steps, own=True):
    for _ in steps:
        pass
    gather.wait_beside()
    if own:
        gather.own().wait()


GATHER_COPIES = 2 * 20 + 1 + 2 * 15


def gather_body(mine, whole, send_sem, recv_sem, own_sem):
    device, slot, sibling = plane_place()
    greet([device(step) for step in NEAR] + [sibling])
    links = Links(send_sem, recv_sem)
    gather = Gather(links, mine, whole, own_sem)
    finish_gather(gather, gather.steps())
    links.finish()


def plane_gather(array, collective_id):
    return pl.pallas_call(
        gather_body,
        out_shape=jax.ShapeDtypeStruct((32 * array.shape[0],) + array.shape[1:], array.dtype),
        in_specs=[pl.BlockSpec(memory_space=pl.ANY)],
        out_specs=pl.BlockSpec(memory_space=pl.ANY),
        scratch_shapes=[
            pltpu.SemaphoreType.DMA((GATHER_COPIES,)),
            pltpu.SemaphoreType.DMA((GATHER_COPIES,)),
            pltpu.SemaphoreType.DMA,
        ],
        compiler_params=pltpu.CompilerParams(
            collective_id=collective_id, has_side_effects=True, vmem_limit_bytes=56 * MIB
        ),
    )(array)


def add_rows(target, sources, offset, size, chunk=16):
    def step(k, carry):
        base = pl.multiple_of(k * chunk, chunk)
        at = pl.ds(offset + base, chunk)
        total = target[at].astype(F32)
        for source, start in sources:
            total = total + source[pl.ds(start + base, chunk)].astype(F32)
        target[at] = total.astype(target.dtype)
        return carry

    lax.fori_loop(0, size // chunk, step, 0)


SLOTS = (
    (2, 2), (1, 2), (2, 1), (-1, 2), (2, -1), (0, 2), (2, 0),
    (1, 1), (1, -1), (-1, 1), (-1, -1), (0, 1), (1, 0), (0, -1), (-1, 0), (0, 0),
)


class Parts:
    def __init__(self, rows, ref, held, own_sem):
        self.rows, self.ref, self.held, self.own_sem = rows, ref, held, own_sem
        self.index = {place: k for k, place in enumerate(SLOTS)}
        self.slot = plane_place()[1]

    def base(self, place):
        return self.index[place] * self.rows

    def slot_rows(self, place, other):
        return rows_at(self.ref, pl.multiple_of(self.slot(place, other) * self.rows, 16), self.rows)

    def make(self, place):
        at = pl.ds(self.base(place), self.rows)
        k = self.index[place]
        return pltpu.make_async_copy(
            self.slot_rows(place, False), self.held.at[at], self.own_sem.at[k]
        )

    def start(self, place):
        self.make(place).start()

    def wait(self, place):
        self.make(place).wait()

    def other(self, place):
        return self.slot_rows(place, True)


def scatter_steps(links, parts, out_ref, near, landed):
    device, slot, sibling = plane_place()
    rows, held, base = parts.rows, parts.held, parts.base
    half, quarter = rows // 2, rows // 4
    shares = {}
    for k, place in enumerate(SLOTS):
        parts.start(place)
        here = functools.partial(rows_at, near, k * rows, rows)
        shares[place] = links.send(functools.partial(parts.other, place), here, sibling, here), k
    merged = set()

    def ready(order, place):
        place = along(*place, order)
        if place not in merged:
            merged.add(place)
            parts.wait(place)
            copy, k = shares[place]
            copy.wait_recv()
            add_rows(held, [(near, k * rows)], base(place), rows)
        return base(place) + order * half

    room = [0]

    def push(start, size, order, axis, sign):
        step = along(sign, 0, order) if axis == 0 else along(0, sign, order)
        at = room[0]
        room[0] += size
        here = functools.partial(rows_at, landed, at, size)
        source = functools.partial(rows_at, held, start, size)
        return links.send(source, here, device(step), here), at

    got = {}

    def reduce_ring(key, order, axis, places, stage):
        opposite, plus, minus, mine = places
        if stage == 0:
            start = ready(order, opposite)
            got[key, 0] = push(start, quarter, order, axis, 1)
            got[key, 1] = push(start + quarter, quarter, order, axis, -1)
        if stage == 1:
            start = ready(order, plus)
            copy, at = got[key, 0]
            copy.wait_recv()
            add_rows(held, [(landed, at)], start, quarter)
            got[key, 2] = push(start, half, order, axis, 1)
            start = ready(order, minus)
            copy, at = got[key, 1]
            copy.wait_recv()
            add_rows(held, [(landed, at)], start + quarter, quarter)
            got[key, 3] = push(start, half, order, axis, -1)
        if stage == 2:
            start = ready(order, mine)
            sources = []
            for k in (2, 3):
                copy, at = got[key, k]
                copy.wait_recv()
                sources.append((landed, at))
            if axis == 1:
                add_rows(held, sources, start, half)
            else:
                for k in range(half // 16):
                    total = held[pl.ds(start + 16 * k, 16)].astype(F32)
                    for source, at in sources:
                        total = total + source[pl.ds(at + 16 * k, 16)].astype(F32)
                    out_ref[pl.ds(order * half + 16 * k, 16)] = total

    def ring(i, order, stage):
        reduce_ring((order, i), order, 1, [(i, j) for j in (2, 1, -1, 0)], stage)

    def last(order, stage):
        reduce_ring((order, "last"), order, 0, [(i, 0) for i in (2, 1, -1, 0)], stage)

    yield
    for i in (2, 1, -1, 0):
        for order in range(2):
            ring(i, order, 0)
    for i in (2, 1, -1, 0):
        yield
        for order in range(2):
            ring(i, order, 1)
    yield
    for order in range(2):
        ring(2, order, 2)
        last(order, 0)
    yield
    for order in range(2):
        ring(1, order, 2)
        ring(-1, order, 2)
        last(order, 1)
    yield
    for order in range(2):
        ring(0, order, 2)
        last(order, 2)


SCATTER_COPIES = 16 + 2 * 20


def scatter_scratch(rows, columns):
    return [
        pltpu.VMEM((16 * rows, columns), BF16),
        pltpu.VMEM((16 * rows, columns), BF16),
        pltpu.VMEM((15 * rows, columns), BF16),
        pltpu.SemaphoreType.DMA((16,)),
    ]


class TensorSum:
    def __init__(self, links, held, landed, out):
        self.links, self.held, self.landed, self.out = links, held, landed, out
        self.x = lax.axis_index("tensor")
        self.quarter = held.shape[0] // 4

    def device(self, step):
        return {"tensor": (self.x + step) % 4}

    def rows(self, step):
        return pl.ds(pl.multiple_of(((self.x + step) % 4) * self.quarter, 16), self.quarter)

    def part(self, ref, step):
        return ref.at[self.rows(step)]

    def send(self):
        self.got = []
        for step in (1, 3, 2):
            here = functools.partial(
                rows_at, self.landed, (step - 1) * self.quarter, self.quarter
            )
            source = functools.partial(self.part, self.held, step)
            self.got.append(self.links.send(source, here, self.device(step), here))

    def add(self, exact):
        for copy in self.got:
            copy.wait_recv()
        mine = self.rows(0)
        total = exact[mine].astype(F32)
        for k in range(3):
            total = total + self.landed[k * self.quarter : (k + 1) * self.quarter].astype(F32)
        self.out[mine] = total.astype(BF16)
        here = functools.partial(self.part, self.out, 0)
        self.got = [
            self.links.send(
                here, here, self.device(step), functools.partial(self.part, self.out, -step)
            )
            for step in (1, 3, 2)
        ]

    def wait(self):
        for copy in self.got:
            copy.wait_recv()


TENSOR_COPIES = 6


def tensor_scratch(rows, columns):
    return [pltpu.VMEM((rows, columns), BF16), pltpu.VMEM((rows * 3 // 4, columns), BF16)]


def greet_all(context):
    device, slot, sibling = plane_place()
    x, position = lax.axis_index("tensor"), lax.axis_index("context")
    others = [{"tensor": (x + step) % 4} for step in range(1, 4)]
    if context:
        others += [device(step) for step in NEAR[:2]]
        others += [{"context": (position + step) % 8} for step in range(1, 8)]
    else:
        others += [device(step) for step in NEAR] + [sibling]
    greet(others)


EPSILON = 1e-06
THETA = 1000000.0
PLANE = ("dp", "context")


def dot(a, b, contract):
    return lax.dot_general(a, b, (contract, ((), ())), preferred_element_type=F32)


PAIR = 256
CAPACITY = 32


def rotate(values, cosines, sines):
    return values * cosines + pltpu.roll(values, values.shape[1] // 2, 1) * sines


def front_body(
    head, qm_ref, km_ref, vm_ref, om_ref, rm_ref, ag_ref, eg_ref, cot_ref, routes_ref, x_ref,
    cos_ref, sin_ref, qg_ref, kg_ref,
    weights_out, cot_out, raw_out, normed_out, query_out, both_out, attended_out, hidden_out,
    sent_out, gates_out, gains_out,
    packed, marked, weights, part, held, landed, mixed, keys, cosines, sines,
    send_sem, recv_sem, own_sem,
):
    rows, width = x_ref.shape
    query_columns = attended_out.shape[1]
    heads = query_columns // head
    experts = rm_ref.shape[1]
    shard = packed.shape[0]
    scale = head ** (-0.5)
    position = lax.axis_index("context")

    def context_device(step):
        return {"context": (position + step) % 8}

    tables = [
        pltpu.make_async_copy(
            ref.at[pl.ds(pl.multiple_of(position * rows, rows), rows)], to, own_sem.at[4 + k]
        )
        for k, (ref, to) in enumerate(((cos_ref, cosines), (sin_ref, sines)))
    ]
    for copy in tables:
        copy.start()
    last = query_columns * 2 + 2 * head
    packed[:, :query_columns] = qm_ref[...]
    packed[:, query_columns : query_columns + head] = km_ref[...]
    packed[:, query_columns + head : query_columns + 2 * head] = vm_ref[...]
    packed[:, query_columns + 2 * head : last] = om_ref[...]
    row = lax.broadcasted_iota(jnp.int32, (shard, shard), 0)
    column = lax.broadcasted_iota(jnp.int32, (shard, shard), 1)
    downs = [
        jnp.sum(jnp.where(row == column, ref[...].astype(F32), 0.0), axis=1, keepdims=True)
        for ref in (ag_ref, eg_ref)
    ]
    few = jnp.where(column == 0, downs[0], jnp.where(column == 1, downs[1], 0.0))
    packed[:, last : last + experts] = rm_ref[...]
    packed[:, last + experts :] = few.astype(BF16)
    lane = lax.broadcasted_iota(jnp.int32, (rows, 128), 1)
    named = lane == routes_ref[:, 0:1]
    for k in range(1, routes_ref.shape[1]):
        named = jnp.logical_or(named, lane == routes_ref[:, k : k + 1])
    mask = jnp.where(named, 1.0, 0.0)
    marked[:, :width] = cot_ref[...]
    marked[:, width:] = mask.astype(BF16)
    greet_all(True)
    links = Links(send_sem, recv_sem)
    weight_gather = Gather(links, packed, weights, own_sem.at[0])
    cot_gather = Gather(links, marked, cot_out, own_sem.at[1])
    first, second = weight_gather.steps(), cot_gather.steps()
    next(first)
    values = x_ref[...].astype(F32)
    inverse = lax.rsqrt(jnp.mean(values * values, axis=-1, keepdims=True) + EPSILON)
    for copy in tables:
        copy.wait()
    for _ in range(3):
        next(first)
    next(second)
    for _ in range(2):
        next(first)
    next(second)
    finish_gather(weight_gather, first)
    store = pltpu.make_async_copy(weights, weights_out, own_sem.at[2])
    store.start()
    take_row = lax.broadcasted_iota(jnp.int32, (8, 128), 0)
    take_lane = lax.broadcasted_iota(jnp.int32, (8, 128), 1)
    take = jnp.where(take_lane == take_row + experts, 1.0, 0.0).astype(BF16)
    gains_out[...] = dot(take, weights[:, last : last + 128], ((1,), (1,)))
    normed_out[...] = (x_ref[...].astype(F32) * inverse * gains_out[0:1]).astype(BF16)

    def turn(values, gain_row):
        inverse = lax.rsqrt(jnp.mean(values * values, axis=-1, keepdims=True) + EPSILON)
        return rotate(values * inverse * gain_row, cosines[...], sines[...])

    normed = normed_out[...]
    raw = dot(normed, weights[:, query_columns : query_columns + 2 * head], ((1,), (0,)))
    raw_out[:, query_columns:] = raw[:, :head]
    keys[:, :head] = turn(raw[:, :head], kg_ref[...].astype(F32)).astype(BF16)
    keys[:, head:] = raw[:, head:].astype(BF16)

    def context_rows(step):
        return both_out.at[pl.ds(pl.multiple_of(((position + step) % 8) * rows, 16), rows)]

    own = pltpu.make_async_copy(keys, context_rows(0), own_sem.at[3])
    own.start()
    got = [
        links.send(
            lambda: keys,
            functools.partial(context_rows, 0),
            context_device(step),
            functools.partial(context_rows, -step),
        )
        for step in range(1, 8)
    ]
    next(second)
    for part_index in range(4):
        columns = slice(part_index * query_columns // 4, (part_index + 1) * query_columns // 4)
        raw_out[:, columns] = dot(normed, weights[:, columns], ((1,), (0,)))
    for h in range(heads):
        columns = slice(h * head, (h + 1) * head)
        query_out[:, columns] = turn(raw_out[:, columns], qg_ref[...].astype(F32)).astype(BF16)
    own.wait()
    for copy in got:
        copy.wait_recv()
    next(second)
    length = 8 * rows
    key_positions = lax.broadcasted_iota(jnp.int32, (rows, length), 1)
    query_positions = lax.broadcasted_iota(jnp.int32, (rows, length), 0) + position * rows
    allowed = key_positions <= query_positions
    for h in range(heads):
        columns = slice(h * head, (h + 1) * head)
        scores = dot(query_out[:, columns], both_out[:, :head], ((1,), (1,))) * scale
        scores = jnp.where(allowed, scores, -1e30)
        terms = jnp.exp(scores - jnp.max(scores, axis=-1, keepdims=True))
        probabilities = (terms * (1.0 / jnp.sum(terms, axis=-1, keepdims=True))).astype(BF16)
        attended_out[:, columns] = dot(probabilities, both_out[:, head:], ((1,), (0,))).astype(BF16)
    next(second)
    matrix = slice(query_columns + 2 * head, last)
    for block in range(4):
        columns = slice(block * width // 4, (block + 1) * width // 4)
        product = dot(attended_out[...], weights[columns, matrix], ((1,), (1,)))
        part[:, columns] = product
        held[:, columns] = product.astype(BF16)
    total = TensorSum(links, held, landed, mixed)
    total.send()
    next(second)
    next(second)
    next(second)
    total.add(part)
    next(second)
    total.wait()
    hidden = x_ref[...].astype(F32) + mixed[...].astype(F32)
    hidden_out[...] = hidden
    inverse = lax.rsqrt(jnp.mean(hidden * hidden, axis=-1, keepdims=True) + EPSILON)
    sent_out[:, :width] = (hidden * inverse * gains_out[1:2]).astype(BF16)
    logits = dot(sent_out[:, :width], weights[:, last : last + 128], ((1,), (0,)))
    chosen = jnp.where(named, logits, -1e30)
    terms = jnp.where(named, jnp.exp(chosen - jnp.max(chosen, axis=-1, keepdims=True)), 0.0)
    gates = terms / jnp.sum(terms, axis=-1, keepdims=True)
    gates_out[...] = gates
    high = gates.astype(BF16).astype(F32)
    sent_out[:, width:] = (high + pltpu.roll(gates - high, 64, 1)).astype(BF16)
    finish_gather(cot_gather, second)
    store.wait()
    links.finish()


def front(matrices, cotangent, routes, tokens, cosines, sines, query_gain, key_gain, collective_id):
    rows, width = tokens.shape
    head = query_gain.shape[1]
    shard, query_columns = matrices[0].shape
    columns = 2 * query_columns + 2 * head + 128
    copies = 2 * GATHER_COPIES + 7 + TENSOR_COPIES
    vmem = pl.BlockSpec(memory_space=pltpu.VMEM)
    hbm = pl.BlockSpec(memory_space=pl.ANY)
    return pl.pallas_call(
        functools.partial(front_body, head),
        out_shape=[
            jax.ShapeDtypeStruct((32 * shard, columns), BF16),
            jax.ShapeDtypeStruct((32 * rows, width + 128), BF16),
            jax.ShapeDtypeStruct((rows, query_columns + head), F32),
            jax.ShapeDtypeStruct((rows, width), BF16),
            jax.ShapeDtypeStruct((rows, query_columns), BF16),
            jax.ShapeDtypeStruct((8 * rows, 2 * head), BF16),
            jax.ShapeDtypeStruct((rows, query_columns), BF16),
            jax.ShapeDtypeStruct((rows, width), F32),
            jax.ShapeDtypeStruct((rows, width + 128), BF16),
            jax.ShapeDtypeStruct((rows, 128), F32),
            jax.ShapeDtypeStruct((8, width), F32),
        ],
        in_specs=[vmem] * 10 + [hbm] * 2 + [vmem] * 2,
        out_specs=[hbm, hbm] + [vmem] * 9,
        scratch_shapes=[
            pltpu.VMEM((shard, columns), BF16),
            pltpu.VMEM((rows, width + 128), BF16),
            pltpu.VMEM((32 * shard, columns), BF16),
            pltpu.VMEM((rows, width), F32),
            pltpu.VMEM((rows, width), BF16),
            pltpu.VMEM((rows * 3 // 4, width), BF16),
            pltpu.VMEM((rows, width), BF16),
            pltpu.VMEM((rows, 2 * head), BF16),
            pltpu.VMEM((rows, head), F32),
            pltpu.VMEM((rows, head), F32),
            pltpu.SemaphoreType.DMA((copies,)),
            pltpu.SemaphoreType.DMA((copies,)),
            pltpu.SemaphoreType.DMA((6,)),
        ],
        compiler_params=pltpu.CompilerParams(
            collective_id=collective_id, has_side_effects=True, vmem_limit_bytes=56 * MIB
        ),
    )(*matrices, cotangent, routes, tokens, cosines, sines, query_gain, key_gain)


def back_body(
    head, part_ref, weights_ref, mixed_ref, query_ref, both_ref, raw_ref, cos_ref, sin_ref, qg_ref, kg_ref,
    out_ref, grad_out, normed_out,
    held, near, landed, own_sem, exact, low, came,
    weights, stacked, grads, chances, slopes, key_terms, key_came, normed, normed_low, normed_came,
    cosines, sines, send_sem, recv_sem, load_sem,
):
    rows, width = mixed_ref.shape
    query_columns = query_ref.shape[1]
    heads = query_columns // head
    scale = head ** (-0.5)
    position = lax.axis_index("context")

    def context_device(step):
        return {"context": (position + step) % 8}

    table_rows = pl.ds(pl.multiple_of(position * rows, rows), rows)
    loads = [
        pltpu.make_async_copy(weights_ref, weights, load_sem.at[0]),
        pltpu.make_async_copy(cos_ref.at[table_rows], cosines, load_sem.at[1]),
        pltpu.make_async_copy(sin_ref.at[table_rows], sines, load_sem.at[2]),
    ]
    for copy in loads:
        copy.start()
    greet_all(True)
    links = Links(send_sem, recv_sem)
    parts = Parts(rows, part_ref, held, own_sem)
    sums = scatter_steps(links, parts, exact, near, landed)
    next(sums, None)
    for copy in loads:
        copy.wait()
    matrix = slice(query_columns + 2 * head, 2 * query_columns + 2 * head)
    attended = dot(mixed_ref[...], weights[:, matrix], ((1,), (0,))).astype(BF16)
    for h in range(heads):
        columns, here = slice(h * head, (h + 1) * head), slice(h * rows, (h + 1) * rows)
        stacked[here] = query_ref[:, columns]
        grads[here] = attended[:, columns]
    next(sums, None)
    length = 8 * rows
    key_positions = lax.broadcasted_iota(jnp.int32, (rows, length), 1)
    query_positions = lax.broadcasted_iota(jnp.int32, (rows, length), 0) + position * rows
    allowed = key_positions <= query_positions
    for h in range(heads):
        here = slice(h * rows, (h + 1) * rows)
        scores = dot(stacked[here], both_ref[:, :head], ((1,), (1,))) * scale
        scores = jnp.where(allowed, scores, -1e30)
        terms = jnp.exp(scores - jnp.max(scores, axis=-1, keepdims=True))
        probabilities = terms * (1.0 / jnp.sum(terms, axis=-1, keepdims=True))
        chances[here] = probabilities.astype(BF16)
        grad = dot(grads[here], both_ref[:, head:], ((1,), (1,)))
        delta = jnp.sum(probabilities * grad, axis=-1, keepdims=True)
        slopes[here] = (scale * probabilities * (grad - delta)).astype(BF16)
    key_terms[:, :head] = dot(slopes[...], stacked[...], ((0,), (0,))).astype(BF16)
    key_terms[:, head:] = dot(chances[...], grads[...], ((0,), (0,))).astype(BF16)
    got = []
    for step in range(1, 8):
        source = functools.partial(
            rows_at, key_terms, pl.multiple_of(((position + step) % 8) * rows, 16), rows
        )
        target = functools.partial(rows_at, key_came, (step - 1) * rows, rows)
        got.append(links.send(source, target, context_device(step), target))
    next(sums, None)

    def turn_back(values, grad, gain_row):
        grad = rotate(grad, cosines[...], -sines[...])
        inverse = lax.rsqrt(jnp.mean(values * values, axis=-1, keepdims=True) + EPSILON)
        scaled = grad * gain_row
        mean = jnp.mean(scaled * values, axis=-1, keepdims=True)
        grad_gain = jnp.sum(grad * values * inverse, axis=0, keepdims=True)
        return inverse * scaled - values * (inverse * inverse * inverse) * mean, grad_gain

    query_gain = jnp.zeros((1, head), F32)
    for h in range(heads):
        columns, here = slice(h * head, (h + 1) * head), slice(h * rows, (h + 1) * rows)
        grad = dot(slopes[here], both_ref[:, :head], ((1,), (0,)))
        grad, gain = turn_back(raw_ref[:, columns], grad, qg_ref[...].astype(F32))
        grad_out[:, columns] = grad.astype(BF16)
        query_gain = query_gain + gain
    for copy in got:
        copy.wait_recv()
    mine = key_terms[pl.ds(pl.multiple_of(position * rows, 16), rows)].astype(F32)
    for k in range(7):
        mine = mine + key_came[k * rows : (k + 1) * rows].astype(F32)
    grad, key_gain = turn_back(raw_ref[:, query_columns:], mine[:, :head], kg_ref[...].astype(F32))
    grad_out[:, query_columns : query_columns + head] = grad.astype(BF16)
    grad_out[:, query_columns + head :] = mine[:, head:].astype(BF16)
    next(sums, None)
    for block in range(4):
        columns = slice(block * width // 4, (block + 1) * width // 4)
        product = dot(grad_out[...], weights[columns, : query_columns + 2 * head], ((1,), (1,)))
        normed[:, columns] = product
        normed_low[:, columns] = product.astype(BF16)
    row = lax.broadcasted_iota(jnp.int32, (rows, head), 0)
    gains = jnp.where(row == 0, query_gain, jnp.where(row == 1, key_gain, 0.0))
    normed[:, width:] = gains
    normed_low[:, width:] = gains.astype(BF16)
    total = TensorSum(links, normed_low, normed_came, normed_out)
    total.send()
    next(sums, None)
    total.add(normed)
    for _ in sums:
        pass
    output = TensorSum(links, low, came, out_ref)
    low[...] = exact[...].astype(BF16)
    output.send()
    total.wait()
    output.add(exact)
    output.wait()
    links.finish()


def back(part, weights, mixed, query_low, both, raw, cosines, sines, query_gain, key_gain, collective_id):
    rows, width = mixed.shape
    head = query_gain.shape[1]
    query_columns = query_low.shape[1]
    stacked = rows * (query_columns // head)
    copies = SCATTER_COPIES + 2 * TENSOR_COPIES + 7
    vmem = pl.BlockSpec(memory_space=pltpu.VMEM)
    hbm = pl.BlockSpec(memory_space=pl.ANY)
    return pl.pallas_call(
        functools.partial(back_body, head),
        out_shape=[
            jax.ShapeDtypeStruct((rows, width), BF16),
            jax.ShapeDtypeStruct((rows, query_columns + 2 * head), BF16),
            jax.ShapeDtypeStruct((rows, width + head), BF16),
        ],
        in_specs=[hbm, hbm] + [vmem] * 4 + [hbm] * 2 + [vmem] * 2,
        out_specs=[vmem] * 3,
        scratch_shapes=scatter_scratch(rows, width)
        + [pltpu.VMEM((rows, width), F32)]
        + tensor_scratch(rows, width)
        + [
            pltpu.VMEM(weights.shape, BF16),
            pltpu.VMEM((stacked, head), BF16),
            pltpu.VMEM((stacked, head), BF16),
            pltpu.VMEM((stacked, 8 * rows), BF16),
            pltpu.VMEM((stacked, 8 * rows), BF16),
            pltpu.VMEM((8 * rows, 2 * head), BF16),
            pltpu.VMEM((7 * rows, 2 * head), BF16),
            pltpu.VMEM((rows, width + head), F32),
        ]
        + tensor_scratch(rows, width + head)
        + [
            pltpu.VMEM((rows, head), F32),
            pltpu.VMEM((rows, head), F32),
            pltpu.SemaphoreType.DMA((copies,)),
            pltpu.SemaphoreType.DMA((copies,)),
            pltpu.SemaphoreType.DMA((3,)),
        ],
        compiler_params=pltpu.CompilerParams(
            collective_id=collective_id, has_side_effects=True, vmem_limit_bytes=60 * MIB
        ),
    )(part, weights, mixed, query_low, both, raw, cosines, sines, query_gain, key_gain)


class Terms:
    def __init__(self, rows, held, work):
        self.rows, self.held, self.work = rows, held, work
        self.index = {place: k for k, place in enumerate(SLOTS)}
        self.core = lax.rem(lax.axis_index("context"), 2)
        self.slot = plane_place()[1]

    def base(self, place):
        return pl.multiple_of((self.index[place] * 2 + self.core) * self.rows, self.rows)

    def other(self, place):
        start = (self.index[place] * 2 + 1 - self.core) * self.rows
        return rows_at(self.held, pl.multiple_of(start, self.rows), self.rows)

    def start(self, place):
        first = pl.multiple_of((self.slot(place) - self.core) * self.rows, 2 * self.rows)
        self.work(pl.ds(first, 2 * self.rows), self.index[place] * 2 * self.rows)

    def wait(self, place):
        pass


def tail_body(
    head, normed_ref, grad_ref, mixed_ref, attended_ref, few_ref, total_ref, hidden_ref, x_ref, gains_ref,
    out, tokens_out, held, near, landed, few, send_sem, recv_sem,
):
    rows, width = x_ref.shape
    shard = out.shape[0]
    greet_all(False)
    links = Links(send_sem, recv_sem)
    values = x_ref[...].astype(F32)
    inverse = lax.rsqrt(jnp.mean(values * values, axis=-1, keepdims=True) + EPSILON)
    grad = total_ref[:, :width].astype(F32)
    scaled = grad * gains_ref[0:1]
    mean = jnp.mean(scaled * values, axis=-1, keepdims=True)
    change = inverse * scaled - values * (inverse * inverse * inverse) * mean
    tokens_out[...] = hidden_ref[...] + change
    gain = jnp.sum(grad * values * inverse, axis=0, keepdims=True)
    entry = lax.broadcasted_iota(jnp.int32, (head, width), 0)
    column = lax.broadcasted_iota(jnp.int32, (head, width), 1)
    each = head * shard // width
    inside = lax.rem(column, shard)
    wanted = jnp.where(inside < each, (column // shard) * each + inside, -1)
    spread = jnp.where(entry == wanted, 1.0, 0.0).astype(BF16)
    heads = dot(total_ref[0:16, width:], spread, ((1,), (0,)))
    at = lax.broadcasted_iota(jnp.int32, (16, width), 0)
    some = few_ref[64:80].astype(F32)
    some = jnp.where(at == 0, gain, some)
    some = jnp.where(at == 2, heads[0:1], jnp.where(at == 3, heads[1:2], some))
    few[...] = few_ref[...]
    few[64:80] = some.astype(BF16)
    first, second = grad_ref.shape[1], attended_ref.shape[1]

    def work(columns, start):
        here = pl.ds(start, 2 * shard)
        held[here, :first] = dot(normed_ref[:, columns].T, grad_ref[...], ((1,), (0,))).astype(BF16)
        held[here, first : first + second] = dot(
            mixed_ref[:, columns].T, attended_ref[...], ((1,), (0,))
        ).astype(BF16)
        held[here, first + second :] = few[:, columns].T

    for _ in scatter_steps(links, Terms(shard, held, work), out, near, landed):
        pass
    links.finish()


def tail(normed, grad, mixed, attended, few, total, hidden, tokens, gains, head, shard, collective_id):
    rows, width = tokens.shape
    columns = grad.shape[1] + attended.shape[1] + few.shape[0]
    vmem = pl.BlockSpec(memory_space=pltpu.VMEM)
    return pl.pallas_call(
        functools.partial(tail_body, head),
        out_shape=[
            jax.ShapeDtypeStruct((shard, columns), F32),
            jax.ShapeDtypeStruct((rows, width), F32),
        ],
        in_specs=[vmem] * 9,
        out_specs=[vmem] * 2,
        scratch_shapes=[
            pltpu.VMEM((32 * shard, columns), BF16),
            pltpu.VMEM((16 * shard, columns), BF16),
            pltpu.VMEM((15 * shard, columns), BF16),
            pltpu.VMEM(few.shape, BF16),
            pltpu.SemaphoreType.DMA((SCATTER_COPIES,)),
            pltpu.SemaphoreType.DMA((SCATTER_COPIES,)),
        ],
        compiler_params=pltpu.CompilerParams(
            collective_id=collective_id, has_side_effects=True, vmem_limit_bytes=56 * MIB
        ),
    )(normed, grad, mixed, attended, few, total, hidden, tokens, gains)


WORK = (
    (0, 0), (1, 0), (-1, 0), (0, 1), (0, -1), (1, 1), (1, -1), (-1, 1),
    (-1, -1), (0, 2), (2, 0), (1, 2), (2, 1), (-1, 2), (2, -1), (2, 2),
)
PUMP = ((2, 0, 1), (0, 0, 1), (1, 0, 1), (0, 1, 0), (1, 0, 1), (1, 0, 0), (1, 0, 0), (0, 0, 0))


def pack_work(axis, which):
    code = 0
    for step in range(len(WORK) // 2):
        code += (WORK[2 * step + which][axis] % 4) * 4**step
    return code


def middle_body(
    mine_ref, grads_ref, lane_ref, low_lane_ref, wg_ref, wu_ref, wd_ref,
    out_ref, back_ref, rows_ref, given_out, inner_out, slope_g_out, slope_u_out,
    whole, fetched, out_held, back_held, rows, given, turned_g, turned_u, raw_grads,
    picks, spots, inner, slope_g, slope_u,
    send_sem, recv_sem, own_sem, load_sem, store_sem, keep_sem,
):
    local, units, width = wg_ref.shape
    per_pair = 2 * CAPACITY
    steps = len(WORK) // 2
    device, slot, sibling = plane_place()
    y = lax.axis_index("dp")
    z = lax.axis_index("context") // 2
    greet([device(step) for step in NEAR] + [sibling])
    links = Links(send_sem, recv_sem)
    gather = Gather(links, mine_ref, whole, own_sem)
    stages = links.plan(gather.steps())
    for action in stages[0]:
        action()

    def pump(at, point):
        begin = 1 + sum(sum(counts) for counts in PUMP[:at]) + sum(PUMP[at][:point])
        for stage in stages[begin : begin + PUMP[at][point]]:
            for action in stage:
                action()

    def fetch(place, buffer):
        return pltpu.make_async_copy(
            grads_ref.at[pl.ds(pl.multiple_of(place * PAIR, PAIR), PAIR)],
            fetched.at[buffer],
            load_sem.at[buffer],
        )

    fetch(0, 0).start()
    row = lax.broadcasted_iota(jnp.int32, (128, 128), 0)
    column = lax.broadcasted_iota(jnp.int32, (128, 128), 1)
    before = jnp.where(column < row, 1.0, 0.0).astype(BF16)
    after = jnp.where(row < column, 1.0, 0.0).astype(BF16)
    slots = lax.broadcasted_iota(jnp.int32, (per_pair, PAIR), 0).astype(F32)
    lane_slots = lax.broadcasted_iota(jnp.int32, (PAIR, per_pair), 1).astype(F32)

    def prepare(place, carry):
        buffer = lax.rem(place, 2)

        @pl.when(place < 15)
        def _():
            fetch(place + 1, 1 - buffer).start()

        fetch(place, buffer).wait()
        marks = fetched[buffer, :, width:]
        named = dot(low_lane_ref[...], marks, ((1,), (1,)))
        across, down = [], []
        for k in range(2):
            tokens = slice(k * 128, (k + 1) * 128)
            across.append(dot(named[:, tokens].astype(BF16), after, ((1,), (0,))) + float(CAPACITY * k))
            down.append(dot(before, marks[tokens], ((1,), (0,))) + float(CAPACITY * k))
        across = jnp.where(named > 0.5, jnp.concatenate(across, axis=1), -1.0)
        down = jnp.where(marks.astype(F32) > 0.5, jnp.concatenate(down, axis=0), -1.0)
        for e in range(local):
            mine = slice(e * per_pair, (e + 1) * per_pair)
            picks[place, mine] = jnp.where(slots == across[e : e + 1], 1.0, 0.0).astype(BF16)
            wanted = jnp.where(lane_ref[2 * e : 2 * e + 1] > 0.5, down, 0.0)
            spot = jnp.sum(wanted, axis=1, keepdims=True)
            spots[place, :, mine] = jnp.where(lane_slots == spot, 1.0, 0.0).astype(BF16)
        taken = dot(picks[place], fetched[buffer, :, :width], ((1,), (0,))).astype(BF16)
        at = pl.ds(pl.multiple_of(place * per_pair, per_pair), per_pair)
        for e in range(local):
            given[e, at] = taken[e * per_pair : (e + 1) * per_pair]
        return carry

    lax.fori_loop(0, 16, prepare, 0)
    keep = pltpu.make_async_copy(given, given_out, keep_sem.at[0])
    keep.start()
    for e in range(local):
        turned_g[e] = wg_ref[e].T
        turned_u[e] = wu_ref[e].T
        raw_grads[e] = dot(given[e], wd_ref[e], ((1,), (1,)))

    def store(places):
        copies = []
        for k, place in enumerate(places):
            here = pl.ds(k * PAIR, PAIR)
            there = pl.ds(pl.multiple_of(place * PAIR, PAIR), PAIR)
            few = pl.ds(pl.multiple_of(place * per_pair, per_pair), per_pair)
            copies += [
                pltpu.make_async_copy(out_held.at[here], out_ref.at[there], store_sem.at[k]),
                pltpu.make_async_copy(back_held.at[here], back_ref.at[there], store_sem.at[2 + k]),
                pltpu.make_async_copy(
                    rows.at[:, pl.ds(k * per_pair, per_pair)], rows_ref.at[:, few], store_sem.at[4 + k]
                ),
            ]
        return copies

    def pump_at(step, point):
        for at in range(steps):
            if PUMP[at][point]:

                @pl.when(step == at)
                def _():
                    pump(at, point)

    def work(step, carry):
        codes = [(carry[0], carry[1]), (carry[2], carry[3])]
        places = [
            lax.rem(y + lax.rem(code[0], 4), 4) * 4 + lax.rem(z + lax.rem(code[1], 4), 4)
            for code in codes
        ]
        pump_at(step, 0)
        for at in range(steps):

            @pl.when(step == at)
            def _():
                gather.wait_beside(WORK[2 * at : 2 * at + 2])
                if at == 0:
                    gather.own().wait()

        @pl.when(step > 0)
        def _():
            for copy in store(places):
                copy.wait()

        weights = [[], []]
        for p, place in enumerate(places):
            here = pl.ds(pl.multiple_of(place * PAIR, PAIR), PAIR)
            pick = picks[place]
            gates = dot(pick, whole[here, width:], ((1,), (0,)))
            taken = dot(pick, whole[here, :width], ((1,), (0,))).astype(BF16)
            for e in range(local):
                mine = slice(e * per_pair, (e + 1) * per_pair)
                lanes = lane_ref[2 * e : 2 * e + 1] + lane_ref[2 * e + 1 : 2 * e + 2]
                weights[e].append(jnp.sum(gates[mine] * lanes, axis=1, keepdims=True))
                rows[e, p * per_pair : (p + 1) * per_pair] = taken[mine]
        pump_at(step, 1)
        sent, returned = [], []
        few = [pl.ds(pl.multiple_of(place * per_pair, per_pair), per_pair) for place in places]
        for e in range(local):
            weight = jnp.concatenate(weights[e], axis=0)
            gate = dot(rows[e], turned_g[e], ((1,), (0,)))
            up = dot(rows[e], turned_u[e], ((1,), (0,)))
            raw = jnp.concatenate([raw_grads[e, at] for at in few], axis=0)
            sigmoid = jax.nn.sigmoid(gate)
            active = gate * sigmoid
            hidden = (active * up * weight).astype(BF16)
            share = jnp.sum(hidden.astype(F32) * raw, axis=1, keepdims=True)
            raw = raw * weight
            grad_gate = (raw * up * sigmoid * (1.0 + gate * (1.0 - sigmoid))).astype(BF16)
            grad_up = (raw * active).astype(BF16)
            for p, at in enumerate(few):
                part = slice(p * per_pair, (p + 1) * per_pair)
                inner[e, at] = hidden[part]
                slope_g[e, at] = grad_gate[part]
                slope_u[e, at] = grad_up[part]
            sent.append(dot(hidden, wd_ref[e], ((1,), (0,))).astype(BF16))
            grad = dot(grad_gate, wg_ref[e], ((1,), (0,)))
            grad = grad + dot(grad_up, wu_ref[e], ((1,), (0,)))
            high = share.astype(BF16).astype(F32)
            lanes = high * lane_ref[2 * e : 2 * e + 1] + (share - high) * lane_ref[2 * e + 1 : 2 * e + 2]
            returned.append((grad.astype(BF16), lanes.astype(BF16)))
        pump_at(step, 2)
        for p, place in enumerate(places):
            tokens = slice(p * PAIR, (p + 1) * PAIR)
            mine = slice(p * per_pair, (p + 1) * per_pair)
            spot = spots[place]
            out_rows = jnp.concatenate([s[mine] for s in sent], axis=0)
            out_held[tokens] = dot(spot, out_rows, ((1,), (0,))).astype(BF16)
            back_rows = jnp.concatenate([r[0][mine] for r in returned], axis=0)
            back_held[tokens, :width] = dot(spot, back_rows, ((1,), (0,))).astype(BF16)
            lane_rows = jnp.concatenate([r[1][mine] for r in returned], axis=0)
            back_held[tokens, width:] = dot(spot, lane_rows, ((1,), (0,))).astype(BF16)
        for copy in store(places):
            copy.start()
        return tuple(part // 4 for code in codes for part in code)

    codes = [pack_work(axis, which) for which in range(2) for axis in range(2)]
    lax.fori_loop(0, steps, work, tuple(codes))
    keeps = [
        pltpu.make_async_copy(inner, inner_out, keep_sem.at[1]),
        pltpu.make_async_copy(slope_g, slope_g_out, keep_sem.at[2]),
        pltpu.make_async_copy(slope_u, slope_u_out, keep_sem.at[3]),
    ]
    for copy in keeps:
        copy.start()
    for copy in store([0, 1]):
        copy.wait()
    for copy in keeps:
        copy.wait()
    keep.wait()
    gather.wait_beside()
    links.finish()


def middle(mine, grads, lanes, low_lanes, wg, wu, wd, collective_id):
    local, units, width = wg.shape
    count = grads.shape[0]
    slots = count // 128 * CAPACITY
    step = 2 * PAIR
    vmem = pl.BlockSpec(memory_space=pltpu.VMEM)
    hbm = pl.BlockSpec(memory_space=pl.ANY)
    return pl.pallas_call(
        middle_body,
        out_shape=[
            jax.ShapeDtypeStruct((count, width), BF16),
            jax.ShapeDtypeStruct((count, width + 128), BF16),
        ]
        + [jax.ShapeDtypeStruct((local, slots, width), BF16)] * 2
        + [jax.ShapeDtypeStruct((local, slots, units), BF16)] * 3,
        in_specs=[hbm, hbm] + [vmem] * 5,
        out_specs=[hbm] * 7,
        scratch_shapes=[
            pltpu.VMEM((count, width + 128), BF16),
            pltpu.VMEM((2, PAIR, width + 128), BF16),
            pltpu.VMEM((step, width), BF16),
            pltpu.VMEM((step, width + 128), BF16),
            pltpu.VMEM((local, 4 * CAPACITY, width), BF16),
            pltpu.VMEM((local, slots, width), BF16),
            pltpu.VMEM((local, width, units), BF16),
            pltpu.VMEM((local, width, units), BF16),
            pltpu.VMEM((local, slots, units), F32),
            pltpu.VMEM((count // PAIR, 4 * CAPACITY, PAIR), BF16),
            pltpu.VMEM((count // PAIR, PAIR, 4 * CAPACITY), BF16),
            pltpu.VMEM((local, slots, units), BF16),
            pltpu.VMEM((local, slots, units), BF16),
            pltpu.VMEM((local, slots, units), BF16),
            pltpu.SemaphoreType.DMA((GATHER_COPIES,)),
            pltpu.SemaphoreType.DMA((GATHER_COPIES,)),
            pltpu.SemaphoreType.DMA,
            pltpu.SemaphoreType.DMA((2,)),
            pltpu.SemaphoreType.DMA((6,)),
            pltpu.SemaphoreType.DMA((4,)),
        ],
        compiler_params=pltpu.CompilerParams(
            collective_id=collective_id, has_side_effects=True, vmem_limit_bytes=63 * MIB
        ),
    )(mine, grads, lanes, low_lanes, wg, wu, wd)


def scatter_sum_body(
    part_ref, rows_ref, given_ref, inner_ref, slope_g_ref, slope_u_ref, weights_ref,
    cot_ref, hidden_ref, sent_ref, gates_ref, gains_ref,
    gg_ref, gu_ref, gd_ref, hidden_out, mixed_out, few_out,
    held, near, landed, own_sem, exact, low, came, out, taken, given, inner, slope_g, slope_u, router,
    send_sem, recv_sem, load_sem,
):
    rows = cot_ref.shape[0]
    local, units, width = gg_ref.shape
    greet_all(False)
    links = Links(send_sem, recv_sem)
    sums = scatter_steps(links, Parts(rows, part_ref, held, own_sem), exact, near, landed)
    next(sums)
    loads = [
        pltpu.make_async_copy(ref, to, load_sem.at[k])
        for k, (ref, to) in enumerate(
            (
                (inner_ref, inner), (given_ref, given), (slope_g_ref, slope_g), (slope_u_ref, slope_u),
                (rows_ref, taken), (weights_ref.at[:, pl.ds(weights_ref.shape[1] - 128, 128)], router),
            )
        )
    ]
    for copy in loads:
        copy.start()
    next(sums)
    for copy in loads:
        copy.wait()
    jobs = [
        (ref, left, right, e)
        for ref, left, right in ((gd_ref, inner, given), (gg_ref, slope_g, taken), (gu_ref, slope_u, taken))
        for e in range(local)
    ]
    for ref, left, right, e in jobs:
        turned = left[e].T
        for block in range(4):
            columns = slice(block * width // 4, (block + 1) * width // 4)
            ref[e, :, columns] = dot(turned, right[e, :, columns], ((1,), (0,))).astype(BF16)
        next(sums, None)
    for _ in sums:
        pass
    total = TensorSum(links, low, came, out)
    low[...] = exact[...].astype(BF16)
    total.send()
    total.add(exact)
    total.wait()
    lane = lax.broadcasted_iota(jnp.int32, (rows, 128), 1)
    shares = out[:, width:].astype(F32)
    shares = jnp.where(lane < 64, shares + pltpu.roll(shares, 64, 1), 0.0)
    shares = shares - gates_ref[...] * jnp.sum(shares, axis=-1, keepdims=True)
    shares = shares.astype(BF16)
    grad = out[:, :width].astype(F32) + dot(shares, router[...], ((1,), (1,)))
    hidden = hidden_ref[...]
    inverse = lax.rsqrt(jnp.mean(hidden * hidden, axis=-1, keepdims=True) + EPSILON)
    scaled = grad * gains_ref[1:2]
    mean = jnp.mean(scaled * hidden, axis=-1, keepdims=True)
    change = inverse * scaled - hidden * (inverse * inverse * inverse) * mean
    result = cot_ref[...].astype(F32) + change
    hidden_out[...] = result
    mixed_out[...] = result.astype(BF16)
    gain = jnp.sum(grad * hidden * inverse, axis=0, keepdims=True)
    few = dot(shares.astype(F32).T.astype(BF16), sent_ref[:, :width], ((1,), (0,)))
    at = lax.broadcasted_iota(jnp.int32, (128, width), 0)
    few_out[...] = jnp.where(at == 65, gain, few).astype(BF16)
    links.finish()


def scatter_sum(
    part, rows_kept, given, inner, slope_g, slope_u, weights, cot, hidden, sent, gates, gains, collective_id
):
    rows, columns = part.shape[0] // 32, part.shape[1]
    local, slots, width = rows_kept.shape
    units = inner.shape[2]
    copies = SCATTER_COPIES + TENSOR_COPIES
    vmem = pl.BlockSpec(memory_space=pltpu.VMEM)
    hbm = pl.BlockSpec(memory_space=pl.ANY)
    return pl.pallas_call(
        scatter_sum_body,
        out_shape=[jax.ShapeDtypeStruct((local, units, width), BF16)] * 3
        + [
            jax.ShapeDtypeStruct((rows, width), F32),
            jax.ShapeDtypeStruct((rows, width), BF16),
            jax.ShapeDtypeStruct((128, width), BF16),
        ],
        in_specs=[hbm] * 7 + [vmem] * 5,
        out_specs=[vmem] * 6,
        scratch_shapes=scatter_scratch(rows, columns)
        + [pltpu.VMEM((rows, columns), F32)]
        + tensor_scratch(rows, columns)
        + [pltpu.VMEM((rows, columns), BF16)]
        + [pltpu.VMEM((local, slots, width), BF16)] * 2
        + [pltpu.VMEM((local, slots, units), BF16)] * 3
        + [pltpu.VMEM((width, 128), BF16)]
        + [
            pltpu.SemaphoreType.DMA((copies,)),
            pltpu.SemaphoreType.DMA((copies,)),
            pltpu.SemaphoreType.DMA((6,)),
        ],
        compiler_params=pltpu.CompilerParams(
            collective_id=collective_id, has_side_effects=True, vmem_limit_bytes=63 * MIB
        ),
    )(part, rows_kept, given, inner, slope_g, slope_u, weights, cot, hidden, sent, gates, gains)


def rotary_tables(length, head_size):
    half_size = head_size // 2
    steps = np.arange(half_size, dtype=np.float32) * np.float32(-2.0 * math.log(THETA) / head_size)
    angles = np.arange(length, dtype=np.float32)[:, None] * np.exp(steps)[None, :]
    cosines, sines = np.cos(angles.astype(np.float64)), np.sin(angles.astype(np.float64))
    cosines = np.concatenate([cosines, cosines], axis=1).astype(np.float32)
    return cosines, np.concatenate([-sines, sines], axis=1).astype(np.float32)


def per_device(
    tokens, routes, attention_gain, query_matrix, key_matrix, value_matrix, query_gain, key_gain,
    output_matrix, experts_gain, router_matrix, gate_weight, up_weight, down_weight, cotangent,
):
    tokens, routes, cotangent = tokens[0], routes[0], cotangent[0]
    rows, width = tokens.shape
    expert_count = router_matrix.shape[1]
    local = gate_weight.shape[0]
    head = query_gain.shape[0]
    query_columns, key_columns = query_matrix.shape[1], key_matrix.shape[1]
    shard = query_matrix.shape[0]
    qkv_columns = query_columns + 2 * key_columns
    cosines, sines = rotary_tables(8 * rows, head)
    matrices = (
        query_matrix, key_matrix, value_matrix, output_matrix.T, router_matrix,
        attention_gain[None], experts_gain[None],
    )
    weights, all_grads, raw, normed_low, query_flat, both, attended_low, hidden, sent, gates, gains = front(
        matrices, cotangent, routes, tokens, cosines, sines, query_gain[None], key_gain[None], 0
    )
    first_expert = (lax.axis_index("dp") * 8 + lax.axis_index("context")) * local
    lane = jnp.arange(128, dtype=jnp.int32)[None, :]
    starts = jnp.arange(2 * local, dtype=jnp.int32)
    wanted = first_expert + starts // 2 + expert_count * (starts % 2)
    lanes = (lane == wanted[:, None]).astype(F32)
    starts = jnp.arange(8, dtype=jnp.int32)
    low_lanes = (lane == jnp.where(starts < local, first_expert + starts, -1)[:, None]).astype(BF16)
    out_terms, back_terms, *kept = middle(
        sent, all_grads, lanes, low_lanes, gate_weight, up_weight, down_weight, 1
    )
    *expert_grads, grad_hidden, grad_mixed, few = scatter_sum(
        back_terms, *kept, weights, cotangent, hidden, sent, gates, gains, 2
    )
    gate_grad, up_grad, down_grad = [grad.astype(F32) for grad in expert_grads]
    experts_out, grad_qkv, normed_total = back(
        out_terms, weights, grad_mixed, query_flat, both, raw, cosines, sines,
        query_gain[None], key_gain[None], 3,
    )
    output = hidden + experts_out.astype(F32)
    total, tokens_grad = tail(
        normed_low, grad_qkv, grad_mixed, attended_low, few, normed_total, grad_hidden, tokens, gains,
        head, shard, 4,
    )
    after = qkv_columns + query_columns
    few_rows = head * shard // width
    return (
        output[None],
        tokens_grad[None],
        total[:, after + expert_count],
        total[:, :query_columns],
        total[:, query_columns : query_columns + key_columns],
        total[:, query_columns + key_columns : qkv_columns],
        total[:few_rows, after + expert_count + 2],
        total[:few_rows, after + expert_count + 3],
        total[:, qkv_columns:after].T,
        total[:, after + expert_count + 1],
        total[:, after : after + expert_count],
        gate_grad,
        up_grad,
        down_grad,
    )


def solution(mesh):
    plane_rows = P(PLANE)
    both = P(PLANE, "tensor")
    tokens = P("dp", "context", None)
    expert_rows = P(PLANE, "tensor", None)
    router = P(PLANE, None)
    output_matrix = P("tensor", PLANE)
    return jax.shard_map(
        per_device,
        mesh=mesh,
        in_specs=(
            tokens, tokens, plane_rows, both, both, both, P(), P(), output_matrix, plane_rows,
            router, expert_rows, expert_rows, expert_rows, tokens,
        ),
        out_specs=(
            tokens, tokens, plane_rows, both, both, both, plane_rows, plane_rows, output_matrix,
            plane_rows, router, expert_rows, expert_rows, expert_rows,
        ),
        check_vma=False,
    )
```

```python
import functools
import math

import jax
import jax.numpy as jnp
import numpy as np
from jax import lax
from jax.experimental import pallas as pl
from jax.experimental.pallas import tpu as pltpu
from jax.sharding import PartitionSpec as P

MESH = pl.DeviceIdType.MESH
F32 = jnp.float32
BF16 = jnp.bfloat16
MIB = 1 << 20


def rows_at(ref, start, size):
    return ref.at[pl.ds(start, size)]


class Arrival:
    def __init__(self, links, make):
        self.links, self.make = links, make

    def wait_recv(self):
        self.links.act(lambda: self.make().wait_recv())


class Links:
    def __init__(self, send_sem, recv_sem):
        self.send_sem, self.recv_sem = send_sem, recv_sem
        self.copies = []
        self.planned = None

    def act(self, action):
        if self.planned is None:
            action()
        else:
            self.planned.append(action)

    def plan(self, steps):
        stages, done = [], object()
        while True:
            self.planned = []
            more = next(steps, done)
            stages.append(self.planned)
            if more is done:
                self.planned = None
                return stages

    def send(self, source, target, device, arriving):
        index = len(self.copies)

        def copy(start, end):
            return pltpu.make_async_remote_copy(
                src_ref=start(),
                dst_ref=end(),
                send_sem=self.send_sem.at[index],
                recv_sem=self.recv_sem.at[index],
                device_id=device,
                device_id_type=MESH,
            )

        self.act(lambda: copy(source, target).start())
        self.copies.append(lambda: copy(source, target))
        return Arrival(self, lambda: copy(arriving, arriving))

    def finish(self):
        for copy in self.copies:
            copy().wait_send()


def greet(devices):
    barrier = pltpu.get_barrier_semaphore()
    for device in devices:
        pl.semaphore_signal(barrier, inc=1, device_id=device, device_id_type=MESH)
    pl.semaphore_wait(barrier, len(devices))


def plane_place():
    y = lax.axis_index("dp")
    position = lax.axis_index("context")
    z = position // 2
    core = position - 2 * z
    ys = [lax.rem(y + step, 4) for step in range(4)]
    zs = [lax.rem(z + step, 4) for step in range(4)]
    near = {(a, b): {"dp": ys[a], "context": zs[b] * 2 + core} for a in range(4) for b in range(4)}
    slots = {
        (a, b, other): ys[a] * 8 + zs[b] * 2 + (1 - core if other else core)
        for a in range(4)
        for b in range(4)
        for other in (False, True)
    }

    def device(step):
        return near[step[0] % 4, step[1] % 4]

    def slot(step, other=False):
        return slots[step[0] % 4, step[1] % 4, other]

    sibling = {"context": 2 * z + 1 - core}
    return device, slot, sibling


def along(first, second, order):
    return (first, second) if order == 0 else (second, first)


NEAR = ((1, 0), (-1, 0), (0, 1), (0, -1))


class Gather:
    def __init__(self, links, mine, whole, own_sem):
        self.links, self.mine, self.whole, self.own_sem = links, mine, whole, own_sem
        self.device, self.slot, self.sibling = plane_place()
        self.rows = mine.shape[0]
        self.beside = {}

    def rows_of(self, order, part):
        start, size = order * (self.rows // 2), self.rows // 2
        if part == 2:
            return 0, self.rows
        if part == 1:
            return start + size // 2, size // 2
        if part == 0:
            return start, size // 2
        return start, size

    def region(self, order, place, part, other=False):
        def make():
            start, size = self.rows_of(order, part)
            base = self.slot(along(*place, order), other) * self.rows + start
            return self.whole.at[pl.ds(pl.multiple_of(base, 16), size)]

        return make

    def push(self, order, place, part, axis, sign):
        step = along(sign, 0, order) if axis == 0 else along(0, sign, order)
        source = self.region(order, place, part)
        if place == (0, 0):
            start, size = self.rows_of(order, part)

            def source():
                return self.mine.at[pl.ds(start, size)]

        came = (place[0] - sign, place[1]) if axis == 0 else (place[0], place[1] - sign)
        return self.links.send(
            source,
            self.region(order, place, part),
            self.device(step),
            self.region(order, came, part),
        )

    def share(self, order, place, part=None):
        source = self.region(order, place, part)
        if part == 2:

            def source():
                return self.mine

        self.beside[order, along(*place, order)] = self.links.send(
            source,
            self.region(order, place, part),
            self.sibling,
            self.region(order, place, part, True),
        )

    def own(self):
        return pltpu.make_async_copy(self.mine, self.region(0, (0, 0), 2)(), self.own_sem)

    def wait_beside(self, places=None):
        for key in list(self.beside):
            if places is None or key[1] in places:
                self.beside.pop(key).wait_recv()

    def steps(self):
        got = {}
        self.own().start()
        for order in range(2):
            for sign in (1, -1):
                got[order, sign] = self.push(order, (0, 0), None, 0, sign)
        for order in range(2):
            for sign in (1, -1):
                got[order, 0, sign] = self.push(order, (0, 0), None, 1, sign)
        self.share(0, (0, 0), 2)
        yield
        for order in range(2):
            for sign in (1, -1):
                got[order, sign].wait_recv()
                got[order, "far", sign] = self.push(
                    order, (-sign, 0), 0 if sign == 1 else 1, 0, sign
                )
            for sign in (1, -1):
                for way in (1, -1):
                    got[order, -sign, way] = self.push(order, (-sign, 0), None, 1, way)
                self.share(order, (-sign, 0))

        def near(i):
            for order in range(2):
                for way in (1, -1):
                    got[order, i, way].wait_recv()
                    got[order, i, "far", way] = self.push(
                        order, (i, -way), 0 if way == 1 else 1, 1, way
                    )
                    self.share(order, (i, -way))

        def far(i):
            for order in range(2):
                for way in (1, -1):
                    got[order, i, "far", way].wait_recv()
                self.share(order, (i, 2))

        yield
        near(0)
        yield
        for order in range(2):
            for sign in (1, -1):
                got[order, "far", sign].wait_recv()
            for way in (1, -1):
                got[order, 2, way] = self.push(order, (2, 0), None, 1, way)
            self.share(order, (2, 0))
        yield
        near(1)
        yield
        near(-1)
        yield
        far(0)
        yield
        near(2)
        yield
        far(1)
        yield
        far(-1)
        yield
        far(2)


def finish_gather(gather, steps, own=True):
    for _ in steps:
        pass
    gather.wait_beside()
    if own:
        gather.own().wait()


GATHER_COPIES = 2 * 20 + 1 + 2 * 15


def gather_body(mine, whole, send_sem, recv_sem, own_sem):
    device, slot, sibling = plane_place()
    greet([device(step) for step in NEAR] + [sibling])
    links = Links(send_sem, recv_sem)
    gather = Gather(links, mine, whole, own_sem)
    finish_gather(gather, gather.steps())
    links.finish()


def plane_gather(array, collective_id):
    return pl.pallas_call(
        gather_body,
        out_shape=jax.ShapeDtypeStruct((32 * array.shape[0],) + array.shape[1:], array.dtype),
        in_specs=[pl.BlockSpec(memory_space=pl.ANY)],
        out_specs=pl.BlockSpec(memory_space=pl.ANY),
        scratch_shapes=[
            pltpu.SemaphoreType.DMA((GATHER_COPIES,)),
            pltpu.SemaphoreType.DMA((GATHER_COPIES,)),
            pltpu.SemaphoreType.DMA,
        ],
        compiler_params=pltpu.CompilerParams(
            collective_id=collective_id, has_side_effects=True, vmem_limit_bytes=56 * MIB
        ),
    )(array)


def add_rows(target, sources, offset, size, chunk=16):
    def step(k, carry):
        base = pl.multiple_of(k * chunk, chunk)
        at = pl.ds(offset + base, chunk)
        total = target[at].astype(F32)
        for source, start in sources:
            total = total + source[pl.ds(start + base, chunk)].astype(F32)
        target[at] = total.astype(target.dtype)
        return carry

    lax.fori_loop(0, size // chunk, step, 0)


SLOTS = (
    (2, 2), (1, 2), (2, 1), (-1, 2), (2, -1), (0, 2), (2, 0),
    (1, 1), (1, -1), (-1, 1), (-1, -1), (0, 1), (1, 0), (0, -1), (-1, 0), (0, 0),
)


class Parts:
    def __init__(self, rows, ref, held, own_sem):
        self.rows, self.ref, self.held, self.own_sem = rows, ref, held, own_sem
        self.index = {place: k for k, place in enumerate(SLOTS)}
        self.slot = plane_place()[1]

    def base(self, place):
        return self.index[place] * self.rows

    def slot_rows(self, place, other):
        return rows_at(self.ref, pl.multiple_of(self.slot(place, other) * self.rows, 16), self.rows)

    def make(self, place):
        at = pl.ds(self.base(place), self.rows)
        k = self.index[place]
        return pltpu.make_async_copy(
            self.slot_rows(place, False), self.held.at[at], self.own_sem.at[k]
        )

    def start(self, place):
        self.make(place).start()

    def wait(self, place):
        self.make(place).wait()

    def other(self, place):
        return self.slot_rows(place, True)


def scatter_steps(links, parts, out_ref, near, landed):
    device, slot, sibling = plane_place()
    rows, held, base = parts.rows, parts.held, parts.base
    half, quarter = rows // 2, rows // 4
    shares = {}
    for k, place in enumerate(SLOTS):
        parts.start(place)
        here = functools.partial(rows_at, near, k * rows, rows)
        shares[place] = links.send(functools.partial(parts.other, place), here, sibling, here), k
    merged = set()

    def ready(order, place):
        place = along(*place, order)
        if place not in merged:
            merged.add(place)
            parts.wait(place)
            copy, k = shares[place]
            copy.wait_recv()
            add_rows(held, [(near, k * rows)], base(place), rows)
        return base(place) + order * half

    room = [0]

    def push(start, size, order, axis, sign):
        step = along(sign, 0, order) if axis == 0 else along(0, sign, order)
        at = room[0]
        room[0] += size
        here = functools.partial(rows_at, landed, at, size)
        source = functools.partial(rows_at, held, start, size)
        return links.send(source, here, device(step), here), at

    got = {}

    def reduce_ring(key, order, axis, places, stage):
        opposite, plus, minus, mine = places
        if stage == 0:
            start = ready(order, opposite)
            got[key, 0] = push(start, quarter, order, axis, 1)
            got[key, 1] = push(start + quarter, quarter, order, axis, -1)
        if stage == 1:
            start = ready(order, plus)
            copy, at = got[key, 0]
            copy.wait_recv()
            add_rows(held, [(landed, at)], start, quarter)
            got[key, 2] = push(start, half, order, axis, 1)
            start = ready(order, minus)
            copy, at = got[key, 1]
            copy.wait_recv()
            add_rows(held, [(landed, at)], start + quarter, quarter)
            got[key, 3] = push(start, half, order, axis, -1)
        if stage == 2:
            start = ready(order, mine)
            sources = []
            for k in (2, 3):
                copy, at = got[key, k]
                copy.wait_recv()
                sources.append((landed, at))
            if axis == 1:
                add_rows(held, sources, start, half)
            else:
                for k in range(half // 16):
                    total = held[pl.ds(start + 16 * k, 16)].astype(F32)
                    for source, at in sources:
                        total = total + source[pl.ds(at + 16 * k, 16)].astype(F32)
                    out_ref[pl.ds(order * half + 16 * k, 16)] = total

    def ring(i, order, stage):
        reduce_ring((order, i), order, 1, [(i, j) for j in (2, 1, -1, 0)], stage)

    def last(order, stage):
        reduce_ring((order, "last"), order, 0, [(i, 0) for i in (2, 1, -1, 0)], stage)

    yield
    for i in (2, 1, -1, 0):
        for order in range(2):
            ring(i, order, 0)
    for i in (2, 1, -1, 0):
        yield
        for order in range(2):
            ring(i, order, 1)
    yield
    for order in range(2):
        ring(2, order, 2)
        last(order, 0)
    yield
    for order in range(2):
        ring(1, order, 2)
        ring(-1, order, 2)
        last(order, 1)
    yield
    for order in range(2):
        ring(0, order, 2)
        last(order, 2)


SCATTER_COPIES = 16 + 2 * 20


def scatter_scratch(rows, columns):
    return [
        pltpu.VMEM((16 * rows, columns), BF16),
        pltpu.VMEM((16 * rows, columns), BF16),
        pltpu.VMEM((15 * rows, columns), BF16),
        pltpu.SemaphoreType.DMA((16,)),
    ]


class TensorSum:
    def __init__(self, links, held, landed, out):
        self.links, self.held, self.landed, self.out = links, held, landed, out
        self.x = lax.axis_index("tensor")
        self.quarter = held.shape[0] // 4

    def device(self, step):
        return {"tensor": (self.x + step) % 4}

    def rows(self, step):
        return pl.ds(pl.multiple_of(((self.x + step) % 4) * self.quarter, 16), self.quarter)

    def part(self, ref, step):
        return ref.at[self.rows(step)]

    def send(self):
        self.got = []
        for step in (1, 3, 2):
            here = functools.partial(
                rows_at, self.landed, (step - 1) * self.quarter, self.quarter
            )
            source = functools.partial(self.part, self.held, step)
            self.got.append(self.links.send(source, here, self.device(step), here))

    def add(self, exact):
        for copy in self.got:
            copy.wait_recv()
        mine = self.rows(0)
        total = exact[mine].astype(F32)
        for k in range(3):
            total = total + self.landed[k * self.quarter : (k + 1) * self.quarter].astype(F32)
        self.out[mine] = total.astype(BF16)
        here = functools.partial(self.part, self.out, 0)
        self.got = [
            self.links.send(
                here, here, self.device(step), functools.partial(self.part, self.out, -step)
            )
            for step in (1, 3, 2)
        ]

    def wait(self):
        for copy in self.got:
            copy.wait_recv()


TENSOR_COPIES = 6


def tensor_scratch(rows, columns):
    return [pltpu.VMEM((rows, columns), BF16), pltpu.VMEM((rows * 3 // 4, columns), BF16)]


def greet_all(context):
    device, slot, sibling = plane_place()
    x, position = lax.axis_index("tensor"), lax.axis_index("context")
    others = [{"tensor": (x + step) % 4} for step in range(1, 4)]
    if context:
        others += [device(step) for step in NEAR[:2]]
        others += [{"context": (position + step) % 8} for step in range(1, 8)]
    else:
        others += [device(step) for step in NEAR] + [sibling]
    greet(others)


EPSILON = 1e-06
THETA = 1000000.0
PLANE = ("dp", "context")


def dot(a, b, contract):
    return lax.dot_general(a, b, (contract, ((), ())), preferred_element_type=F32)


PAIR = 256
CAPACITY = 32


def rotate(values, cosines, sines):
    return values * cosines + pltpu.roll(values, values.shape[1] // 2, 1) * sines


FRONT_PUMP = (0, 0, 1, 1, 1, 1, 1, 1, 2, 2, 0)


def front_body(
    head, qm_ref, km_ref, vm_ref, om_ref, rm_ref, ag_ref, eg_ref, cot_ref, routes_ref, x_ref,
    cos_ref, sin_ref, qg_ref, kg_ref,
    weights_out, cot_out, raw_out, normed_out, query_out, both_out, attended_out, hidden_out,
    sent_out, gates_out, gains_out,
    packed, marked, weights, part, held, landed, mixed, keys, cosines, sines,
    send_sem, recv_sem, own_sem,
):
    rows, width = x_ref.shape
    query_columns = attended_out.shape[1]
    heads = query_columns // head
    experts = rm_ref.shape[1]
    shard = packed.shape[0]
    scale = head ** (-0.5)
    position = lax.axis_index("context")

    def context_device(step):
        return {"context": (position + step) % 8}

    tables = [
        pltpu.make_async_copy(
            ref.at[pl.ds(pl.multiple_of(position * rows, rows), rows)], to, own_sem.at[4 + k]
        )
        for k, (ref, to) in enumerate(((cos_ref, cosines), (sin_ref, sines)))
    ]
    for copy in tables:
        copy.start()
    last = query_columns * 2 + 2 * head
    packed[:, :query_columns] = qm_ref[...]
    packed[:, query_columns : query_columns + head] = km_ref[...]
    packed[:, query_columns + head : query_columns + 2 * head] = vm_ref[...]
    packed[:, query_columns + 2 * head : last] = om_ref[...]
    row = lax.broadcasted_iota(jnp.int32, (shard, shard), 0)
    column = lax.broadcasted_iota(jnp.int32, (shard, shard), 1)
    downs = [
        jnp.sum(jnp.where(row == column, ref[...].astype(F32), 0.0), axis=1, keepdims=True)
        for ref in (ag_ref, eg_ref)
    ]
    few = jnp.where(column == 0, downs[0], jnp.where(column == 1, downs[1], 0.0))
    packed[:, last : last + experts] = rm_ref[...]
    packed[:, last + experts :] = few.astype(BF16)
    lane = lax.broadcasted_iota(jnp.int32, (rows, 128), 1)
    named = lane == routes_ref[:, 0:1]
    for k in range(1, routes_ref.shape[1]):
        named = jnp.logical_or(named, lane == routes_ref[:, k : k + 1])
    mask = jnp.where(named, 1.0, 0.0)
    marked[:, :width] = cot_ref[...]
    marked[:, width:] = mask.astype(BF16)
    greet_all(True)
    links = Links(send_sem, recv_sem)
    weight_gather = Gather(links, packed, weights, own_sem.at[0])
    cot_gather = Gather(links, marked, cot_out, own_sem.at[1])
    first, second = weight_gather.steps(), cot_gather.steps()
    next(first)

    def pump(point):
        for _ in range(FRONT_PUMP[point]):
            next(second, None)

    values = x_ref[...].astype(F32)
    inverse = lax.rsqrt(jnp.mean(values * values, axis=-1, keepdims=True) + EPSILON)
    for copy in tables:
        copy.wait()
    next(first)
    pump(0)
    for _ in range(2):
        next(first)
    pump(1)
    for _ in range(2):
        next(first)
    pump(2)
    finish_gather(weight_gather, first)
    pump(3)
    store = pltpu.make_async_copy(weights, weights_out, own_sem.at[2])
    store.start()
    take_row = lax.broadcasted_iota(jnp.int32, (8, 128), 0)
    take_lane = lax.broadcasted_iota(jnp.int32, (8, 128), 1)
    take = jnp.where(take_lane == take_row + experts, 1.0, 0.0).astype(BF16)
    gains_out[...] = dot(take, weights[:, last : last + 128], ((1,), (1,)))
    normed_out[...] = (x_ref[...].astype(F32) * inverse * gains_out[0:1]).astype(BF16)

    def turn(values, gain_row):
        inverse = lax.rsqrt(jnp.mean(values * values, axis=-1, keepdims=True) + EPSILON)
        return rotate(values * inverse * gain_row, cosines[...], sines[...])

    normed = normed_out[...]
    raw = dot(normed, weights[:, query_columns : query_columns + 2 * head], ((1,), (0,)))
    raw_out[:, query_columns:] = raw[:, :head]
    keys[:, :head] = turn(raw[:, :head], kg_ref[...].astype(F32)).astype(BF16)
    keys[:, head:] = raw[:, head:].astype(BF16)

    def context_rows(step):
        return both_out.at[pl.ds(pl.multiple_of(((position + step) % 8) * rows, 16), rows)]

    own = pltpu.make_async_copy(keys, context_rows(0), own_sem.at[3])
    own.start()
    got = [
        links.send(
            lambda: keys,
            functools.partial(context_rows, 0),
            context_device(step),
            functools.partial(context_rows, -step),
        )
        for step in range(1, 8)
    ]
    pump(4)
    for part_index in range(4):
        columns = slice(part_index * query_columns // 4, (part_index + 1) * query_columns // 4)
        raw_out[:, columns] = dot(normed, weights[:, columns], ((1,), (0,)))
    for h in range(heads):
        columns = slice(h * head, (h + 1) * head)
        query_out[:, columns] = turn(raw_out[:, columns], qg_ref[...].astype(F32)).astype(BF16)
    pump(5)
    own.wait()
    for copy in got:
        copy.wait_recv()
    pump(6)
    length = 8 * rows
    key_positions = lax.broadcasted_iota(jnp.int32, (rows, length), 1)
    query_positions = lax.broadcasted_iota(jnp.int32, (rows, length), 0) + position * rows
    allowed = key_positions <= query_positions
    for h in range(heads):
        columns = slice(h * head, (h + 1) * head)
        scores = dot(query_out[:, columns], both_out[:, :head], ((1,), (1,))) * scale
        scores = jnp.where(allowed, scores, -1e30)
        terms = jnp.exp(scores - jnp.max(scores, axis=-1, keepdims=True))
        probabilities = (terms * (1.0 / jnp.sum(terms, axis=-1, keepdims=True))).astype(BF16)
        attended_out[:, columns] = dot(probabilities, both_out[:, head:], ((1,), (0,))).astype(BF16)
    pump(7)
    matrix = slice(query_columns + 2 * head, last)
    for block in range(4):
        columns = slice(block * width // 4, (block + 1) * width // 4)
        product = dot(attended_out[...], weights[columns, matrix], ((1,), (1,)))
        part[:, columns] = product
        held[:, columns] = product.astype(BF16)
    total = TensorSum(links, held, landed, mixed)
    total.send()
    pump(8)
    total.add(part)
    pump(9)
    total.wait()
    pump(10)
    hidden = x_ref[...].astype(F32) + mixed[...].astype(F32)
    hidden_out[...] = hidden
    inverse = lax.rsqrt(jnp.mean(hidden * hidden, axis=-1, keepdims=True) + EPSILON)
    sent_out[:, :width] = (hidden * inverse * gains_out[1:2]).astype(BF16)
    logits = dot(sent_out[:, :width], weights[:, last : last + 128], ((1,), (0,)))
    chosen = jnp.where(named, logits, -1e30)
    terms = jnp.where(named, jnp.exp(chosen - jnp.max(chosen, axis=-1, keepdims=True)), 0.0)
    gates = terms / jnp.sum(terms, axis=-1, keepdims=True)
    gates_out[...] = gates
    high = gates.astype(BF16).astype(F32)
    sent_out[:, width:] = (high + pltpu.roll(gates - high, 64, 1)).astype(BF16)
    finish_gather(cot_gather, second)
    store.wait()
    links.finish()


def front(matrices, cotangent, routes, tokens, cosines, sines, query_gain, key_gain, collective_id):
    rows, width = tokens.shape
    head = query_gain.shape[1]
    shard, query_columns = matrices[0].shape
    columns = 2 * query_columns + 2 * head + 128
    copies = 2 * GATHER_COPIES + 7 + TENSOR_COPIES
    vmem = pl.BlockSpec(memory_space=pltpu.VMEM)
    hbm = pl.BlockSpec(memory_space=pl.ANY)
    return pl.pallas_call(
        functools.partial(front_body, head),
        out_shape=[
            jax.ShapeDtypeStruct((32 * shard, columns), BF16),
            jax.ShapeDtypeStruct((32 * rows, width + 128), BF16),
            jax.ShapeDtypeStruct((rows, query_columns + head), F32),
            jax.ShapeDtypeStruct((rows, width), BF16),
            jax.ShapeDtypeStruct((rows, query_columns), BF16),
            jax.ShapeDtypeStruct((8 * rows, 2 * head), BF16),
            jax.ShapeDtypeStruct((rows, query_columns), BF16),
            jax.ShapeDtypeStruct((rows, width), F32),
            jax.ShapeDtypeStruct((rows, width + 128), BF16),
            jax.ShapeDtypeStruct((rows, 128), F32),
            jax.ShapeDtypeStruct((8, width), F32),
        ],
        in_specs=[vmem] * 10 + [hbm] * 2 + [vmem] * 2,
        out_specs=[hbm, hbm] + [vmem] * 9,
        scratch_shapes=[
            pltpu.VMEM((shard, columns), BF16),
            pltpu.VMEM((rows, width + 128), BF16),
            pltpu.VMEM((32 * shard, columns), BF16),
            pltpu.VMEM((rows, width), F32),
            pltpu.VMEM((rows, width), BF16),
            pltpu.VMEM((rows * 3 // 4, width), BF16),
            pltpu.VMEM((rows, width), BF16),
            pltpu.VMEM((rows, 2 * head), BF16),
            pltpu.VMEM((rows, head), F32),
            pltpu.VMEM((rows, head), F32),
            pltpu.SemaphoreType.DMA((copies,)),
            pltpu.SemaphoreType.DMA((copies,)),
            pltpu.SemaphoreType.DMA((6,)),
        ],
        compiler_params=pltpu.CompilerParams(
            collective_id=collective_id, has_side_effects=True, vmem_limit_bytes=56 * MIB
        ),
    )(*matrices, cotangent, routes, tokens, cosines, sines, query_gain, key_gain)


def back_body(
    head, part_ref, weights_ref, mixed_ref, query_ref, both_ref, raw_ref, cos_ref, sin_ref, qg_ref, kg_ref,
    out_ref, grad_out, normed_out,
    held, near, landed, own_sem,
    weights, stacked, grads, chances, slopes, key_terms, key_came, normed, normed_low, normed_came,
    cosines, sines, send_sem, recv_sem, load_sem,
):
    rows, width = mixed_ref.shape
    query_columns = query_ref.shape[1]
    heads = query_columns // head
    scale = head ** (-0.5)
    position = lax.axis_index("context")

    def context_device(step):
        return {"context": (position + step) % 8}

    table_rows = pl.ds(pl.multiple_of(position * rows, rows), rows)
    loads = [
        pltpu.make_async_copy(weights_ref, weights, load_sem.at[0]),
        pltpu.make_async_copy(cos_ref.at[table_rows], cosines, load_sem.at[1]),
        pltpu.make_async_copy(sin_ref.at[table_rows], sines, load_sem.at[2]),
    ]
    for copy in loads:
        copy.start()
    greet_all(True)
    links = Links(send_sem, recv_sem)
    parts = Parts(rows, part_ref, held, own_sem)
    sums = scatter_steps(links, parts, out_ref, near, landed)
    next(sums, None)
    for copy in loads:
        copy.wait()
    matrix = slice(query_columns + 2 * head, 2 * query_columns + 2 * head)
    attended = dot(mixed_ref[...], weights[:, matrix], ((1,), (0,))).astype(BF16)
    for h in range(heads):
        columns, here = slice(h * head, (h + 1) * head), slice(h * rows, (h + 1) * rows)
        stacked[here] = query_ref[:, columns]
        grads[here] = attended[:, columns]
    next(sums, None)
    length = 8 * rows
    key_positions = lax.broadcasted_iota(jnp.int32, (rows, length), 1)
    query_positions = lax.broadcasted_iota(jnp.int32, (rows, length), 0) + position * rows
    allowed = key_positions <= query_positions
    for h in range(heads):
        here = slice(h * rows, (h + 1) * rows)
        scores = dot(stacked[here], both_ref[:, :head], ((1,), (1,))) * scale
        scores = jnp.where(allowed, scores, -1e30)
        terms = jnp.exp(scores - jnp.max(scores, axis=-1, keepdims=True))
        probabilities = terms * (1.0 / jnp.sum(terms, axis=-1, keepdims=True))
        chances[here] = probabilities.astype(BF16)
        grad = dot(grads[here], both_ref[:, head:], ((1,), (1,)))
        delta = jnp.sum(probabilities * grad, axis=-1, keepdims=True)
        slopes[here] = (scale * probabilities * (grad - delta)).astype(BF16)
    key_terms[:, :head] = dot(slopes[...], stacked[...], ((0,), (0,))).astype(BF16)
    key_terms[:, head:] = dot(chances[...], grads[...], ((0,), (0,))).astype(BF16)
    got = []
    for step in range(1, 8):
        source = functools.partial(
            rows_at, key_terms, pl.multiple_of(((position + step) % 8) * rows, 16), rows
        )
        target = functools.partial(rows_at, key_came, (step - 1) * rows, rows)
        got.append(links.send(source, target, context_device(step), target))
    next(sums, None)

    def turn_back(values, grad, gain_row):
        grad = rotate(grad, cosines[...], -sines[...])
        inverse = lax.rsqrt(jnp.mean(values * values, axis=-1, keepdims=True) + EPSILON)
        scaled = grad * gain_row
        mean = jnp.mean(scaled * values, axis=-1, keepdims=True)
        grad_gain = jnp.sum(grad * values * inverse, axis=0, keepdims=True)
        return inverse * scaled - values * (inverse * inverse * inverse) * mean, grad_gain

    query_gain = jnp.zeros((1, head), F32)
    for h in range(heads):
        columns, here = slice(h * head, (h + 1) * head), slice(h * rows, (h + 1) * rows)
        grad = dot(slopes[here], both_ref[:, :head], ((1,), (0,)))
        grad, gain = turn_back(raw_ref[:, columns], grad, qg_ref[...].astype(F32))
        grad_out[:, columns] = grad.astype(BF16)
        query_gain = query_gain + gain
    for copy in got:
        copy.wait_recv()
    mine = key_terms[pl.ds(pl.multiple_of(position * rows, 16), rows)].astype(F32)
    for k in range(7):
        mine = mine + key_came[k * rows : (k + 1) * rows].astype(F32)
    grad, key_gain = turn_back(raw_ref[:, query_columns:], mine[:, :head], kg_ref[...].astype(F32))
    grad_out[:, query_columns : query_columns + head] = grad.astype(BF16)
    grad_out[:, query_columns + head :] = mine[:, head:].astype(BF16)
    next(sums, None)
    for block in range(4):
        columns = slice(block * width // 4, (block + 1) * width // 4)
        product = dot(grad_out[...], weights[columns, : query_columns + 2 * head], ((1,), (1,)))
        normed[:, columns] = product
        normed_low[:, columns] = product.astype(BF16)
    row = lax.broadcasted_iota(jnp.int32, (rows, head), 0)
    gains = jnp.where(row == 0, query_gain, jnp.where(row == 1, key_gain, 0.0))
    normed[:, width:] = gains
    normed_low[:, width:] = gains.astype(BF16)
    total = TensorSum(links, normed_low, normed_came, normed_out)
    total.send()
    next(sums, None)
    total.add(normed)
    for _ in sums:
        pass
    total.wait()
    links.finish()


def back(part, weights, mixed, query_low, both, raw, cosines, sines, query_gain, key_gain, collective_id):
    rows, width = mixed.shape
    head = query_gain.shape[1]
    query_columns = query_low.shape[1]
    stacked = rows * (query_columns // head)
    copies = SCATTER_COPIES + TENSOR_COPIES + 7
    vmem = pl.BlockSpec(memory_space=pltpu.VMEM)
    hbm = pl.BlockSpec(memory_space=pl.ANY)
    return pl.pallas_call(
        functools.partial(back_body, head),
        out_shape=[
            jax.ShapeDtypeStruct((rows, width), F32),
            jax.ShapeDtypeStruct((rows, query_columns + 2 * head), BF16),
            jax.ShapeDtypeStruct((rows, width + head), BF16),
        ],
        in_specs=[hbm, hbm] + [vmem] * 4 + [hbm] * 2 + [vmem] * 2,
        out_specs=[vmem] * 3,
        scratch_shapes=scatter_scratch(rows, width)
        + [
            pltpu.VMEM(weights.shape, BF16),
            pltpu.VMEM((stacked, head), BF16),
            pltpu.VMEM((stacked, head), BF16),
            pltpu.VMEM((stacked, 8 * rows), BF16),
            pltpu.VMEM((stacked, 8 * rows), BF16),
            pltpu.VMEM((8 * rows, 2 * head), BF16),
            pltpu.VMEM((7 * rows, 2 * head), BF16),
            pltpu.VMEM((rows, width + head), F32),
        ]
        + tensor_scratch(rows, width + head)
        + [
            pltpu.VMEM((rows, head), F32),
            pltpu.VMEM((rows, head), F32),
            pltpu.SemaphoreType.DMA((copies,)),
            pltpu.SemaphoreType.DMA((copies,)),
            pltpu.SemaphoreType.DMA((3,)),
        ],
        compiler_params=pltpu.CompilerParams(
            collective_id=collective_id, has_side_effects=True, vmem_limit_bytes=60 * MIB
        ),
    )(part, weights, mixed, query_low, both, raw, cosines, sines, query_gain, key_gain)


class Terms:
    def __init__(self, rows, held, work):
        self.rows, self.held, self.work = rows, held, work
        self.index = {place: k for k, place in enumerate(SLOTS)}
        self.core = lax.rem(lax.axis_index("context"), 2)
        self.slot = plane_place()[1]

    def base(self, place):
        return pl.multiple_of((self.index[place] * 2 + self.core) * self.rows, self.rows)

    def other(self, place):
        start = (self.index[place] * 2 + 1 - self.core) * self.rows
        return rows_at(self.held, pl.multiple_of(start, self.rows), self.rows)

    def start(self, place):
        first = pl.multiple_of((self.slot(place) - self.core) * self.rows, 2 * self.rows)
        self.work(pl.ds(first, 2 * self.rows), self.index[place] * 2 * self.rows)

    def wait(self, place):
        pass


def tail_body(
    head, normed_ref, grad_ref, mixed_ref, attended_ref, few_ref, total_ref, hidden_ref, x_ref, gains_ref,
    sum_ref, state_ref,
    out, tokens_out, output, held, near, landed, few, low, came, summed, send_sem, recv_sem,
):
    rows, width = x_ref.shape
    shard = out.shape[0]
    greet_all(False)
    links = Links(send_sem, recv_sem)
    low[...] = sum_ref[...].astype(BF16)
    terms = TensorSum(links, low, came, summed)
    terms.send()
    values = x_ref[...].astype(F32)
    inverse = lax.rsqrt(jnp.mean(values * values, axis=-1, keepdims=True) + EPSILON)
    grad = total_ref[:, :width].astype(F32)
    scaled = grad * gains_ref[0:1]
    mean = jnp.mean(scaled * values, axis=-1, keepdims=True)
    change = inverse * scaled - values * (inverse * inverse * inverse) * mean
    tokens_out[...] = hidden_ref[...] + change
    gain = jnp.sum(grad * values * inverse, axis=0, keepdims=True)
    entry = lax.broadcasted_iota(jnp.int32, (head, width), 0)
    column = lax.broadcasted_iota(jnp.int32, (head, width), 1)
    each = head * shard // width
    inside = lax.rem(column, shard)
    wanted = jnp.where(inside < each, (column // shard) * each + inside, -1)
    spread = jnp.where(entry == wanted, 1.0, 0.0).astype(BF16)
    heads = dot(total_ref[0:16, width:], spread, ((1,), (0,)))
    at = lax.broadcasted_iota(jnp.int32, (16, width), 0)
    some = few_ref[64:80].astype(F32)
    some = jnp.where(at == 0, gain, some)
    some = jnp.where(at == 2, heads[0:1], jnp.where(at == 3, heads[1:2], some))
    few[...] = few_ref[...]
    few[64:80] = some.astype(BF16)
    first, second = grad_ref.shape[1], attended_ref.shape[1]

    def work(columns, start):
        here = pl.ds(start, 2 * shard)
        held[here, :first] = dot(normed_ref[:, columns].T, grad_ref[...], ((1,), (0,))).astype(BF16)
        held[here, first : first + second] = dot(
            mixed_ref[:, columns].T, attended_ref[...], ((1,), (0,))
        ).astype(BF16)
        held[here, first + second :] = few[:, columns].T

    sums = scatter_steps(links, Terms(shard, held, work), out, near, landed)
    next(sums)
    next(sums)
    terms.add(sum_ref)
    for _ in sums:
        pass
    terms.wait()
    output[...] = state_ref[...] + summed[...].astype(F32)
    links.finish()


def tail(
    normed, grad, mixed, attended, few, total, hidden, tokens, gains, sums, state, head, shard, collective_id
):
    rows, width = tokens.shape
    columns = grad.shape[1] + attended.shape[1] + few.shape[0]
    vmem = pl.BlockSpec(memory_space=pltpu.VMEM)
    return pl.pallas_call(
        functools.partial(tail_body, head),
        out_shape=[
            jax.ShapeDtypeStruct((shard, columns), F32),
            jax.ShapeDtypeStruct((rows, width), F32),
            jax.ShapeDtypeStruct((rows, width), F32),
        ],
        in_specs=[vmem] * 11,
        out_specs=[vmem] * 3,
        scratch_shapes=[
            pltpu.VMEM((32 * shard, columns), BF16),
            pltpu.VMEM((16 * shard, columns), BF16),
            pltpu.VMEM((15 * shard, columns), BF16),
            pltpu.VMEM(few.shape, BF16),
        ]
        + tensor_scratch(rows, width)
        + [
            pltpu.VMEM((rows, width), BF16),
            pltpu.SemaphoreType.DMA((SCATTER_COPIES + TENSOR_COPIES,)),
            pltpu.SemaphoreType.DMA((SCATTER_COPIES + TENSOR_COPIES,)),
        ],
        compiler_params=pltpu.CompilerParams(
            collective_id=collective_id, has_side_effects=True, vmem_limit_bytes=56 * MIB
        ),
    )(normed, grad, mixed, attended, few, total, hidden, tokens, gains, sums, state)


def unpack_body(sizes, total_ref, gg_ref, gu_ref, gd_ref, q_ref, k_ref, v_ref, o_ref, r_ref, *rest):
    ag_ref, eg_ref, qg_ref, kg_ref, gg_out, gu_out, gd_out = rest
    gg_out[...] = gg_ref[...].astype(F32)
    gu_out[...] = gu_ref[...].astype(F32)
    gd_out[...] = gd_ref[...].astype(F32)

    @pl.when(pl.program_id(0) == 0)
    def _():
        query, key, experts, few = sizes
        q_ref[...] = total_ref[:, :query]
        k_ref[...] = total_ref[:, query : query + key]
        v_ref[...] = total_ref[:, query + key : query + 2 * key]
        last = 2 * query + 2 * key
        o_ref[...] = total_ref[:, query + 2 * key : last].T
        block = total_ref[:, last : last + 128]
        r_ref[...] = block[:, :experts]
        turned = block.T
        ag_ref[...] = turned[experts : experts + 1].reshape(ag_ref.shape)
        eg_ref[...] = turned[experts + 1 : experts + 2].reshape(eg_ref.shape)
        qg_ref[...] = turned[experts + 2 : experts + 3, :few].reshape(qg_ref.shape)
        kg_ref[...] = turned[experts + 3 : experts + 4, :few].reshape(kg_ref.shape)


def unpack(total, grads, query, key, experts, few):
    shard = total.shape[0]
    local, units, width = grads[0].shape
    steps = 4

    def whole(*shape):
        return pl.BlockSpec(shape, lambda i: (0,) * len(shape))

    part = pl.BlockSpec((local, units, width // steps), lambda i: (0, 0, i))
    shapes = [
        (shard, query), (shard, key), (shard, key), (query, shard), (shard, experts),
        (1, shard), (1, shard), (1, few), (1, few),
    ]
    return pl.pallas_call(
        functools.partial(unpack_body, (query, key, experts, few)),
        grid=(steps,),
        out_shape=[jax.ShapeDtypeStruct(shape, F32) for shape in shapes]
        + [jax.ShapeDtypeStruct(grad.shape, F32) for grad in grads],
        in_specs=[whole(*total.shape)] + [part] * 3,
        out_specs=[whole(*shape) for shape in shapes] + [part] * 3,
        compiler_params=pltpu.CompilerParams(vmem_limit_bytes=32 * MIB),
    )(total, *grads)


WORK = (
    (0, 0), (1, 0), (-1, 0), (0, 1), (0, -1), (1, 1), (1, -1), (-1, 1),
    (-1, -1), (0, 2), (2, 0), (1, 2), (2, 1), (-1, 2), (2, -1), (2, 2),
)
PUMP = ((2, 0, 1), (0, 0, 1), (1, 0, 1), (0, 1, 0), (1, 0, 1), (1, 0, 0), (1, 0, 0), (0, 0, 0))


def pack_work(axis, which):
    code = 0
    for step in range(len(WORK) // 2):
        code += (WORK[2 * step + which][axis] % 4) * 4**step
    return code


def middle_body(
    mine_ref, grads_ref, lane_ref, low_lane_ref, wg_ref, wu_ref, wd_ref,
    out_ref, back_ref, rows_ref, given_out, inner_out, slope_g_out, slope_u_out,
    whole, fetched, out_held, back_held, rows, given, turned_g, turned_u, raw_grads,
    picks, spots, inner, slope_g, slope_u,
    send_sem, recv_sem, own_sem, load_sem, store_sem, keep_sem,
):
    local, units, width = wg_ref.shape
    per_pair = 2 * CAPACITY
    steps = len(WORK) // 2
    device, slot, sibling = plane_place()
    y = lax.axis_index("dp")
    z = lax.axis_index("context") // 2
    greet([device(step) for step in NEAR] + [sibling])
    links = Links(send_sem, recv_sem)
    gather = Gather(links, mine_ref, whole, own_sem)
    stages = links.plan(gather.steps())
    for action in stages[0]:
        action()

    def pump(at, point):
        begin = 1 + sum(sum(counts) for counts in PUMP[:at]) + sum(PUMP[at][:point])
        for stage in stages[begin : begin + PUMP[at][point]]:
            for action in stage:
                action()

    def fetch(place, buffer):
        return pltpu.make_async_copy(
            grads_ref.at[pl.ds(pl.multiple_of(place * PAIR, PAIR), PAIR)],
            fetched.at[buffer],
            load_sem.at[buffer],
        )

    fetch(0, 0).start()
    row = lax.broadcasted_iota(jnp.int32, (128, 128), 0)
    column = lax.broadcasted_iota(jnp.int32, (128, 128), 1)
    before = jnp.where(column < row, 1.0, 0.0).astype(BF16)
    after = jnp.where(row < column, 1.0, 0.0).astype(BF16)
    slots = lax.broadcasted_iota(jnp.int32, (per_pair, PAIR), 0).astype(F32)
    lane_slots = lax.broadcasted_iota(jnp.int32, (PAIR, per_pair), 1).astype(F32)

    def prepare(place, carry):
        buffer = lax.rem(place, 2)

        @pl.when(place < 15)
        def _():
            fetch(place + 1, 1 - buffer).start()

        fetch(place, buffer).wait()
        marks = fetched[buffer, :, width:]
        named = dot(low_lane_ref[...], marks, ((1,), (1,)))
        across, down = [], []
        for k in range(2):
            tokens = slice(k * 128, (k + 1) * 128)
            across.append(dot(named[:, tokens].astype(BF16), after, ((1,), (0,))) + float(CAPACITY * k))
            down.append(dot(before, marks[tokens], ((1,), (0,))) + float(CAPACITY * k))
        across = jnp.where(named > 0.5, jnp.concatenate(across, axis=1), -1.0)
        down = jnp.where(marks.astype(F32) > 0.5, jnp.concatenate(down, axis=0), -1.0)
        for e in range(local):
            mine = slice(e * per_pair, (e + 1) * per_pair)
            picks[place, mine] = jnp.where(slots == across[e : e + 1], 1.0, 0.0).astype(BF16)
            wanted = jnp.where(lane_ref[2 * e : 2 * e + 1] > 0.5, down, 0.0)
            spot = jnp.sum(wanted, axis=1, keepdims=True)
            spots[place, :, mine] = jnp.where(lane_slots == spot, 1.0, 0.0).astype(BF16)
        taken = dot(picks[place], fetched[buffer, :, :width], ((1,), (0,))).astype(BF16)
        at = pl.ds(pl.multiple_of(place * per_pair, per_pair), per_pair)
        for e in range(local):
            given[e, at] = taken[e * per_pair : (e + 1) * per_pair]
        return carry

    lax.fori_loop(0, 16, prepare, 0)
    keep = pltpu.make_async_copy(given, given_out, keep_sem.at[0])
    keep.start()
    for e in range(local):
        turned_g[e] = wg_ref[e].T
        turned_u[e] = wu_ref[e].T
        raw_grads[e] = dot(given[e], wd_ref[e], ((1,), (1,)))

    def store(places, which):
        copies = []
        for k, place in enumerate(places):
            here = pl.ds(k * PAIR, PAIR)
            there = pl.ds(pl.multiple_of(place * PAIR, PAIR), PAIR)
            few = pl.ds(pl.multiple_of(place * per_pair, per_pair), per_pair)
            if which == 0:
                copies += [
                    pltpu.make_async_copy(
                        rows.at[:, pl.ds(k * per_pair, per_pair)],
                        rows_ref.at[:, few],
                        store_sem.at[4 + k],
                    ),
                ]
            else:
                copies += [
                    pltpu.make_async_copy(out_held.at[here], out_ref.at[there], store_sem.at[k]),
                    pltpu.make_async_copy(back_held.at[here], back_ref.at[there], store_sem.at[2 + k]),
                ]
        return copies

    def pump_at(step, point):
        for at in range(steps):
            if PUMP[at][point]:

                @pl.when(step == at)
                def _():
                    pump(at, point)

    def work(step, carry):
        codes = [(carry[0], carry[1]), (carry[2], carry[3])]
        places = [
            lax.rem(y + lax.rem(code[0], 4), 4) * 4 + lax.rem(z + lax.rem(code[1], 4), 4)
            for code in codes
        ]
        pump_at(step, 0)
        for at in range(steps):

            @pl.when(step == at)
            def _():
                gather.wait_beside(WORK[2 * at : 2 * at + 2])
                if at == 0:
                    gather.own().wait()

        @pl.when(step > 0)
        def _():
            for copy in store(places, 0):
                copy.wait()

        weights = [[], []]
        for p, place in enumerate(places):
            here = pl.ds(pl.multiple_of(place * PAIR, PAIR), PAIR)
            pick = picks[place]
            gates = dot(pick, whole[here, width:], ((1,), (0,)))
            taken = dot(pick, whole[here, :width], ((1,), (0,))).astype(BF16)
            for e in range(local):
                mine = slice(e * per_pair, (e + 1) * per_pair)
                lanes = lane_ref[2 * e : 2 * e + 1] + lane_ref[2 * e + 1 : 2 * e + 2]
                weights[e].append(jnp.sum(gates[mine] * lanes, axis=1, keepdims=True))
                rows[e, p * per_pair : (p + 1) * per_pair] = taken[mine]
        for copy in store(places, 0):
            copy.start()
        pump_at(step, 1)
        sent, returned = [], []
        few = [pl.ds(pl.multiple_of(place * per_pair, per_pair), per_pair) for place in places]
        for e in range(local):
            weight = jnp.concatenate(weights[e], axis=0)
            gate = dot(rows[e], turned_g[e], ((1,), (0,)))
            up = dot(rows[e], turned_u[e], ((1,), (0,)))
            raw = jnp.concatenate([raw_grads[e, at] for at in few], axis=0)
            sigmoid = jax.nn.sigmoid(gate)
            active = gate * sigmoid
            hidden = (active * up * weight).astype(BF16)
            share = jnp.sum(hidden.astype(F32) * raw, axis=1, keepdims=True)
            raw = raw * weight
            grad_gate = (raw * up * sigmoid * (1.0 + gate * (1.0 - sigmoid))).astype(BF16)
            grad_up = (raw * active).astype(BF16)
            for p, at in enumerate(few):
                part = slice(p * per_pair, (p + 1) * per_pair)
                inner[e, at] = hidden[part]
                slope_g[e, at] = grad_gate[part]
                slope_u[e, at] = grad_up[part]
            sent.append(dot(hidden, wd_ref[e], ((1,), (0,))).astype(BF16))
            grad = dot(grad_gate, wg_ref[e], ((1,), (0,)))
            grad = grad + dot(grad_up, wu_ref[e], ((1,), (0,)))
            high = share.astype(BF16).astype(F32)
            lanes = high * lane_ref[2 * e : 2 * e + 1] + (share - high) * lane_ref[2 * e + 1 : 2 * e + 2]
            returned.append((grad.astype(BF16), lanes.astype(BF16)))
        pump_at(step, 2)

        @pl.when(step > 0)
        def _():
            for copy in store(places, 1):
                copy.wait()

        for p, place in enumerate(places):
            tokens = slice(p * PAIR, (p + 1) * PAIR)
            mine = slice(p * per_pair, (p + 1) * per_pair)
            spot = spots[place]
            out_rows = jnp.concatenate([s[mine] for s in sent], axis=0)
            out_held[tokens] = dot(spot, out_rows, ((1,), (0,))).astype(BF16)
            back_rows = jnp.concatenate([r[0][mine] for r in returned], axis=0)
            back_held[tokens, :width] = dot(spot, back_rows, ((1,), (0,))).astype(BF16)
            lane_rows = jnp.concatenate([r[1][mine] for r in returned], axis=0)
            back_held[tokens, width:] = dot(spot, lane_rows, ((1,), (0,))).astype(BF16)
        for copy in store(places, 1):
            copy.start()
        return tuple(part // 4 for code in codes for part in code)

    codes = [pack_work(axis, which) for which in range(2) for axis in range(2)]
    lax.fori_loop(0, steps, work, tuple(codes))
    keeps = [
        pltpu.make_async_copy(inner, inner_out, keep_sem.at[1]),
        pltpu.make_async_copy(slope_g, slope_g_out, keep_sem.at[2]),
        pltpu.make_async_copy(slope_u, slope_u_out, keep_sem.at[3]),
    ]
    for copy in keeps:
        copy.start()
    for copy in store([0, 1], 0) + store([0, 1], 1):
        copy.wait()
    for copy in keeps:
        copy.wait()
    keep.wait()
    gather.wait_beside()
    links.finish()


def middle(mine, grads, lanes, low_lanes, wg, wu, wd, collective_id):
    local, units, width = wg.shape
    count = grads.shape[0]
    slots = count // 128 * CAPACITY
    step = 2 * PAIR
    vmem = pl.BlockSpec(memory_space=pltpu.VMEM)
    hbm = pl.BlockSpec(memory_space=pl.ANY)
    return pl.pallas_call(
        middle_body,
        out_shape=[
            jax.ShapeDtypeStruct((count, width), BF16),
            jax.ShapeDtypeStruct((count, width + 128), BF16),
        ]
        + [jax.ShapeDtypeStruct((local, slots, width), BF16)] * 2
        + [jax.ShapeDtypeStruct((local, slots, units), BF16)] * 3,
        in_specs=[hbm, hbm] + [vmem] * 5,
        out_specs=[hbm] * 7,
        scratch_shapes=[
            pltpu.VMEM((count, width + 128), BF16),
            pltpu.VMEM((2, PAIR, width + 128), BF16),
            pltpu.VMEM((step, width), BF16),
            pltpu.VMEM((step, width + 128), BF16),
            pltpu.VMEM((local, 4 * CAPACITY, width), BF16),
            pltpu.VMEM((local, slots, width), BF16),
            pltpu.VMEM((local, width, units), BF16),
            pltpu.VMEM((local, width, units), BF16),
            pltpu.VMEM((local, slots, units), F32),
            pltpu.VMEM((count // PAIR, 4 * CAPACITY, PAIR), BF16),
            pltpu.VMEM((count // PAIR, PAIR, 4 * CAPACITY), BF16),
            pltpu.VMEM((local, slots, units), BF16),
            pltpu.VMEM((local, slots, units), BF16),
            pltpu.VMEM((local, slots, units), BF16),
            pltpu.SemaphoreType.DMA((GATHER_COPIES,)),
            pltpu.SemaphoreType.DMA((GATHER_COPIES,)),
            pltpu.SemaphoreType.DMA,
            pltpu.SemaphoreType.DMA((2,)),
            pltpu.SemaphoreType.DMA((6,)),
            pltpu.SemaphoreType.DMA((4,)),
        ],
        compiler_params=pltpu.CompilerParams(
            collective_id=collective_id, has_side_effects=True, vmem_limit_bytes=63 * MIB
        ),
    )(mine, grads, lanes, low_lanes, wg, wu, wd)


def scatter_sum_body(
    part_ref, rows_ref, given_ref, inner_ref, slope_g_ref, slope_u_ref, weights_ref,
    cot_ref, hidden_ref, sent_ref, gates_ref, gains_ref,
    gg_ref, gu_ref, gd_ref, hidden_out, mixed_out, few_out,
    held, near, landed, own_sem, exact, low, came, out, taken, given, inner, slope_g, slope_u, router,
    send_sem, recv_sem, load_sem,
):
    rows = cot_ref.shape[0]
    local, units, width = gg_ref.shape
    greet_all(False)
    links = Links(send_sem, recv_sem)
    sums = scatter_steps(links, Parts(rows, part_ref, held, own_sem), exact, near, landed)
    next(sums)
    loads = [
        pltpu.make_async_copy(ref, to, load_sem.at[k])
        for k, (ref, to) in enumerate(
            (
                (inner_ref, inner), (given_ref, given), (slope_g_ref, slope_g), (slope_u_ref, slope_u),
                (rows_ref, taken), (weights_ref.at[:, pl.ds(weights_ref.shape[1] - 128, 128)], router),
            )
        )
    ]
    for copy in loads:
        copy.start()
    next(sums)
    for copy in loads:
        copy.wait()
    jobs = [
        (ref, left, right, e)
        for ref, left, right in ((gd_ref, inner, given), (gg_ref, slope_g, taken), (gu_ref, slope_u, taken))
        for e in range(local)
    ]
    for ref, left, right, e in jobs:
        turned = left[e].T
        for block in range(4):
            columns = slice(block * width // 4, (block + 1) * width // 4)
            ref[e, :, columns] = dot(turned, right[e, :, columns], ((1,), (0,))).astype(BF16)
        next(sums, None)
    for _ in sums:
        pass
    total = TensorSum(links, low, came, out)
    low[...] = exact[...].astype(BF16)
    total.send()
    total.add(exact)
    total.wait()
    lane = lax.broadcasted_iota(jnp.int32, (rows, 128), 1)
    shares = out[:, width:].astype(F32)
    shares = jnp.where(lane < 64, shares + pltpu.roll(shares, 64, 1), 0.0)
    shares = shares - gates_ref[...] * jnp.sum(shares, axis=-1, keepdims=True)
    shares = shares.astype(BF16)
    grad = out[:, :width].astype(F32) + dot(shares, router[...], ((1,), (1,)))
    hidden = hidden_ref[...]
    inverse = lax.rsqrt(jnp.mean(hidden * hidden, axis=-1, keepdims=True) + EPSILON)
    scaled = grad * gains_ref[1:2]
    mean = jnp.mean(scaled * hidden, axis=-1, keepdims=True)
    change = inverse * scaled - hidden * (inverse * inverse * inverse) * mean
    result = cot_ref[...].astype(F32) + change
    hidden_out[...] = result
    mixed_out[...] = result.astype(BF16)
    gain = jnp.sum(grad * hidden * inverse, axis=0, keepdims=True)
    few = dot(shares.astype(F32).T.astype(BF16), sent_ref[:, :width], ((1,), (0,)))
    at = lax.broadcasted_iota(jnp.int32, (128, width), 0)
    few_out[...] = jnp.where(at == 65, gain, few).astype(BF16)
    links.finish()


def scatter_sum(
    part, rows_kept, given, inner, slope_g, slope_u, weights, cot, hidden, sent, gates, gains, collective_id
):
    rows, columns = part.shape[0] // 32, part.shape[1]
    local, slots, width = rows_kept.shape
    units = inner.shape[2]
    copies = SCATTER_COPIES + TENSOR_COPIES
    vmem = pl.BlockSpec(memory_space=pltpu.VMEM)
    hbm = pl.BlockSpec(memory_space=pl.ANY)
    return pl.pallas_call(
        scatter_sum_body,
        out_shape=[jax.ShapeDtypeStruct((local, units, width), BF16)] * 3
        + [
            jax.ShapeDtypeStruct((rows, width), F32),
            jax.ShapeDtypeStruct((rows, width), BF16),
            jax.ShapeDtypeStruct((128, width), BF16),
        ],
        in_specs=[hbm] * 7 + [vmem] * 5,
        out_specs=[vmem] * 6,
        scratch_shapes=scatter_scratch(rows, columns)
        + [pltpu.VMEM((rows, columns), F32)]
        + tensor_scratch(rows, columns)
        + [pltpu.VMEM((rows, columns), BF16)]
        + [pltpu.VMEM((local, slots, width), BF16)] * 2
        + [pltpu.VMEM((local, slots, units), BF16)] * 3
        + [pltpu.VMEM((width, 128), BF16)]
        + [
            pltpu.SemaphoreType.DMA((copies,)),
            pltpu.SemaphoreType.DMA((copies,)),
            pltpu.SemaphoreType.DMA((6,)),
        ],
        compiler_params=pltpu.CompilerParams(
            collective_id=collective_id, has_side_effects=True, vmem_limit_bytes=63 * MIB
        ),
    )(part, rows_kept, given, inner, slope_g, slope_u, weights, cot, hidden, sent, gates, gains)


def rotary_tables(length, head_size):
    half_size = head_size // 2
    steps = np.arange(half_size, dtype=np.float32) * np.float32(-2.0 * math.log(THETA) / head_size)
    angles = np.arange(length, dtype=np.float32)[:, None] * np.exp(steps)[None, :]
    cosines, sines = np.cos(angles.astype(np.float64)), np.sin(angles.astype(np.float64))
    cosines = np.concatenate([cosines, cosines], axis=1).astype(np.float32)
    return cosines, np.concatenate([-sines, sines], axis=1).astype(np.float32)


def per_device(
    tokens, routes, attention_gain, query_matrix, key_matrix, value_matrix, query_gain, key_gain,
    output_matrix, experts_gain, router_matrix, gate_weight, up_weight, down_weight, cotangent,
):
    tokens, routes, cotangent = tokens[0], routes[0], cotangent[0]
    rows, width = tokens.shape
    expert_count = router_matrix.shape[1]
    local = gate_weight.shape[0]
    head = query_gain.shape[0]
    query_columns, key_columns = query_matrix.shape[1], key_matrix.shape[1]
    shard = query_matrix.shape[0]
    cosines, sines = rotary_tables(8 * rows, head)
    matrices = (
        query_matrix, key_matrix, value_matrix, output_matrix.T, router_matrix,
        attention_gain[None], experts_gain[None],
    )
    weights, all_grads, raw, normed_low, query_flat, both, attended_low, hidden, sent, gates, gains = front(
        matrices, cotangent, routes, tokens, cosines, sines, query_gain[None], key_gain[None], 0
    )
    first_expert = (lax.axis_index("dp") * 8 + lax.axis_index("context")) * local
    lane = jnp.arange(128, dtype=jnp.int32)[None, :]
    starts = jnp.arange(2 * local, dtype=jnp.int32)
    wanted = first_expert + starts // 2 + expert_count * (starts % 2)
    lanes = (lane == wanted[:, None]).astype(F32)
    starts = jnp.arange(8, dtype=jnp.int32)
    low_lanes = (lane == jnp.where(starts < local, first_expert + starts, -1)[:, None]).astype(BF16)
    out_terms, back_terms, *kept = middle(
        sent, all_grads, lanes, low_lanes, gate_weight, up_weight, down_weight, 1
    )
    *expert_grads, grad_hidden, grad_mixed, few = scatter_sum(
        back_terms, *kept, weights, cotangent, hidden, sent, gates, gains, 2
    )
    out_sum, grad_qkv, normed_total = back(
        out_terms, weights, grad_mixed, query_flat, both, raw, cosines, sines,
        query_gain[None], key_gain[None], 3,
    )
    total, tokens_grad, output = tail(
        normed_low, grad_qkv, grad_mixed, attended_low, few, normed_total, grad_hidden, tokens, gains,
        out_sum, hidden, head, shard, 4,
    )
    (
        query_grad, key_grad, value_grad, output_grad, router_grad, first_gain, second_gain,
        query_gain_grad, key_gain_grad, gate_grad, up_grad, down_grad,
    ) = unpack(total, expert_grads, query_columns, key_columns, expert_count, head * shard // width)
    return (
        output[None],
        tokens_grad[None],
        first_gain[0],
        query_grad,
        key_grad,
        value_grad,
        query_gain_grad[0],
        key_gain_grad[0],
        output_grad,
        second_gain[0],
        router_grad,
        gate_grad,
        up_grad,
        down_grad,
    )


def solution(mesh):
    plane_rows = P(PLANE)
    both = P(PLANE, "tensor")
    tokens = P("dp", "context", None)
    expert_rows = P(PLANE, "tensor", None)
    router = P(PLANE, None)
    output_matrix = P("tensor", PLANE)
    return jax.shard_map(
        per_device,
        mesh=mesh,
        in_specs=(
            tokens, tokens, plane_rows, both, both, both, P(), P(), output_matrix, plane_rows,
            router, expert_rows, expert_rows, expert_rows, tokens,
        ),
        out_specs=(
            tokens, tokens, plane_rows, both, both, both, plane_rows, plane_rows, output_matrix,
            plane_rows, router, expert_rows, expert_rows, expert_rows,
        ),
        check_vma=False,
    )
```

```python
import functools
import math

import jax
import jax.numpy as jnp
import numpy as np
from jax import lax
from jax.experimental import pallas as pl
from jax.experimental.pallas import tpu as pltpu
from jax.sharding import PartitionSpec as P

MESH = pl.DeviceIdType.MESH
F32 = jnp.float32
BF16 = jnp.bfloat16
MIB = 1 << 20


def rows_at(ref, start, size):
    return ref.at[pl.ds(start, size)]


class Arrival:
    def __init__(self, links, make):
        self.links, self.make = links, make

    def wait_recv(self):
        self.links.act(lambda: self.make().wait_recv())


class Links:
    def __init__(self, send_sem, recv_sem):
        self.send_sem, self.recv_sem = send_sem, recv_sem
        self.copies = []
        self.planned = None

    def act(self, action):
        if self.planned is None:
            action()
        else:
            self.planned.append(action)

    def plan(self, steps):
        stages, done = [], object()
        while True:
            self.planned = []
            more = next(steps, done)
            stages.append(self.planned)
            if more is done:
                self.planned = None
                return stages

    def send(self, source, target, device, arriving):
        index = len(self.copies)

        def copy(start, end):
            return pltpu.make_async_remote_copy(
                src_ref=start(),
                dst_ref=end(),
                send_sem=self.send_sem.at[index],
                recv_sem=self.recv_sem.at[index],
                device_id=device,
                device_id_type=MESH,
            )

        self.act(lambda: copy(source, target).start())
        self.copies.append(lambda: copy(source, target))
        return Arrival(self, lambda: copy(arriving, arriving))

    def finish(self):
        for copy in self.copies:
            copy().wait_send()


def greet(devices):
    barrier = pltpu.get_barrier_semaphore()
    for device in devices:
        pl.semaphore_signal(barrier, inc=1, device_id=device, device_id_type=MESH)
    pl.semaphore_wait(barrier, len(devices))


def plane_place():
    y = lax.axis_index("dp")
    position = lax.axis_index("context")
    z = position // 2
    core = position - 2 * z
    ys = [lax.rem(y + step, 4) for step in range(4)]
    zs = [lax.rem(z + step, 4) for step in range(4)]
    near = {(a, b): {"dp": ys[a], "context": zs[b] * 2 + core} for a in range(4) for b in range(4)}
    slots = {
        (a, b, other): ys[a] * 8 + zs[b] * 2 + (1 - core if other else core)
        for a in range(4)
        for b in range(4)
        for other in (False, True)
    }

    def device(step):
        return near[step[0] % 4, step[1] % 4]

    def slot(step, other=False):
        return slots[step[0] % 4, step[1] % 4, other]

    sibling = {"context": 2 * z + 1 - core}
    return device, slot, sibling


def along(first, second, order):
    return (first, second) if order == 0 else (second, first)


NEAR = ((1, 0), (-1, 0), (0, 1), (0, -1))


class Gather:
    def __init__(self, links, mine, whole, own_sem):
        self.links, self.mine, self.whole, self.own_sem = links, mine, whole, own_sem
        self.device, self.slot, self.sibling = plane_place()
        self.rows = mine.shape[0]
        self.beside = {}

    def rows_of(self, order, part):
        start, size = order * (self.rows // 2), self.rows // 2
        if part == 2:
            return 0, self.rows
        if part == 1:
            return start + size // 2, size // 2
        if part == 0:
            return start, size // 2
        return start, size

    def region(self, order, place, part, other=False):
        def make():
            start, size = self.rows_of(order, part)
            base = self.slot(along(*place, order), other) * self.rows + start
            return self.whole.at[pl.ds(pl.multiple_of(base, 16), size)]

        return make

    def push(self, order, place, part, axis, sign):
        step = along(sign, 0, order) if axis == 0 else along(0, sign, order)
        source = self.region(order, place, part)
        if place == (0, 0):
            start, size = self.rows_of(order, part)

            def source():
                return self.mine.at[pl.ds(start, size)]

        came = (place[0] - sign, place[1]) if axis == 0 else (place[0], place[1] - sign)
        return self.links.send(
            source,
            self.region(order, place, part),
            self.device(step),
            self.region(order, came, part),
        )

    def share(self, order, place, part=None):
        source = self.region(order, place, part)
        if part == 2:

            def source():
                return self.mine

        self.beside[order, along(*place, order)] = self.links.send(
            source,
            self.region(order, place, part),
            self.sibling,
            self.region(order, place, part, True),
        )

    def own(self):
        return pltpu.make_async_copy(self.mine, self.region(0, (0, 0), 2)(), self.own_sem)

    def wait_beside(self, places=None):
        for key in list(self.beside):
            if places is None or key[1] in places:
                self.beside.pop(key).wait_recv()

    def steps(self):
        got = {}
        self.own().start()
        for order in range(2):
            for sign in (1, -1):
                got[order, sign] = self.push(order, (0, 0), None, 0, sign)
        for order in range(2):
            for sign in (1, -1):
                got[order, 0, sign] = self.push(order, (0, 0), None, 1, sign)
        self.share(0, (0, 0), 2)
        yield
        for order in range(2):
            for sign in (1, -1):
                got[order, sign].wait_recv()
                got[order, "far", sign] = self.push(
                    order, (-sign, 0), 0 if sign == 1 else 1, 0, sign
                )
            for sign in (1, -1):
                for way in (1, -1):
                    got[order, -sign, way] = self.push(order, (-sign, 0), None, 1, way)
                self.share(order, (-sign, 0))

        def near(i):
            for order in range(2):
                for way in (1, -1):
                    got[order, i, way].wait_recv()
                    got[order, i, "far", way] = self.push(
                        order, (i, -way), 0 if way == 1 else 1, 1, way
                    )
                    self.share(order, (i, -way))

        def far(i):
            for order in range(2):
                for way in (1, -1):
                    got[order, i, "far", way].wait_recv()
                self.share(order, (i, 2))

        yield
        near(0)
        yield
        for order in range(2):
            for sign in (1, -1):
                got[order, "far", sign].wait_recv()
            for way in (1, -1):
                got[order, 2, way] = self.push(order, (2, 0), None, 1, way)
            self.share(order, (2, 0))
        yield
        near(1)
        yield
        near(-1)
        yield
        far(0)
        yield
        near(2)
        yield
        far(1)
        yield
        far(-1)
        yield
        far(2)


def finish_gather(gather, steps, own=True):
    for _ in steps:
        pass
    gather.wait_beside()
    if own:
        gather.own().wait()


GATHER_COPIES = 2 * 20 + 1 + 2 * 15


def gather_body(mine, whole, send_sem, recv_sem, own_sem):
    device, slot, sibling = plane_place()
    greet([device(step) for step in NEAR] + [sibling])
    links = Links(send_sem, recv_sem)
    gather = Gather(links, mine, whole, own_sem)
    finish_gather(gather, gather.steps())
    links.finish()


def plane_gather(array, collective_id):
    return pl.pallas_call(
        gather_body,
        out_shape=jax.ShapeDtypeStruct((32 * array.shape[0],) + array.shape[1:], array.dtype),
        in_specs=[pl.BlockSpec(memory_space=pl.ANY)],
        out_specs=pl.BlockSpec(memory_space=pl.ANY),
        scratch_shapes=[
            pltpu.SemaphoreType.DMA((GATHER_COPIES,)),
            pltpu.SemaphoreType.DMA((GATHER_COPIES,)),
            pltpu.SemaphoreType.DMA,
        ],
        compiler_params=pltpu.CompilerParams(
            collective_id=collective_id, has_side_effects=True, vmem_limit_bytes=56 * MIB
        ),
    )(array)


def add_rows(target, sources, offset, size, chunk=16):
    def step(k, carry):
        base = pl.multiple_of(k * chunk, chunk)
        at = pl.ds(offset + base, chunk)
        total = target[at].astype(F32)
        for source, start in sources:
            total = total + source[pl.ds(start + base, chunk)].astype(F32)
        target[at] = total.astype(target.dtype)
        return carry

    lax.fori_loop(0, size // chunk, step, 0)


SLOTS = (
    (2, 2), (1, 2), (2, 1), (-1, 2), (2, -1), (0, 2), (2, 0),
    (1, 1), (1, -1), (-1, 1), (-1, -1), (0, 1), (1, 0), (0, -1), (-1, 0), (0, 0),
)


class Parts:
    early = len(SLOTS)

    def __init__(self, rows, ref, held, own_sem, columns=None):
        self.rows, self.ref, self.held, self.own_sem = rows, ref, held, own_sem
        self.columns = columns
        self.index = {place: k for k, place in enumerate(SLOTS)}
        self.slot = plane_place()[1]

    def base(self, place):
        return self.index[place] * self.rows

    def slot_rows(self, place, other):
        at = pl.ds(pl.multiple_of(self.slot(place, other) * self.rows, 16), self.rows)
        return self.ref.at[at] if self.columns is None else self.ref.at[at, self.columns]

    def make(self, place):
        at = pl.ds(self.base(place), self.rows)
        k = self.index[place]
        return pltpu.make_async_copy(
            self.slot_rows(place, False), self.held.at[at], self.own_sem.at[k]
        )

    def start(self, place):
        self.make(place).start()

    def wait(self, place):
        self.make(place).wait()

    def other(self, place):
        return self.slot_rows(place, True)


class CrossParts:
    early = 0

    def __init__(self, links, parts, near, came, held):
        self.links, self.parts, self.near, self.came, self.held = links, parts, near, came, held
        self.rows = parts.rows // 4
        self.x = lax.axis_index("tensor")
        self.quarters = [
            pl.multiple_of(lax.rem(self.x + step, 4) * self.rows, self.rows) for step in range(4)
        ]
        self.got = {}

    def begin(self):
        sibling = plane_place()[2]
        self.shares = {}
        for k, place in enumerate(SLOTS):
            self.parts.start(place)
            here = functools.partial(rows_at, self.near, k * self.parts.rows, self.parts.rows)
            there = functools.partial(self.parts.other, place)
            self.shares[place] = self.links.send(there, here, sibling, here)

    def cross(self, places):
        for place in places:
            base = self.parts.base(place)
            self.parts.wait(place)
            self.shares[place].wait_recv()
            add_rows(self.parts.held, [(self.near, base)], base, self.parts.rows)
            self.got[place] = []
            for step in (1, 3, 2):
                source = functools.partial(
                    rows_at, self.parts.held, base + self.quarters[step], self.rows
                )
                at = (self.parts.index[place] * 3 + step - 1) * self.rows
                here = functools.partial(rows_at, self.came, at, self.rows)
                device = {"tensor": lax.rem(self.x + step, 4)}
                self.got[place].append(self.links.send(source, here, device, here))

    def base(self, place):
        return self.parts.index[place] * self.rows

    def wait(self, place):
        for copy in self.got[place]:
            copy.wait_recv()
        mine = self.parts.base(place) + self.quarters[0]
        for start in range(0, self.rows, 16):
            total = self.parts.held[pl.ds(mine + start, 16)].astype(F32)
            for k in range(3):
                at = (self.parts.index[place] * 3 + k) * self.rows + start
                total = total + self.came[pl.ds(at, 16)].astype(F32)
            self.held[pl.ds(self.base(place) + start, 16)] = total.astype(BF16)


CROSS_COPIES = 16 + 48 + 2 * 15


def scatter_steps(links, parts, out_ref, near, landed):
    device, slot, sibling = plane_place()
    rows, held, base = parts.rows, parts.held, parts.base
    half, quarter = rows // 2, rows // 4
    entire = quarter % 16 != 0
    shares = {}

    def launch(first, last):
        for k in range(first, last if near is not None else first):
            place = SLOTS[k]
            parts.start(place)
            here = functools.partial(rows_at, near, k * rows, rows)
            there = functools.partial(parts.other, place)
            shares[place] = links.send(there, here, sibling, here), k

    launch(0, parts.early)
    merged = set()

    def ready(order, place):
        place = along(*place, order)
        if place not in merged:
            merged.add(place)
            parts.wait(place)
            if near is not None:
                copy, k = shares[place]
                copy.wait_recv()
                add_rows(held, [(near, k * rows)], base(place), rows)
        return base(place) + order * half

    room = [0]

    def push(start, size, order, axis, sign):
        step = along(sign, 0, order) if axis == 0 else along(0, sign, order)
        at = room[0]
        room[0] += size
        here = functools.partial(rows_at, landed, at, size)
        source = functools.partial(rows_at, held, start, size)
        return links.send(source, here, device(step), here), at

    got = {}

    def reduce_ring(key, order, axis, places, stage):
        opposite, plus, minus, mine = places
        if stage == 0:
            start = ready(order, opposite)
            if entire:
                got[key, order] = push(start, half, order, axis, 1 - 2 * order)
            else:
                got[key, 0] = push(start, quarter, order, axis, 1)
                got[key, 1] = push(start + quarter, quarter, order, axis, -1)
        if stage == 1:
            for k, place in enumerate((plus, minus)):
                start = ready(order, place)
                if (key, k) in got:
                    copy, at = got[key, k]
                    copy.wait_recv()
                    if entire:
                        add_rows(held, [(landed, at)], start, half)
                    else:
                        add_rows(held, [(landed, at)], start + k * quarter, quarter)
                got[key, 2 + k] = push(start, half, order, axis, 1 - 2 * k)
        if stage == 2:
            start = ready(order, mine)
            sources = []
            for k in (2, 3):
                copy, at = got[key, k]
                copy.wait_recv()
                sources.append((landed, at))
            if axis == 1:
                add_rows(held, sources, start, half)
            else:
                for k in range(half // 16):
                    total = held[pl.ds(start + 16 * k, 16)].astype(F32)
                    for source, at in sources:
                        total = total + source[pl.ds(at + 16 * k, 16)].astype(F32)
                    out_ref[pl.ds(order * half + 16 * k, 16)] = total

    def ring(i, order, stage):
        reduce_ring((order, i), order, 1, [(i, j) for j in (2, 1, -1, 0)], stage)

    def last(order, stage):
        reduce_ring((order, "last"), order, 0, [(i, 0) for i in (2, 1, -1, 0)], stage)

    yield
    for i in (2, 1, -1, 0):
        for order in range(2):
            ring(i, order, 0)
    launch(parts.early, len(SLOTS))
    for i in (2, 1, -1, 0):
        yield
        for order in range(2):
            ring(i, order, 1)
    yield
    for order in range(2):
        ring(2, order, 2)
        last(order, 0)
    yield
    for order in range(2):
        ring(1, order, 2)
        ring(-1, order, 2)
        last(order, 1)
    yield
    for order in range(2):
        ring(0, order, 2)
        last(order, 2)


SCATTER_COPIES = 16 + 2 * 20


def scatter_scratch(rows, columns):
    return [
        pltpu.VMEM((16 * rows, columns), BF16),
        pltpu.VMEM((16 * rows, columns), BF16),
        pltpu.VMEM((15 * rows, columns), BF16),
        pltpu.SemaphoreType.DMA((16,)),
    ]


class TensorSum:
    def __init__(self, links, held, landed, out):
        self.links, self.held, self.landed, self.out = links, held, landed, out
        self.x = lax.axis_index("tensor")
        self.quarter = held.shape[0] // 4

    def device(self, step):
        return {"tensor": (self.x + step) % 4}

    def rows(self, step):
        return pl.ds(pl.multiple_of(((self.x + step) % 4) * self.quarter, 16), self.quarter)

    def part(self, ref, step):
        return ref.at[self.rows(step)]

    def send(self):
        self.got = []
        for step in (1, 3, 2):
            here = functools.partial(
                rows_at, self.landed, (step - 1) * self.quarter, self.quarter
            )
            source = functools.partial(self.part, self.held, step)
            self.got.append(self.links.send(source, here, self.device(step), here))

    def add(self, exact, ready=None):
        for copy in self.got:
            copy.wait_recv()
        mine = self.rows(0)
        total = exact[mine].astype(F32)
        for k in range(3):
            total = total + self.landed[k * self.quarter : (k + 1) * self.quarter].astype(F32)
        if ready is None:
            self.out[mine] = total.astype(BF16)
        else:
            self.out[mine, : total.shape[1]] = total.astype(BF16)
            self.out[mine, total.shape[1] :] = ready[...].astype(BF16)
        here = functools.partial(self.part, self.out, 0)
        self.got = [
            self.links.send(
                here, here, self.device(step), functools.partial(self.part, self.out, -step)
            )
            for step in (1, 3, 2)
        ]

    def wait(self):
        for copy in self.got:
            copy.wait_recv()


TENSOR_COPIES = 6


def tensor_scratch(rows, columns):
    return [pltpu.VMEM((rows, columns), BF16), pltpu.VMEM((rows * 3 // 4, columns), BF16)]


def greet_all(context):
    device, slot, sibling = plane_place()
    x, position = lax.axis_index("tensor"), lax.axis_index("context")
    others = [{"tensor": (x + step) % 4} for step in range(1, 4)]
    if context:
        others += [device(step) for step in NEAR[:2]]
        others += [{"context": (position + step) % 8} for step in range(1, 8)]
    else:
        others += [device(step) for step in NEAR] + [sibling]
    greet(others)


EPSILON = 1e-06
THETA = 1000000.0
PLANE = ("dp", "context")


def dot(a, b, contract):
    return lax.dot_general(a, b, (contract, ((), ())), preferred_element_type=F32)


PAIR = 256
CAPACITY = 32


def rotate(values, cosines, sines):
    return values * cosines + pltpu.roll(values, values.shape[1] // 2, 1) * sines


FRONT_PUMP = (0, 0, 1, 1, 1, 1, 1, 1, 2, 2, 0)


def front_body(
    head, qm_ref, km_ref, vm_ref, om_ref, rm_ref, ag_ref, eg_ref, cot_ref, routes_ref, x_ref,
    cos_ref, sin_ref, qg_ref, kg_ref,
    weights_out, cot_out, raw_out, normed_out, query_out, both_out, attended_out, hidden_out,
    sent_out, gates_out, gains_out,
    packed, marked, weights, part, held, landed, mixed, keys, cosines, sines,
    send_sem, recv_sem, own_sem,
):
    rows, width = x_ref.shape
    query_columns = attended_out.shape[1]
    heads = query_columns // head
    experts = rm_ref.shape[1]
    shard = packed.shape[0]
    scale = head ** (-0.5)
    position = lax.axis_index("context")

    def context_device(step):
        return {"context": (position + step) % 8}

    tables = [
        pltpu.make_async_copy(
            ref.at[pl.ds(pl.multiple_of(position * rows, rows), rows)], to, own_sem.at[4 + k]
        )
        for k, (ref, to) in enumerate(((cos_ref, cosines), (sin_ref, sines)))
    ]
    for copy in tables:
        copy.start()
    last = query_columns * 2 + 2 * head
    packed[:, :query_columns] = qm_ref[...]
    packed[:, query_columns : query_columns + head] = km_ref[...]
    packed[:, query_columns + head : query_columns + 2 * head] = vm_ref[...]
    packed[:, query_columns + 2 * head : last] = om_ref[...]
    row = lax.broadcasted_iota(jnp.int32, (shard, shard), 0)
    column = lax.broadcasted_iota(jnp.int32, (shard, shard), 1)
    downs = [
        jnp.sum(jnp.where(row == column, ref[...].astype(F32), 0.0), axis=1, keepdims=True)
        for ref in (ag_ref, eg_ref)
    ]
    few = jnp.where(column == 0, downs[0], jnp.where(column == 1, downs[1], 0.0))
    packed[:, last : last + experts] = rm_ref[...]
    packed[:, last + experts :] = few.astype(BF16)
    lane = lax.broadcasted_iota(jnp.int32, (rows, 128), 1)
    named = lane == routes_ref[:, 0:1]
    for k in range(1, routes_ref.shape[1]):
        named = jnp.logical_or(named, lane == routes_ref[:, k : k + 1])
    mask = jnp.where(named, 1.0, 0.0)
    marked[:, :width] = cot_ref[...]
    marked[:, width:] = mask.astype(BF16)
    greet_all(True)
    links = Links(send_sem, recv_sem)
    weight_gather = Gather(links, packed, weights, own_sem.at[0])
    cot_gather = Gather(links, marked, cot_out, own_sem.at[1])
    first, second = weight_gather.steps(), cot_gather.steps()
    next(first)

    def pump(point):
        for _ in range(FRONT_PUMP[point]):
            next(second, None)

    values = x_ref[...].astype(F32)
    inverse = lax.rsqrt(jnp.mean(values * values, axis=-1, keepdims=True) + EPSILON)
    for copy in tables:
        copy.wait()
    next(first)
    pump(0)
    for _ in range(2):
        next(first)
    pump(1)
    for _ in range(2):
        next(first)
    pump(2)
    finish_gather(weight_gather, first)
    pump(3)
    store = pltpu.make_async_copy(weights, weights_out, own_sem.at[2])
    store.start()
    take_row = lax.broadcasted_iota(jnp.int32, (8, 128), 0)
    take_lane = lax.broadcasted_iota(jnp.int32, (8, 128), 1)
    take = jnp.where(take_lane == take_row + experts, 1.0, 0.0).astype(BF16)
    gains_out[...] = dot(take, weights[:, last : last + 128], ((1,), (1,)))
    normed_out[...] = (x_ref[...].astype(F32) * inverse * gains_out[0:1]).astype(BF16)

    def turn(values, gain_row):
        inverse = lax.rsqrt(jnp.mean(values * values, axis=-1, keepdims=True) + EPSILON)
        return rotate(values * inverse * gain_row, cosines[...], sines[...])

    normed = normed_out[...]
    raw = dot(normed, weights[:, query_columns : query_columns + 2 * head], ((1,), (0,)))
    raw_out[:, query_columns:] = raw[:, :head]
    keys[:, :head] = turn(raw[:, :head], kg_ref[...].astype(F32)).astype(BF16)
    keys[:, head:] = raw[:, head:].astype(BF16)

    def context_rows(step):
        return both_out.at[pl.ds(pl.multiple_of(((position + step) % 8) * rows, 16), rows)]

    own = pltpu.make_async_copy(keys, context_rows(0), own_sem.at[3])
    own.start()
    got = [
        links.send(
            lambda: keys,
            functools.partial(context_rows, 0),
            context_device(step),
            functools.partial(context_rows, -step),
        )
        for step in range(1, 8)
    ]
    pump(4)
    for part_index in range(4):
        columns = slice(part_index * query_columns // 4, (part_index + 1) * query_columns // 4)
        raw_out[:, columns] = dot(normed, weights[:, columns], ((1,), (0,)))
    for h in range(heads):
        columns = slice(h * head, (h + 1) * head)
        query_out[:, columns] = turn(raw_out[:, columns], qg_ref[...].astype(F32)).astype(BF16)
    pump(5)
    own.wait()
    for copy in got:
        copy.wait_recv()
    pump(6)
    length = 8 * rows
    key_positions = lax.broadcasted_iota(jnp.int32, (rows, length), 1)
    query_positions = lax.broadcasted_iota(jnp.int32, (rows, length), 0) + position * rows
    allowed = key_positions <= query_positions
    for h in range(heads):
        columns = slice(h * head, (h + 1) * head)
        scores = dot(query_out[:, columns], both_out[:, :head], ((1,), (1,))) * scale
        scores = jnp.where(allowed, scores, -1e30)
        terms = jnp.exp(scores - jnp.max(scores, axis=-1, keepdims=True))
        probabilities = (terms * (1.0 / jnp.sum(terms, axis=-1, keepdims=True))).astype(BF16)
        attended_out[:, columns] = dot(probabilities, both_out[:, head:], ((1,), (0,))).astype(BF16)
    pump(7)
    matrix = slice(query_columns + 2 * head, last)
    for block in range(4):
        columns = slice(block * width // 4, (block + 1) * width // 4)
        product = dot(attended_out[...], weights[columns, matrix], ((1,), (1,)))
        part[:, columns] = product
        held[:, columns] = product.astype(BF16)
    total = TensorSum(links, held, landed, mixed)
    total.send()
    pump(8)
    total.add(part)
    pump(9)
    total.wait()
    pump(10)
    hidden = x_ref[...].astype(F32) + mixed[...].astype(F32)
    hidden_out[...] = hidden
    inverse = lax.rsqrt(jnp.mean(hidden * hidden, axis=-1, keepdims=True) + EPSILON)
    sent_out[:, :width] = (hidden * inverse * gains_out[1:2]).astype(BF16)
    logits = dot(sent_out[:, :width], weights[:, last : last + 128], ((1,), (0,)))
    chosen = jnp.where(named, logits, -1e30)
    terms = jnp.where(named, jnp.exp(chosen - jnp.max(chosen, axis=-1, keepdims=True)), 0.0)
    gates = terms / jnp.sum(terms, axis=-1, keepdims=True)
    gates_out[...] = gates
    high = gates.astype(BF16).astype(F32)
    sent_out[:, width:] = (high + pltpu.roll(gates - high, 64, 1)).astype(BF16)
    finish_gather(cot_gather, second)
    store.wait()
    links.finish()


def front(matrices, cotangent, routes, tokens, cosines, sines, query_gain, key_gain, collective_id):
    rows, width = tokens.shape
    head = query_gain.shape[1]
    shard, query_columns = matrices[0].shape
    columns = 2 * query_columns + 2 * head + 128
    copies = 2 * GATHER_COPIES + 7 + TENSOR_COPIES
    vmem = pl.BlockSpec(memory_space=pltpu.VMEM)
    hbm = pl.BlockSpec(memory_space=pl.ANY)
    return pl.pallas_call(
        functools.partial(front_body, head),
        out_shape=[
            jax.ShapeDtypeStruct((32 * shard, columns), BF16),
            jax.ShapeDtypeStruct((32 * rows, width + 128), BF16),
            jax.ShapeDtypeStruct((rows, query_columns + head), F32),
            jax.ShapeDtypeStruct((rows, width), BF16),
            jax.ShapeDtypeStruct((rows, query_columns), BF16),
            jax.ShapeDtypeStruct((8 * rows, 2 * head), BF16),
            jax.ShapeDtypeStruct((rows, query_columns), BF16),
            jax.ShapeDtypeStruct((rows, width), F32),
            jax.ShapeDtypeStruct((rows, width + 128), BF16),
            jax.ShapeDtypeStruct((rows, 128), F32),
            jax.ShapeDtypeStruct((8, width), F32),
        ],
        in_specs=[vmem] * 10 + [hbm] * 2 + [vmem] * 2,
        out_specs=[hbm, hbm] + [vmem] * 9,
        scratch_shapes=[
            pltpu.VMEM((shard, columns), BF16),
            pltpu.VMEM((rows, width + 128), BF16),
            pltpu.VMEM((32 * shard, columns), BF16),
            pltpu.VMEM((rows, width), F32),
            pltpu.VMEM((rows, width), BF16),
            pltpu.VMEM((rows * 3 // 4, width), BF16),
            pltpu.VMEM((rows, width), BF16),
            pltpu.VMEM((rows, 2 * head), BF16),
            pltpu.VMEM((rows, head), F32),
            pltpu.VMEM((rows, head), F32),
            pltpu.SemaphoreType.DMA((copies,)),
            pltpu.SemaphoreType.DMA((copies,)),
            pltpu.SemaphoreType.DMA((6,)),
        ],
        compiler_params=pltpu.CompilerParams(
            collective_id=collective_id, has_side_effects=True, vmem_limit_bytes=56 * MIB
        ),
    )(*matrices, cotangent, routes, tokens, cosines, sines, query_gain, key_gain)


def back_body(
    head, part_ref, weights_ref, mixed_ref, query_ref, both_ref, raw_ref, cos_ref, sin_ref, qg_ref, kg_ref,
    out_ref, grad_out, normed_out,
    held, near, landed, own_sem,
    weights, stacked, grads, chances, slopes, key_terms, key_came, normed, normed_low, normed_came,
    cosines, sines, send_sem, recv_sem, load_sem,
):
    rows, width = mixed_ref.shape
    query_columns = query_ref.shape[1]
    heads = query_columns // head
    scale = head ** (-0.5)
    position = lax.axis_index("context")

    def context_device(step):
        return {"context": (position + step) % 8}

    table_rows = pl.ds(pl.multiple_of(position * rows, rows), rows)
    loads = [
        pltpu.make_async_copy(weights_ref, weights, load_sem.at[0]),
        pltpu.make_async_copy(cos_ref.at[table_rows], cosines, load_sem.at[1]),
        pltpu.make_async_copy(sin_ref.at[table_rows], sines, load_sem.at[2]),
    ]
    for copy in loads:
        copy.start()
    greet_all(True)
    links = Links(send_sem, recv_sem)
    parts = Parts(rows, part_ref, held, own_sem)
    sums = scatter_steps(links, parts, out_ref, near, landed)
    next(sums, None)
    for copy in loads:
        copy.wait()
    matrix = slice(query_columns + 2 * head, 2 * query_columns + 2 * head)
    attended = dot(mixed_ref[...], weights[:, matrix], ((1,), (0,))).astype(BF16)
    for h in range(heads):
        columns, here = slice(h * head, (h + 1) * head), slice(h * rows, (h + 1) * rows)
        stacked[here] = query_ref[:, columns]
        grads[here] = attended[:, columns]
    next(sums, None)
    length = 8 * rows
    key_positions = lax.broadcasted_iota(jnp.int32, (rows, length), 1)
    query_positions = lax.broadcasted_iota(jnp.int32, (rows, length), 0) + position * rows
    allowed = key_positions <= query_positions
    for h in range(heads):
        here = slice(h * rows, (h + 1) * rows)
        scores = dot(stacked[here], both_ref[:, :head], ((1,), (1,))) * scale
        scores = jnp.where(allowed, scores, -1e30)
        terms = jnp.exp(scores - jnp.max(scores, axis=-1, keepdims=True))
        probabilities = terms * (1.0 / jnp.sum(terms, axis=-1, keepdims=True))
        chances[here] = probabilities.astype(BF16)
        grad = dot(grads[here], both_ref[:, head:], ((1,), (1,)))
        delta = jnp.sum(probabilities * grad, axis=-1, keepdims=True)
        slopes[here] = (scale * probabilities * (grad - delta)).astype(BF16)
    key_terms[:, :head] = dot(slopes[...], stacked[...], ((0,), (0,))).astype(BF16)
    key_terms[:, head:] = dot(chances[...], grads[...], ((0,), (0,))).astype(BF16)
    got = []
    for step in range(1, 8):
        source = functools.partial(
            rows_at, key_terms, pl.multiple_of(((position + step) % 8) * rows, 16), rows
        )
        target = functools.partial(rows_at, key_came, (step - 1) * rows, rows)
        got.append(links.send(source, target, context_device(step), target))
    next(sums, None)

    def turn_back(values, grad, gain_row):
        grad = rotate(grad, cosines[...], -sines[...])
        inverse = lax.rsqrt(jnp.mean(values * values, axis=-1, keepdims=True) + EPSILON)
        scaled = grad * gain_row
        mean = jnp.mean(scaled * values, axis=-1, keepdims=True)
        grad_gain = jnp.sum(grad * values * inverse, axis=0, keepdims=True)
        return inverse * scaled - values * (inverse * inverse * inverse) * mean, grad_gain

    query_gain = jnp.zeros((1, head), F32)
    for h in range(heads):
        columns, here = slice(h * head, (h + 1) * head), slice(h * rows, (h + 1) * rows)
        grad = dot(slopes[here], both_ref[:, :head], ((1,), (0,)))
        grad, gain = turn_back(raw_ref[:, columns], grad, qg_ref[...].astype(F32))
        grad_out[:, columns] = grad.astype(BF16)
        query_gain = query_gain + gain
    for copy in got:
        copy.wait_recv()
    mine = key_terms[pl.ds(pl.multiple_of(position * rows, 16), rows)].astype(F32)
    for k in range(7):
        mine = mine + key_came[k * rows : (k + 1) * rows].astype(F32)
    grad, key_gain = turn_back(raw_ref[:, query_columns:], mine[:, :head], kg_ref[...].astype(F32))
    grad_out[:, query_columns : query_columns + head] = grad.astype(BF16)
    grad_out[:, query_columns + head :] = mine[:, head:].astype(BF16)
    next(sums, None)
    for block in range(4):
        columns = slice(block * width // 4, (block + 1) * width // 4)
        product = dot(grad_out[...], weights[columns, : query_columns + 2 * head], ((1,), (1,)))
        normed[:, columns] = product
        normed_low[:, columns] = product.astype(BF16)
    row = lax.broadcasted_iota(jnp.int32, (rows, head), 0)
    gains = jnp.where(row == 0, query_gain, jnp.where(row == 1, key_gain, 0.0))
    normed[:, width:] = gains
    normed_low[:, width:] = gains.astype(BF16)
    total = TensorSum(links, normed_low, normed_came, normed_out)
    total.send()
    next(sums, None)
    total.add(normed)
    for _ in sums:
        pass
    total.wait()
    links.finish()


def back(part, weights, mixed, query_low, both, raw, cosines, sines, query_gain, key_gain, collective_id):
    rows, width = mixed.shape
    head = query_gain.shape[1]
    query_columns = query_low.shape[1]
    stacked = rows * (query_columns // head)
    copies = SCATTER_COPIES + TENSOR_COPIES + 7
    vmem = pl.BlockSpec(memory_space=pltpu.VMEM)
    hbm = pl.BlockSpec(memory_space=pl.ANY)
    return pl.pallas_call(
        functools.partial(back_body, head),
        out_shape=[
            jax.ShapeDtypeStruct((rows, width), F32),
            jax.ShapeDtypeStruct((rows, query_columns + 2 * head), BF16),
            jax.ShapeDtypeStruct((rows, width + head), BF16),
        ],
        in_specs=[hbm, hbm] + [vmem] * 4 + [hbm] * 2 + [vmem] * 2,
        out_specs=[vmem] * 3,
        scratch_shapes=scatter_scratch(rows, width)
        + [
            pltpu.VMEM(weights.shape, BF16),
            pltpu.VMEM((stacked, head), BF16),
            pltpu.VMEM((stacked, head), BF16),
            pltpu.VMEM((stacked, 8 * rows), BF16),
            pltpu.VMEM((stacked, 8 * rows), BF16),
            pltpu.VMEM((8 * rows, 2 * head), BF16),
            pltpu.VMEM((7 * rows, 2 * head), BF16),
            pltpu.VMEM((rows, width + head), F32),
        ]
        + tensor_scratch(rows, width + head)
        + [
            pltpu.VMEM((rows, head), F32),
            pltpu.VMEM((rows, head), F32),
            pltpu.SemaphoreType.DMA((copies,)),
            pltpu.SemaphoreType.DMA((copies,)),
            pltpu.SemaphoreType.DMA((3,)),
        ],
        compiler_params=pltpu.CompilerParams(
            collective_id=collective_id, has_side_effects=True, vmem_limit_bytes=60 * MIB
        ),
    )(part, weights, mixed, query_low, both, raw, cosines, sines, query_gain, key_gain)


class Terms:
    early = 7

    def __init__(self, rows, held, work):
        self.rows, self.held, self.work = rows, held, work
        self.index = {place: k for k, place in enumerate(SLOTS)}
        self.core = lax.rem(lax.axis_index("context"), 2)
        self.slot = plane_place()[1]

    def base(self, place):
        return pl.multiple_of((self.index[place] * 2 + self.core) * self.rows, self.rows)

    def other(self, place):
        start = (self.index[place] * 2 + 1 - self.core) * self.rows
        return rows_at(self.held, pl.multiple_of(start, self.rows), self.rows)

    def start(self, place):
        first = pl.multiple_of((self.slot(place) - self.core) * self.rows, 2 * self.rows)
        self.work(pl.ds(first, 2 * self.rows), self.index[place] * 2 * self.rows)

    def wait(self, place):
        pass


def tail_body(
    head, normed_ref, grad_ref, mixed_ref, attended_ref, few_ref, total_ref, hidden_ref, x_ref, gains_ref,
    sum_ref, state_ref,
    out, tokens_out, output, held, near, landed, few, low, came, summed, send_sem, recv_sem,
):
    rows, width = x_ref.shape
    shard = out.shape[0]
    greet_all(False)
    links = Links(send_sem, recv_sem)
    low[...] = sum_ref[...].astype(BF16)
    terms = TensorSum(links, low, came, summed)
    terms.send()
    values = x_ref[...].astype(F32)
    inverse = lax.rsqrt(jnp.mean(values * values, axis=-1, keepdims=True) + EPSILON)
    grad = total_ref[:, :width].astype(F32)
    scaled = grad * gains_ref[0:1]
    mean = jnp.mean(scaled * values, axis=-1, keepdims=True)
    change = inverse * scaled - values * (inverse * inverse * inverse) * mean
    tokens_out[...] = hidden_ref[...] + change
    gain = jnp.sum(grad * values * inverse, axis=0, keepdims=True)
    entry = lax.broadcasted_iota(jnp.int32, (head, width), 0)
    column = lax.broadcasted_iota(jnp.int32, (head, width), 1)
    each = head * shard // width
    inside = lax.rem(column, shard)
    wanted = jnp.where(inside < each, (column // shard) * each + inside, -1)
    spread = jnp.where(entry == wanted, 1.0, 0.0).astype(BF16)
    heads = dot(total_ref[0:16, width:], spread, ((1,), (0,)))
    at = lax.broadcasted_iota(jnp.int32, (16, width), 0)
    some = few_ref[64:80].astype(F32)
    some = jnp.where(at == 0, gain, some)
    some = jnp.where(at == 2, heads[0:1], jnp.where(at == 3, heads[1:2], some))
    few[...] = few_ref[...]
    few[64:80] = some.astype(BF16)
    first, second = grad_ref.shape[1], attended_ref.shape[1]

    def work(columns, start):
        here = pl.ds(start, 2 * shard)
        held[here, :first] = dot(normed_ref[:, columns].T, grad_ref[...], ((1,), (0,))).astype(BF16)
        held[here, first : first + second] = dot(
            mixed_ref[:, columns].T, attended_ref[...], ((1,), (0,))
        ).astype(BF16)
        held[here, first + second :] = few[:, columns].T

    sums = scatter_steps(links, Terms(shard, held, work), out, near, landed)
    next(sums)
    next(sums)
    terms.add(sum_ref)
    for _ in sums:
        pass
    terms.wait()
    output[...] = state_ref[...] + summed[...].astype(F32)
    links.finish()


def tail(
    normed, grad, mixed, attended, few, total, hidden, tokens, gains, sums, state, head, shard, collective_id
):
    rows, width = tokens.shape
    columns = grad.shape[1] + attended.shape[1] + few.shape[0]
    vmem = pl.BlockSpec(memory_space=pltpu.VMEM)
    return pl.pallas_call(
        functools.partial(tail_body, head),
        out_shape=[
            jax.ShapeDtypeStruct((shard, columns), F32),
            jax.ShapeDtypeStruct((rows, width), F32),
            jax.ShapeDtypeStruct((rows, width), F32),
        ],
        in_specs=[vmem] * 11,
        out_specs=[vmem] * 3,
        scratch_shapes=[
            pltpu.VMEM((32 * shard, columns), BF16),
            pltpu.VMEM((16 * shard, columns), BF16),
            pltpu.VMEM((15 * shard, columns), BF16),
            pltpu.VMEM(few.shape, BF16),
        ]
        + tensor_scratch(rows, width)
        + [
            pltpu.VMEM((rows, width), BF16),
            pltpu.SemaphoreType.DMA((SCATTER_COPIES + TENSOR_COPIES,)),
            pltpu.SemaphoreType.DMA((SCATTER_COPIES + TENSOR_COPIES,)),
        ],
        compiler_params=pltpu.CompilerParams(
            collective_id=collective_id, has_side_effects=True, vmem_limit_bytes=56 * MIB
        ),
    )(normed, grad, mixed, attended, few, total, hidden, tokens, gains, sums, state)


def unpack_body(sizes, total_ref, gg_ref, gu_ref, gd_ref, q_ref, k_ref, v_ref, o_ref, r_ref, *rest):
    ag_ref, eg_ref, qg_ref, kg_ref, gg_out, gu_out, gd_out = rest
    gg_out[...] = gg_ref[...].astype(F32)
    gu_out[...] = gu_ref[...].astype(F32)
    gd_out[...] = gd_ref[...].astype(F32)

    @pl.when(pl.program_id(0) == 0)
    def _():
        query, key, experts, few = sizes
        q_ref[...] = total_ref[:, :query]
        k_ref[...] = total_ref[:, query : query + key]
        v_ref[...] = total_ref[:, query + key : query + 2 * key]
        last = 2 * query + 2 * key
        o_ref[...] = total_ref[:, query + 2 * key : last].T
        block = total_ref[:, last : last + 128]
        r_ref[...] = block[:, :experts]
        turned = block.T
        ag_ref[...] = turned[experts : experts + 1].reshape(ag_ref.shape)
        eg_ref[...] = turned[experts + 1 : experts + 2].reshape(eg_ref.shape)
        qg_ref[...] = turned[experts + 2 : experts + 3, :few].reshape(qg_ref.shape)
        kg_ref[...] = turned[experts + 3 : experts + 4, :few].reshape(kg_ref.shape)


def unpack(total, grads, query, key, experts, few):
    shard = total.shape[0]
    local, units, width = grads[0].shape
    steps = 4

    def whole(*shape):
        return pl.BlockSpec(shape, lambda i: (0,) * len(shape))

    part = pl.BlockSpec((local, units, width // steps), lambda i: (0, 0, i))
    shapes = [
        (shard, query), (shard, key), (shard, key), (query, shard), (shard, experts),
        (1, shard), (1, shard), (1, few), (1, few),
    ]
    return pl.pallas_call(
        functools.partial(unpack_body, (query, key, experts, few)),
        grid=(steps,),
        out_shape=[jax.ShapeDtypeStruct(shape, F32) for shape in shapes]
        + [jax.ShapeDtypeStruct(grad.shape, F32) for grad in grads],
        in_specs=[whole(*total.shape)] + [part] * 3,
        out_specs=[whole(*shape) for shape in shapes] + [part] * 3,
        compiler_params=pltpu.CompilerParams(vmem_limit_bytes=32 * MIB),
    )(total, *grads)


WORK = (
    (0, 0), (1, 0), (-1, 0), (0, 1), (0, -1), (1, 1), (1, -1), (-1, 1),
    (-1, -1), (0, 2), (2, 0), (1, 2), (2, 1), (-1, 2), (2, -1), (2, 2),
)
PUMP = ((2, 0, 1), (0, 0, 1), (1, 0, 1), (0, 1, 0), (1, 0, 1), (1, 0, 0), (1, 0, 0), (0, 0, 0))


def pack_work(axis, which):
    code = 0
    for step in range(len(WORK) // 2):
        code += (WORK[2 * step + which][axis] % 4) * 4**step
    return code


def middle_body(
    mine_ref, grads_ref, wg_ref, wu_ref, wd_ref,
    out_ref, back_ref, rows_ref, given_out, inner_out, slope_g_out, slope_u_out,
    whole, fetched, out_held, back_held, rows, given, turned_g, turned_u, raw_grads,
    picks, spots, inner, slope_g, slope_u,
    send_sem, recv_sem, own_sem, load_sem, store_sem, keep_sem,
):
    local, units, width = wg_ref.shape
    per_pair = 2 * CAPACITY
    steps = len(WORK) // 2
    device, slot, sibling = plane_place()
    y = lax.axis_index("dp")
    z = lax.axis_index("context") // 2
    greet([device(step) for step in NEAR] + [sibling])
    links = Links(send_sem, recv_sem)
    gather = Gather(links, mine_ref, whole, own_sem)
    stages = links.plan(gather.steps())
    for action in stages[0]:
        action()

    def pump(at, point):
        begin = 1 + sum(sum(counts) for counts in PUMP[:at]) + sum(PUMP[at][:point])
        for stage in stages[begin : begin + PUMP[at][point]]:
            for action in stage:
                action()

    def fetch(place, buffer):
        return pltpu.make_async_copy(
            grads_ref.at[pl.ds(pl.multiple_of(place * PAIR, PAIR), PAIR)],
            fetched.at[buffer],
            load_sem.at[buffer],
        )

    fetch(0, 0).start()
    first_expert = (y * 8 + lax.axis_index("context")) * local
    lane = lax.broadcasted_iota(jnp.int32, (1, 128), 1)
    high_lanes = [jnp.where(lane == first_expert + e, 1.0, 0.0) for e in range(local)]
    low_lanes = [jnp.where(lane == first_expert + 64 + e, 1.0, 0.0) for e in range(local)]
    names = lax.broadcasted_iota(jnp.int32, (8, 128), 0)
    names = jnp.where(names < local, names + first_expert, -1)
    marked = jnp.where(lax.broadcasted_iota(jnp.int32, (8, 128), 1) == names, 1.0, 0.0).astype(BF16)
    row = lax.broadcasted_iota(jnp.int32, (128, 128), 0)
    column = lax.broadcasted_iota(jnp.int32, (128, 128), 1)
    before = jnp.where(column < row, 1.0, 0.0).astype(BF16)
    after = jnp.where(row < column, 1.0, 0.0).astype(BF16)
    slots = lax.broadcasted_iota(jnp.int32, (per_pair, PAIR), 0).astype(F32)
    lane_slots = lax.broadcasted_iota(jnp.int32, (PAIR, per_pair), 1).astype(F32)

    def prepare(place, carry):
        buffer = lax.rem(place, 2)

        @pl.when(place < 15)
        def _():
            fetch(place + 1, 1 - buffer).start()

        fetch(place, buffer).wait()
        marks = fetched[buffer, :, width:]
        named = dot(marked, marks, ((1,), (1,)))
        across, down = [], []
        for k in range(2):
            tokens = slice(k * 128, (k + 1) * 128)
            across.append(dot(named[:, tokens].astype(BF16), after, ((1,), (0,))) + float(CAPACITY * k))
            down.append(dot(before, marks[tokens], ((1,), (0,))) + float(CAPACITY * k))
        across = jnp.where(named > 0.5, jnp.concatenate(across, axis=1), -1.0)
        down = jnp.where(marks.astype(F32) > 0.5, jnp.concatenate(down, axis=0), -1.0)
        for e in range(local):
            mine = slice(e * per_pair, (e + 1) * per_pair)
            picks[place, mine] = jnp.where(slots == across[e : e + 1], 1.0, 0.0).astype(BF16)
            wanted = jnp.where(high_lanes[e] > 0.5, down, 0.0)
            spot = jnp.sum(wanted, axis=1, keepdims=True)
            spots[place, :, mine] = jnp.where(lane_slots == spot, 1.0, 0.0).astype(BF16)
        taken = dot(picks[place], fetched[buffer, :, :width], ((1,), (0,))).astype(BF16)
        at = pl.ds(pl.multiple_of(place * per_pair, per_pair), per_pair)
        for e in range(local):
            given[e, at] = taken[e * per_pair : (e + 1) * per_pair]
        return carry

    lax.fori_loop(0, 16, prepare, 0)
    keep = pltpu.make_async_copy(given, given_out, keep_sem.at[0])
    keep.start()
    for e in range(local):
        turned_g[e] = wg_ref[e].T
        turned_u[e] = wu_ref[e].T
        raw_grads[e] = dot(given[e], wd_ref[e], ((1,), (1,)))

    def store(places, which):
        copies = []
        for k, place in enumerate(places):
            here = pl.ds(k * PAIR, PAIR)
            there = pl.ds(pl.multiple_of(place * PAIR, PAIR), PAIR)
            few = pl.ds(pl.multiple_of(place * per_pair, per_pair), per_pair)
            if which == 0:
                copies += [
                    pltpu.make_async_copy(
                        rows.at[:, pl.ds(k * per_pair, per_pair)],
                        rows_ref.at[:, few],
                        store_sem.at[4 + k],
                    ),
                ]
            else:
                copies += [
                    pltpu.make_async_copy(out_held.at[here], out_ref.at[there], store_sem.at[k]),
                    pltpu.make_async_copy(back_held.at[here], back_ref.at[there], store_sem.at[2 + k]),
                ]
        return copies

    def pump_at(step, point):
        for at in range(steps):
            if PUMP[at][point]:

                @pl.when(step == at)
                def _():
                    pump(at, point)

    def work(step, carry):
        codes = [(carry[0], carry[1]), (carry[2], carry[3])]
        places = [
            lax.rem(y + lax.rem(code[0], 4), 4) * 4 + lax.rem(z + lax.rem(code[1], 4), 4)
            for code in codes
        ]
        pump_at(step, 0)
        for at in range(steps):

            @pl.when(step == at)
            def _():
                gather.wait_beside(WORK[2 * at : 2 * at + 2])
                if at == 0:
                    gather.own().wait()

        @pl.when(step > 0)
        def _():
            for copy in store(places, 0):
                copy.wait()

        weights = [[], []]
        for p, place in enumerate(places):
            here = pl.ds(pl.multiple_of(place * PAIR, PAIR), PAIR)
            pick = picks[place]
            gates = dot(pick, whole[here, width:], ((1,), (0,)))
            taken = dot(pick, whole[here, :width], ((1,), (0,))).astype(BF16)
            for e in range(local):
                mine = slice(e * per_pair, (e + 1) * per_pair)
                lanes = high_lanes[e] + low_lanes[e]
                weights[e].append(jnp.sum(gates[mine] * lanes, axis=1, keepdims=True))
                rows[e, p * per_pair : (p + 1) * per_pair] = taken[mine]
        for copy in store(places, 0):
            copy.start()
        pump_at(step, 1)
        sent, returned = [], []
        few = [pl.ds(pl.multiple_of(place * per_pair, per_pair), per_pair) for place in places]
        for e in range(local):
            weight = jnp.concatenate(weights[e], axis=0)
            gate = dot(rows[e], turned_g[e], ((1,), (0,)))
            up = dot(rows[e], turned_u[e], ((1,), (0,)))
            raw = jnp.concatenate([raw_grads[e, at] for at in few], axis=0)
            sigmoid = jax.nn.sigmoid(gate)
            active = gate * sigmoid
            hidden = (active * up * weight).astype(BF16)
            share = jnp.sum(hidden.astype(F32) * raw, axis=1, keepdims=True)
            raw = raw * weight
            grad_gate = (raw * up * sigmoid * (1.0 + gate * (1.0 - sigmoid))).astype(BF16)
            grad_up = (raw * active).astype(BF16)
            for p, at in enumerate(few):
                part = slice(p * per_pair, (p + 1) * per_pair)
                inner[e, at] = hidden[part]
                slope_g[e, at] = grad_gate[part]
                slope_u[e, at] = grad_up[part]
            sent.append(dot(hidden, wd_ref[e], ((1,), (0,))).astype(BF16))
            grad = dot(grad_gate, wg_ref[e], ((1,), (0,)))
            grad = grad + dot(grad_up, wu_ref[e], ((1,), (0,)))
            high = share.astype(BF16).astype(F32)
            lanes = high * high_lanes[e] + (share - high) * low_lanes[e]
            returned.append((grad.astype(BF16), lanes.astype(BF16)))
        pump_at(step, 2)

        @pl.when(step > 0)
        def _():
            for copy in store(places, 1):
                copy.wait()

        for p, place in enumerate(places):
            tokens = slice(p * PAIR, (p + 1) * PAIR)
            mine = slice(p * per_pair, (p + 1) * per_pair)
            spot = spots[place]
            out_rows = jnp.concatenate([s[mine] for s in sent], axis=0)
            out_held[tokens] = dot(spot, out_rows, ((1,), (0,))).astype(BF16)
            back_rows = jnp.concatenate([r[0][mine] for r in returned], axis=0)
            back_held[tokens, :width] = dot(spot, back_rows, ((1,), (0,))).astype(BF16)
            lane_rows = jnp.concatenate([r[1][mine] for r in returned], axis=0)
            back_held[tokens, width:] = dot(spot, lane_rows, ((1,), (0,))).astype(BF16)
        for copy in store(places, 1):
            copy.start()
        return tuple(part // 4 for code in codes for part in code)

    codes = [pack_work(axis, which) for which in range(2) for axis in range(2)]
    lax.fori_loop(0, steps, work, tuple(codes))
    keeps = [
        pltpu.make_async_copy(inner, inner_out, keep_sem.at[1]),
        pltpu.make_async_copy(slope_g, slope_g_out, keep_sem.at[2]),
        pltpu.make_async_copy(slope_u, slope_u_out, keep_sem.at[3]),
    ]
    for copy in keeps:
        copy.start()
    for copy in store([0, 1], 0) + store([0, 1], 1):
        copy.wait()
    for copy in keeps:
        copy.wait()
    keep.wait()
    gather.wait_beside()
    links.finish()


def middle(mine, grads, wg, wu, wd, collective_id):
    local, units, width = wg.shape
    count = grads.shape[0]
    slots = count // 128 * CAPACITY
    step = 2 * PAIR
    vmem = pl.BlockSpec(memory_space=pltpu.VMEM)
    hbm = pl.BlockSpec(memory_space=pl.ANY)
    return pl.pallas_call(
        middle_body,
        out_shape=[
            jax.ShapeDtypeStruct((count, width), BF16),
            jax.ShapeDtypeStruct((count, width + 128), BF16),
        ]
        + [jax.ShapeDtypeStruct((local, slots, width), BF16)] * 2
        + [jax.ShapeDtypeStruct((local, slots, units), BF16)] * 3,
        in_specs=[hbm, hbm] + [vmem] * 3,
        out_specs=[hbm] * 7,
        scratch_shapes=[
            pltpu.VMEM((count, width + 128), BF16),
            pltpu.VMEM((2, PAIR, width + 128), BF16),
            pltpu.VMEM((step, width), BF16),
            pltpu.VMEM((step, width + 128), BF16),
            pltpu.VMEM((local, 4 * CAPACITY, width), BF16),
            pltpu.VMEM((local, slots, width), BF16),
            pltpu.VMEM((local, width, units), BF16),
            pltpu.VMEM((local, width, units), BF16),
            pltpu.VMEM((local, slots, units), F32),
            pltpu.VMEM((count // PAIR, 4 * CAPACITY, PAIR), BF16),
            pltpu.VMEM((count // PAIR, PAIR, 4 * CAPACITY), BF16),
            pltpu.VMEM((local, slots, units), BF16),
            pltpu.VMEM((local, slots, units), BF16),
            pltpu.VMEM((local, slots, units), BF16),
            pltpu.SemaphoreType.DMA((GATHER_COPIES,)),
            pltpu.SemaphoreType.DMA((GATHER_COPIES,)),
            pltpu.SemaphoreType.DMA,
            pltpu.SemaphoreType.DMA((2,)),
            pltpu.SemaphoreType.DMA((6,)),
            pltpu.SemaphoreType.DMA((4,)),
        ],
        compiler_params=pltpu.CompilerParams(
            collective_id=collective_id, has_side_effects=True, vmem_limit_bytes=63 * MIB
        ),
    )(mine, grads, wg, wu, wd)


CROSS_COLUMNS = 640
CROSS_PUMP = (0, 0, 0, 0, 1, 2)


def scatter_sum_body(
    part_ref, rows_ref, given_ref, inner_ref, slope_g_ref, slope_u_ref, weights_ref,
    cot_ref, hidden_ref, sent_ref, gates_ref, gains_ref,
    gg_ref, gu_ref, gd_ref, hidden_out, mixed_out, few_out,
    held, near, landed, own_sem, exact, low, came,
    cross_held, cross_near, cross_landed, cross_sem, cross_came, crossed, cross_exact,
    out, taken, given, inner, slope_g, slope_u, router,
    send_sem, recv_sem, load_sem,
):
    rows = cot_ref.shape[0]
    local, units, width = gg_ref.shape
    greet_all(False)
    links = Links(send_sem, recv_sem)
    split = exact.shape[1]
    parts = Parts(rows, part_ref, held, own_sem, pl.ds(0, split))
    sums = scatter_steps(links, parts, exact, near, landed)
    next(sums)
    parts = Parts(rows, part_ref, cross_held, cross_sem, pl.ds(split, width + 128 - split))
    cross = CrossParts(links, parts, cross_near, cross_came, crossed)
    cross.begin()
    cross_sums = scatter_steps(links, cross, cross_exact, None, cross_landed)
    loads = [
        pltpu.make_async_copy(ref, to, load_sem.at[k])
        for k, (ref, to) in enumerate(
            (
                (inner_ref, inner), (given_ref, given), (slope_g_ref, slope_g), (slope_u_ref, slope_u),
                (rows_ref, taken), (weights_ref.at[:, pl.ds(weights_ref.shape[1] - 128, 128)], router),
            )
        )
    ]
    for copy in loads:
        copy.start()
    next(sums)
    cross.cross(SLOTS[:8])
    next(cross_sums)
    for copy in loads:
        copy.wait()
    jobs = [
        (ref, left, right, e)
        for ref, left, right in ((gd_ref, inner, given), (gg_ref, slope_g, taken), (gu_ref, slope_u, taken))
        for e in range(local)
    ]
    for job, (ref, left, right, e) in enumerate(jobs):
        turned = left[e].T
        for block in range(4):
            columns = slice(block * width // 4, (block + 1) * width // 4)
            ref[e, :, columns] = dot(turned, right[e, :, columns], ((1,), (0,))).astype(BF16)
        next(sums, None)
        if job == 0:
            cross.cross(SLOTS[8:])
        for _ in range(CROSS_PUMP[job]):
            next(cross_sums, None)
    for _ in sums:
        pass
    total = TensorSum(links, low, came, out)
    low[...] = exact[...].astype(BF16)
    total.send()
    for _ in cross_sums:
        pass
    total.add(exact, cross_exact)
    total.wait()
    lane = lax.broadcasted_iota(jnp.int32, (rows, 128), 1)
    shares = out[:, width:].astype(F32)
    shares = jnp.where(lane < 64, shares + pltpu.roll(shares, 64, 1), 0.0)
    shares = shares - gates_ref[...] * jnp.sum(shares, axis=-1, keepdims=True)
    shares = shares.astype(BF16)
    grad = out[:, :width].astype(F32) + dot(shares, router[...], ((1,), (1,)))
    hidden = hidden_ref[...]
    inverse = lax.rsqrt(jnp.mean(hidden * hidden, axis=-1, keepdims=True) + EPSILON)
    scaled = grad * gains_ref[1:2]
    mean = jnp.mean(scaled * hidden, axis=-1, keepdims=True)
    change = inverse * scaled - hidden * (inverse * inverse * inverse) * mean
    result = cot_ref[...].astype(F32) + change
    hidden_out[...] = result
    mixed_out[...] = result.astype(BF16)
    gain = jnp.sum(grad * hidden * inverse, axis=0, keepdims=True)
    few = dot(shares.astype(F32).T.astype(BF16), sent_ref[:, :width], ((1,), (0,)))
    at = lax.broadcasted_iota(jnp.int32, (128, width), 0)
    few_out[...] = jnp.where(at == 65, gain, few).astype(BF16)
    links.finish()


def scatter_sum(
    part, rows_kept, given, inner, slope_g, slope_u, weights, cot, hidden, sent, gates, gains, collective_id
):
    rows, columns = part.shape[0] // 32, part.shape[1]
    local, slots, width = rows_kept.shape
    units = inner.shape[2]
    copies = SCATTER_COPIES + TENSOR_COPIES + CROSS_COPIES
    split = columns - CROSS_COLUMNS
    vmem = pl.BlockSpec(memory_space=pltpu.VMEM)
    hbm = pl.BlockSpec(memory_space=pl.ANY)
    return pl.pallas_call(
        scatter_sum_body,
        out_shape=[jax.ShapeDtypeStruct((local, units, width), BF16)] * 3
        + [
            jax.ShapeDtypeStruct((rows, width), F32),
            jax.ShapeDtypeStruct((rows, width), BF16),
            jax.ShapeDtypeStruct((128, width), BF16),
        ],
        in_specs=[hbm] * 7 + [vmem] * 5,
        out_specs=[vmem] * 6,
        scratch_shapes=scatter_scratch(rows, split)
        + [pltpu.VMEM((rows, split), F32)]
        + tensor_scratch(rows, split)
        + [
            pltpu.VMEM((16 * rows, CROSS_COLUMNS), BF16),
            pltpu.VMEM((16 * rows, CROSS_COLUMNS), BF16),
            pltpu.VMEM((15 * rows // 4, CROSS_COLUMNS), BF16),
            pltpu.SemaphoreType.DMA((16,)),
            pltpu.VMEM((16 * 3 * rows // 4, CROSS_COLUMNS), BF16),
            pltpu.VMEM((16 * rows // 4, CROSS_COLUMNS), BF16),
            pltpu.VMEM((rows // 4, CROSS_COLUMNS), F32),
        ]
        + [pltpu.VMEM((rows, columns), BF16)]
        + [pltpu.VMEM((local, slots, width), BF16)] * 2
        + [pltpu.VMEM((local, slots, units), BF16)] * 3
        + [pltpu.VMEM((width, 128), BF16)]
        + [
            pltpu.SemaphoreType.DMA((copies,)),
            pltpu.SemaphoreType.DMA((copies,)),
            pltpu.SemaphoreType.DMA((6,)),
        ],
        compiler_params=pltpu.CompilerParams(
            collective_id=collective_id, has_side_effects=True, vmem_limit_bytes=63 * MIB
        ),
    )(part, rows_kept, given, inner, slope_g, slope_u, weights, cot, hidden, sent, gates, gains)


def rotary_tables(length, head_size):
    half_size = head_size // 2
    steps = np.arange(half_size, dtype=np.float32) * np.float32(-2.0 * math.log(THETA) / head_size)
    angles = np.arange(length, dtype=np.float32)[:, None] * np.exp(steps)[None, :]
    cosines, sines = np.cos(angles.astype(np.float64)), np.sin(angles.astype(np.float64))
    cosines = np.concatenate([cosines, cosines], axis=1).astype(np.float32)
    return cosines, np.concatenate([-sines, sines], axis=1).astype(np.float32)


def per_device(
    tokens, routes, attention_gain, query_matrix, key_matrix, value_matrix, query_gain, key_gain,
    output_matrix, experts_gain, router_matrix, gate_weight, up_weight, down_weight, cotangent,
):
    tokens, routes, cotangent = tokens[0], routes[0], cotangent[0]
    rows, width = tokens.shape
    expert_count = router_matrix.shape[1]
    local = gate_weight.shape[0]
    head = query_gain.shape[0]
    query_columns, key_columns = query_matrix.shape[1], key_matrix.shape[1]
    shard = query_matrix.shape[0]
    cosines, sines = rotary_tables(8 * rows, head)
    matrices = (
        query_matrix, key_matrix, value_matrix, output_matrix.T, router_matrix,
        attention_gain[None], experts_gain[None],
    )
    weights, all_grads, raw, normed_low, query_flat, both, attended_low, hidden, sent, gates, gains = front(
        matrices, cotangent, routes, tokens, cosines, sines, query_gain[None], key_gain[None], 0
    )
    out_terms, back_terms, *kept = middle(
        sent, all_grads, gate_weight, up_weight, down_weight, 1
    )
    *expert_grads, grad_hidden, grad_mixed, few = scatter_sum(
        back_terms, *kept, weights, cotangent, hidden, sent, gates, gains, 2
    )
    out_sum, grad_qkv, normed_total = back(
        out_terms, weights, grad_mixed, query_flat, both, raw, cosines, sines,
        query_gain[None], key_gain[None], 3,
    )
    total, tokens_grad, output = tail(
        normed_low, grad_qkv, grad_mixed, attended_low, few, normed_total, grad_hidden, tokens, gains,
        out_sum, hidden, head, shard, 4,
    )
    (
        query_grad, key_grad, value_grad, output_grad, router_grad, first_gain, second_gain,
        query_gain_grad, key_gain_grad, gate_grad, up_grad, down_grad,
    ) = unpack(total, expert_grads, query_columns, key_columns, expert_count, head * shard // width)
    return (
        output[None],
        tokens_grad[None],
        first_gain[0],
        query_grad,
        key_grad,
        value_grad,
        query_gain_grad[0],
        key_gain_grad[0],
        output_grad,
        second_gain[0],
        router_grad,
        gate_grad,
        up_grad,
        down_grad,
    )


def solution(mesh):
    plane_rows = P(PLANE)
    both = P(PLANE, "tensor")
    tokens = P("dp", "context", None)
    expert_rows = P(PLANE, "tensor", None)
    router = P(PLANE, None)
    output_matrix = P("tensor", PLANE)
    return jax.shard_map(
        per_device,
        mesh=mesh,
        in_specs=(
            tokens, tokens, plane_rows, both, both, both, P(), P(), output_matrix, plane_rows,
            router, expert_rows, expert_rows, expert_rows, tokens,
        ),
        out_specs=(
            tokens, tokens, plane_rows, both, both, both, plane_rows, plane_rows, output_matrix,
            plane_rows, router, expert_rows, expert_rows, expert_rows,
        ),
        check_vma=False,
    )
```

```python
import functools
import math

import jax
import jax.numpy as jnp
import numpy as np
from jax import lax
from jax.experimental import pallas as pl
from jax.experimental.pallas import tpu as pltpu
from jax.sharding import PartitionSpec as P

MESH = pl.DeviceIdType.MESH
F32 = jnp.float32
BF16 = jnp.bfloat16
MIB = 1 << 20


def rows_at(ref, start, size):
    return ref.at[pl.ds(start, size)]


class Arrival:
    def __init__(self, links, make):
        self.links, self.make = links, make

    def wait_recv(self):
        self.links.act(lambda: self.make().wait_recv())


class Links:
    def __init__(self, send_sem, recv_sem):
        self.send_sem, self.recv_sem = send_sem, recv_sem
        self.copies = []
        self.planned = None

    def act(self, action):
        if self.planned is None:
            action()
        else:
            self.planned.append(action)

    def plan(self, steps):
        stages, done = [], object()
        while True:
            self.planned = []
            more = next(steps, done)
            stages.append(self.planned)
            if more is done:
                self.planned = None
                return stages

    def send(self, source, target, device, arriving):
        index = len(self.copies)

        def copy(start, end):
            return pltpu.make_async_remote_copy(
                src_ref=start(),
                dst_ref=end(),
                send_sem=self.send_sem.at[index],
                recv_sem=self.recv_sem.at[index],
                device_id=device,
                device_id_type=MESH,
            )

        self.act(lambda: copy(source, target).start())
        self.copies.append(lambda: copy(source, target))
        return Arrival(self, lambda: copy(arriving, arriving))

    def finish(self):
        for copy in self.copies:
            copy().wait_send()


def greet(devices):
    barrier = pltpu.get_barrier_semaphore()
    for device in devices:
        pl.semaphore_signal(barrier, inc=1, device_id=device, device_id_type=MESH)
    pl.semaphore_wait(barrier, len(devices))


def plane_place():
    y = lax.axis_index("dp")
    position = lax.axis_index("context")
    z = position // 2
    core = position - 2 * z
    ys = [lax.rem(y + step, 4) for step in range(4)]
    zs = [lax.rem(z + step, 4) for step in range(4)]
    near = {(a, b): {"dp": ys[a], "context": zs[b] * 2 + core} for a in range(4) for b in range(4)}
    slots = {
        (a, b, other): ys[a] * 8 + zs[b] * 2 + (1 - core if other else core)
        for a in range(4)
        for b in range(4)
        for other in (False, True)
    }

    def device(step):
        return near[step[0] % 4, step[1] % 4]

    def slot(step, other=False):
        return slots[step[0] % 4, step[1] % 4, other]

    sibling = {"context": 2 * z + 1 - core}
    return device, slot, sibling


def along(first, second, order):
    return (first, second) if order == 0 else (second, first)


NEAR = ((1, 0), (-1, 0), (0, 1), (0, -1))


class Gather:
    def __init__(self, links, mine, whole, own_sem):
        self.links, self.mine, self.whole, self.own_sem = links, mine, whole, own_sem
        self.device, self.slot, self.sibling = plane_place()
        self.rows = mine.shape[0]
        self.beside = {}

    def rows_of(self, order, part):
        start, size = order * (self.rows // 2), self.rows // 2
        if part == 2:
            return 0, self.rows
        if part == 1:
            return start + size // 2, size // 2
        if part == 0:
            return start, size // 2
        return start, size

    def region(self, order, place, part, other=False):
        def make():
            start, size = self.rows_of(order, part)
            base = self.slot(along(*place, order), other) * self.rows + start
            return self.whole.at[pl.ds(pl.multiple_of(base, 16), size)]

        return make

    def push(self, order, place, part, axis, sign):
        step = along(sign, 0, order) if axis == 0 else along(0, sign, order)
        source = self.region(order, place, part)
        if place == (0, 0):
            start, size = self.rows_of(order, part)

            def source():
                return self.mine.at[pl.ds(start, size)]

        came = (place[0] - sign, place[1]) if axis == 0 else (place[0], place[1] - sign)
        return self.links.send(
            source,
            self.region(order, place, part),
            self.device(step),
            self.region(order, came, part),
        )

    def share(self, order, place, part=None):
        source = self.region(order, place, part)
        if part == 2:

            def source():
                return self.mine

        self.beside[order, along(*place, order)] = self.links.send(
            source,
            self.region(order, place, part),
            self.sibling,
            self.region(order, place, part, True),
        )

    def own(self):
        return pltpu.make_async_copy(self.mine, self.region(0, (0, 0), 2)(), self.own_sem)

    def wait_beside(self, places=None):
        for key in list(self.beside):
            if places is None or key[1] in places:
                self.beside.pop(key).wait_recv()

    def steps(self):
        got = {}
        self.own().start()
        for order in range(2):
            for sign in (1, -1):
                got[order, sign] = self.push(order, (0, 0), None, 0, sign)
        for order in range(2):
            for sign in (1, -1):
                got[order, 0, sign] = self.push(order, (0, 0), None, 1, sign)
        self.share(0, (0, 0), 2)
        yield
        for order in range(2):
            for sign in (1, -1):
                got[order, sign].wait_recv()
                got[order, "far", sign] = self.push(
                    order, (-sign, 0), 0 if sign == 1 else 1, 0, sign
                )
            for sign in (1, -1):
                for way in (1, -1):
                    got[order, -sign, way] = self.push(order, (-sign, 0), None, 1, way)
                self.share(order, (-sign, 0))

        def near(i):
            for order in range(2):
                for way in (1, -1):
                    got[order, i, way].wait_recv()
                    got[order, i, "far", way] = self.push(
                        order, (i, -way), 0 if way == 1 else 1, 1, way
                    )
                    self.share(order, (i, -way))

        def far(i):
            for order in range(2):
                for way in (1, -1):
                    got[order, i, "far", way].wait_recv()
                self.share(order, (i, 2))

        yield
        near(0)
        yield
        for order in range(2):
            for sign in (1, -1):
                got[order, "far", sign].wait_recv()
            for way in (1, -1):
                got[order, 2, way] = self.push(order, (2, 0), None, 1, way)
            self.share(order, (2, 0))
        yield
        near(1)
        yield
        near(-1)
        yield
        far(0)
        yield
        near(2)
        yield
        far(1)
        yield
        far(-1)
        yield
        far(2)


def finish_gather(gather, steps, own=True):
    for _ in steps:
        pass
    gather.wait_beside()
    if own:
        gather.own().wait()


GATHER_COPIES = 2 * 20 + 1 + 2 * 15


def gather_body(mine, whole, send_sem, recv_sem, own_sem):
    device, slot, sibling = plane_place()
    greet([device(step) for step in NEAR] + [sibling])
    links = Links(send_sem, recv_sem)
    gather = Gather(links, mine, whole, own_sem)
    finish_gather(gather, gather.steps())
    links.finish()


def plane_gather(array, collective_id):
    return pl.pallas_call(
        gather_body,
        out_shape=jax.ShapeDtypeStruct((32 * array.shape[0],) + array.shape[1:], array.dtype),
        in_specs=[pl.BlockSpec(memory_space=pl.ANY)],
        out_specs=pl.BlockSpec(memory_space=pl.ANY),
        scratch_shapes=[
            pltpu.SemaphoreType.DMA((GATHER_COPIES,)),
            pltpu.SemaphoreType.DMA((GATHER_COPIES,)),
            pltpu.SemaphoreType.DMA,
        ],
        compiler_params=pltpu.CompilerParams(
            collective_id=collective_id, has_side_effects=True, vmem_limit_bytes=56 * MIB
        ),
    )(array)


def add_rows(target, sources, offset, size, chunk=16):
    def step(k, carry):
        base = pl.multiple_of(k * chunk, chunk)
        at = pl.ds(offset + base, chunk)
        total = target[at].astype(F32)
        for source, start in sources:
            total = total + source[pl.ds(start + base, chunk)].astype(F32)
        target[at] = total.astype(target.dtype)
        return carry

    lax.fori_loop(0, size // chunk, step, 0)


SLOTS = (
    (2, 2), (1, 2), (2, 1), (-1, 2), (2, -1), (0, 2), (2, 0),
    (1, 1), (1, -1), (-1, 1), (-1, -1), (0, 1), (1, 0), (0, -1), (-1, 0), (0, 0),
)


class Parts:
    early = len(SLOTS)

    def __init__(self, rows, ref, held, own_sem, columns=None):
        self.rows, self.ref, self.held, self.own_sem = rows, ref, held, own_sem
        self.columns = columns
        self.index = {place: k for k, place in enumerate(SLOTS)}
        self.slot = plane_place()[1]

    def base(self, place):
        return self.index[place] * self.rows

    def slot_rows(self, place, other):
        at = pl.ds(pl.multiple_of(self.slot(place, other) * self.rows, 16), self.rows)
        return self.ref.at[at] if self.columns is None else self.ref.at[at, self.columns]

    def make(self, place):
        at = pl.ds(self.base(place), self.rows)
        k = self.index[place]
        return pltpu.make_async_copy(
            self.slot_rows(place, False), self.held.at[at], self.own_sem.at[k]
        )

    def start(self, place):
        self.make(place).start()

    def wait(self, place):
        self.make(place).wait()

    def other(self, place):
        return self.slot_rows(place, True)


class CrossParts:
    early = 0

    def __init__(self, links, parts, near, came, held):
        self.links, self.parts, self.near, self.came, self.held = links, parts, near, came, held
        self.rows = parts.rows // 4
        self.x = lax.axis_index("tensor")
        self.quarters = [
            pl.multiple_of(lax.rem(self.x + step, 4) * self.rows, self.rows) for step in range(4)
        ]
        self.got = {}

    def begin(self):
        sibling = plane_place()[2]
        self.shares = {}
        for k, place in enumerate(SLOTS):
            self.parts.start(place)
            here = functools.partial(rows_at, self.near, k * self.parts.rows, self.parts.rows)
            there = functools.partial(self.parts.other, place)
            self.shares[place] = self.links.send(there, here, sibling, here)

    def cross(self, places):
        for place in places:
            base = self.parts.base(place)
            self.parts.wait(place)
            self.shares[place].wait_recv()
            add_rows(self.parts.held, [(self.near, base)], base, self.parts.rows)
            self.got[place] = []
            for step in (1, 3, 2):
                source = functools.partial(
                    rows_at, self.parts.held, base + self.quarters[step], self.rows
                )
                at = (self.parts.index[place] * 3 + step - 1) * self.rows
                here = functools.partial(rows_at, self.came, at, self.rows)
                device = {"tensor": lax.rem(self.x + step, 4)}
                self.got[place].append(self.links.send(source, here, device, here))

    def base(self, place):
        return self.parts.index[place] * self.rows

    def wait(self, place):
        for copy in self.got[place]:
            copy.wait_recv()
        mine = self.parts.base(place) + self.quarters[0]
        for start in range(0, self.rows, 16):
            total = self.parts.held[pl.ds(mine + start, 16)].astype(F32)
            for k in range(3):
                at = (self.parts.index[place] * 3 + k) * self.rows + start
                total = total + self.came[pl.ds(at, 16)].astype(F32)
            self.held[pl.ds(self.base(place) + start, 16)] = total.astype(BF16)


CROSS_COPIES = 16 + 48 + 2 * 15


def scatter_steps(links, parts, out_ref, near, landed):
    device, slot, sibling = plane_place()
    rows, held, base = parts.rows, parts.held, parts.base
    half, quarter = rows // 2, rows // 4
    entire = quarter % 16 != 0
    shares = {}

    def launch(first, last):
        for k in range(first, last if near is not None else first):
            place = SLOTS[k]
            parts.start(place)
            here = functools.partial(rows_at, near, k * rows, rows)
            there = functools.partial(parts.other, place)
            shares[place] = links.send(there, here, sibling, here), k

    launch(0, parts.early)
    merged = set()

    def ready(order, place):
        place = along(*place, order)
        if place not in merged:
            merged.add(place)
            parts.wait(place)
            if near is not None:
                copy, k = shares[place]
                copy.wait_recv()
                add_rows(held, [(near, k * rows)], base(place), rows)
        return base(place) + order * half

    room = [0]

    def push(start, size, order, axis, sign):
        step = along(sign, 0, order) if axis == 0 else along(0, sign, order)
        at = room[0]
        room[0] += size
        here = functools.partial(rows_at, landed, at, size)
        source = functools.partial(rows_at, held, start, size)
        return links.send(source, here, device(step), here), at

    got = {}

    def reduce_ring(key, order, axis, places, stage):
        opposite, plus, minus, mine = places
        if stage == 0:
            start = ready(order, opposite)
            if entire:
                got[key, order] = push(start, half, order, axis, 1 - 2 * order)
            else:
                got[key, 0] = push(start, quarter, order, axis, 1)
                got[key, 1] = push(start + quarter, quarter, order, axis, -1)
        if stage == 1:
            for k, place in enumerate((plus, minus)):
                start = ready(order, place)
                if (key, k) in got:
                    copy, at = got[key, k]
                    copy.wait_recv()
                    if entire:
                        add_rows(held, [(landed, at)], start, half)
                    else:
                        add_rows(held, [(landed, at)], start + k * quarter, quarter)
                got[key, 2 + k] = push(start, half, order, axis, 1 - 2 * k)
        if stage == 2:
            start = ready(order, mine)
            sources = []
            for k in (2, 3):
                copy, at = got[key, k]
                copy.wait_recv()
                sources.append((landed, at))
            if axis == 1:
                add_rows(held, sources, start, half)
            else:
                for k in range(half // 16):
                    total = held[pl.ds(start + 16 * k, 16)].astype(F32)
                    for source, at in sources:
                        total = total + source[pl.ds(at + 16 * k, 16)].astype(F32)
                    out_ref[pl.ds(order * half + 16 * k, 16)] = total

    def ring(i, order, stage):
        reduce_ring((order, i), order, 1, [(i, j) for j in (2, 1, -1, 0)], stage)

    def last(order, stage):
        reduce_ring((order, "last"), order, 0, [(i, 0) for i in (2, 1, -1, 0)], stage)

    yield
    for i in (2, 1, -1, 0):
        for order in range(2):
            ring(i, order, 0)
    launch(parts.early, len(SLOTS))
    for i in (2, 1, -1, 0):
        yield
        for order in range(2):
            ring(i, order, 1)
    yield
    for order in range(2):
        ring(2, order, 2)
        last(order, 0)
    yield
    for order in range(2):
        ring(1, order, 2)
        ring(-1, order, 2)
        last(order, 1)
    yield
    for order in range(2):
        ring(0, order, 2)
        last(order, 2)


SCATTER_COPIES = 16 + 2 * 20


def scatter_scratch(rows, columns):
    return [
        pltpu.VMEM((16 * rows, columns), BF16),
        pltpu.VMEM((16 * rows, columns), BF16),
        pltpu.VMEM((15 * rows, columns), BF16),
        pltpu.SemaphoreType.DMA((16,)),
    ]


class TensorSum:
    def __init__(self, links, held, landed, out):
        self.links, self.held, self.landed, self.out = links, held, landed, out
        self.x = lax.axis_index("tensor")
        self.quarter = held.shape[0] // 4

    def device(self, step):
        return {"tensor": (self.x + step) % 4}

    def rows(self, step):
        return pl.ds(pl.multiple_of(((self.x + step) % 4) * self.quarter, 16), self.quarter)

    def part(self, ref, step):
        return ref.at[self.rows(step)]

    def send(self):
        self.got = []
        for step in (1, 3, 2):
            here = functools.partial(
                rows_at, self.landed, (step - 1) * self.quarter, self.quarter
            )
            source = functools.partial(self.part, self.held, step)
            self.got.append(self.links.send(source, here, self.device(step), here))

    def add(self, exact, ready=None):
        for copy in self.got:
            copy.wait_recv()
        mine = self.rows(0)
        total = exact[mine].astype(F32)
        for k in range(3):
            total = total + self.landed[k * self.quarter : (k + 1) * self.quarter].astype(F32)
        if ready is None:
            self.out[mine] = total.astype(BF16)
        else:
            self.out[mine, : total.shape[1]] = total.astype(BF16)
            self.out[mine, total.shape[1] :] = ready[...].astype(BF16)
        here = functools.partial(self.part, self.out, 0)
        self.got = [
            self.links.send(
                here, here, self.device(step), functools.partial(self.part, self.out, -step)
            )
            for step in (1, 3, 2)
        ]

    def wait(self):
        for copy in self.got:
            copy.wait_recv()


TENSOR_COPIES = 6


def tensor_scratch(rows, columns):
    return [pltpu.VMEM((rows, columns), BF16), pltpu.VMEM((rows * 3 // 4, columns), BF16)]


def greet_all(context):
    device, slot, sibling = plane_place()
    x, position = lax.axis_index("tensor"), lax.axis_index("context")
    others = [{"tensor": (x + step) % 4} for step in range(1, 4)]
    if context:
        others += [device(step) for step in NEAR[:2]]
        others += [{"context": (position + step) % 8} for step in range(1, 8)]
    else:
        others += [device(step) for step in NEAR] + [sibling]
    greet(others)


EPSILON = 1e-06
THETA = 1000000.0
PLANE = ("dp", "context")


def dot(a, b, contract):
    return lax.dot_general(a, b, (contract, ((), ())), preferred_element_type=F32)


PAIR = 256
CAPACITY = 32


def rotate(values, cosines, sines):
    return values * cosines + pltpu.roll(values, values.shape[1] // 2, 1) * sines


FRONT_PUMP = (0, 0, 1, 1, 1, 1, 1, 1, 2, 2, 0)


def front_body(
    head, qm_ref, km_ref, vm_ref, om_ref, rm_ref, ag_ref, eg_ref, cot_ref, routes_ref, x_ref,
    cos_ref, sin_ref, qg_ref, kg_ref,
    weights_out, cot_out, raw_out, normed_out, query_out, both_out, attended_out, hidden_out,
    sent_out, gates_out, gains_out,
    packed, marked, weights, part, held, landed, mixed, keys, cosines, sines,
    send_sem, recv_sem, own_sem,
):
    rows, width = x_ref.shape
    query_columns = attended_out.shape[1]
    heads = query_columns // head
    experts = rm_ref.shape[1]
    shard = packed.shape[0]
    scale = head ** (-0.5)
    position = lax.axis_index("context")

    def context_device(step):
        return {"context": (position + step) % 8}

    tables = [
        pltpu.make_async_copy(
            ref.at[pl.ds(pl.multiple_of(position * rows, rows), rows)], to, own_sem.at[4 + k]
        )
        for k, (ref, to) in enumerate(((cos_ref, cosines), (sin_ref, sines)))
    ]
    for copy in tables:
        copy.start()
    last = query_columns * 2 + 2 * head
    packed[:, :query_columns] = qm_ref[...]
    packed[:, query_columns : query_columns + head] = km_ref[...]
    packed[:, query_columns + head : query_columns + 2 * head] = vm_ref[...]
    packed[:, query_columns + 2 * head : last] = om_ref[...]
    row = lax.broadcasted_iota(jnp.int32, (shard, shard), 0)
    column = lax.broadcasted_iota(jnp.int32, (shard, shard), 1)
    downs = [
        jnp.sum(jnp.where(row == column, ref[...].astype(F32), 0.0), axis=1, keepdims=True)
        for ref in (ag_ref, eg_ref)
    ]
    few = jnp.where(column == 0, downs[0], jnp.where(column == 1, downs[1], 0.0))
    packed[:, last : last + experts] = rm_ref[...]
    packed[:, last + experts :] = few.astype(BF16)
    lane = lax.broadcasted_iota(jnp.int32, (rows, 128), 1)
    named = lane == routes_ref[:, 0:1]
    for k in range(1, routes_ref.shape[1]):
        named = jnp.logical_or(named, lane == routes_ref[:, k : k + 1])
    mask = jnp.where(named, 1.0, 0.0)
    marked[:, :width] = cot_ref[...]
    marked[:, width:] = mask.astype(BF16)
    greet_all(True)
    links = Links(send_sem, recv_sem)
    weight_gather = Gather(links, packed, weights, own_sem.at[0])
    cot_gather = Gather(links, marked, cot_out, own_sem.at[1])
    first, second = weight_gather.steps(), cot_gather.steps()
    next(first)

    def pump(point):
        for _ in range(FRONT_PUMP[point]):
            next(second, None)

    values = x_ref[...].astype(F32)
    inverse = lax.rsqrt(jnp.mean(values * values, axis=-1, keepdims=True) + EPSILON)
    for copy in tables:
        copy.wait()
    next(first)
    pump(0)
    for _ in range(2):
        next(first)
    pump(1)
    for _ in range(2):
        next(first)
    pump(2)
    finish_gather(weight_gather, first)
    pump(3)
    store = pltpu.make_async_copy(weights, weights_out, own_sem.at[2])
    store.start()
    take_row = lax.broadcasted_iota(jnp.int32, (8, 128), 0)
    take_lane = lax.broadcasted_iota(jnp.int32, (8, 128), 1)
    take = jnp.where(take_lane == take_row + experts, 1.0, 0.0).astype(BF16)
    gains_out[...] = dot(take, weights[:, last : last + 128], ((1,), (1,)))
    normed_out[...] = (x_ref[...].astype(F32) * inverse * gains_out[0:1]).astype(BF16)

    def turn(values, gain_row):
        inverse = lax.rsqrt(jnp.mean(values * values, axis=-1, keepdims=True) + EPSILON)
        return rotate(values * inverse * gain_row, cosines[...], sines[...])

    normed = normed_out[...]
    raw = dot(normed, weights[:, query_columns : query_columns + 2 * head], ((1,), (0,)))
    raw_out[:, query_columns:] = raw[:, :head]
    keys[:, :head] = turn(raw[:, :head], kg_ref[...].astype(F32)).astype(BF16)
    keys[:, head:] = raw[:, head:].astype(BF16)

    def context_rows(step):
        return both_out.at[pl.ds(pl.multiple_of(((position + step) % 8) * rows, 16), rows)]

    own = pltpu.make_async_copy(keys, context_rows(0), own_sem.at[3])
    own.start()
    got = [
        links.send(
            lambda: keys,
            functools.partial(context_rows, 0),
            context_device(step),
            functools.partial(context_rows, -step),
        )
        for step in range(1, 8)
    ]
    pump(4)
    for part_index in range(4):
        columns = slice(part_index * query_columns // 4, (part_index + 1) * query_columns // 4)
        raw_out[:, columns] = dot(normed, weights[:, columns], ((1,), (0,)))
    for h in range(heads):
        columns = slice(h * head, (h + 1) * head)
        query_out[:, columns] = turn(raw_out[:, columns], qg_ref[...].astype(F32)).astype(BF16)
    pump(5)
    own.wait()
    for copy in got:
        copy.wait_recv()
    pump(6)
    length = 8 * rows
    key_positions = lax.broadcasted_iota(jnp.int32, (rows, length), 1)
    query_positions = lax.broadcasted_iota(jnp.int32, (rows, length), 0) + position * rows
    allowed = key_positions <= query_positions
    for h in range(heads):
        columns = slice(h * head, (h + 1) * head)
        scores = dot(query_out[:, columns], both_out[:, :head], ((1,), (1,))) * scale
        scores = jnp.where(allowed, scores, -1e30)
        terms = jnp.exp(scores - jnp.max(scores, axis=-1, keepdims=True))
        probabilities = (terms * (1.0 / jnp.sum(terms, axis=-1, keepdims=True))).astype(BF16)
        attended_out[:, columns] = dot(probabilities, both_out[:, head:], ((1,), (0,))).astype(BF16)
    pump(7)
    matrix = slice(query_columns + 2 * head, last)
    for block in range(4):
        columns = slice(block * width // 4, (block + 1) * width // 4)
        product = dot(attended_out[...], weights[columns, matrix], ((1,), (1,)))
        part[:, columns] = product
        held[:, columns] = product.astype(BF16)
    total = TensorSum(links, held, landed, mixed)
    total.send()
    pump(8)
    total.add(part)
    pump(9)
    total.wait()
    pump(10)
    hidden = x_ref[...].astype(F32) + mixed[...].astype(F32)
    hidden_out[...] = hidden
    inverse = lax.rsqrt(jnp.mean(hidden * hidden, axis=-1, keepdims=True) + EPSILON)
    sent_out[:, :width] = (hidden * inverse * gains_out[1:2]).astype(BF16)
    logits = dot(sent_out[:, :width], weights[:, last : last + 128], ((1,), (0,)))
    chosen = jnp.where(named, logits, -1e30)
    terms = jnp.where(named, jnp.exp(chosen - jnp.max(chosen, axis=-1, keepdims=True)), 0.0)
    gates = terms / jnp.sum(terms, axis=-1, keepdims=True)
    gates_out[...] = gates
    high = gates.astype(BF16).astype(F32)
    sent_out[:, width:] = (high + pltpu.roll(gates - high, 64, 1)).astype(BF16)
    finish_gather(cot_gather, second)
    store.wait()
    links.finish()


def front(matrices, cotangent, routes, tokens, cosines, sines, query_gain, key_gain, collective_id):
    rows, width = tokens.shape
    head = query_gain.shape[1]
    shard, query_columns = matrices[0].shape
    columns = 2 * query_columns + 2 * head + 128
    copies = 2 * GATHER_COPIES + 7 + TENSOR_COPIES
    vmem = pl.BlockSpec(memory_space=pltpu.VMEM)
    hbm = pl.BlockSpec(memory_space=pl.ANY)
    return pl.pallas_call(
        functools.partial(front_body, head),
        out_shape=[
            jax.ShapeDtypeStruct((32 * shard, columns), BF16),
            jax.ShapeDtypeStruct((32 * rows, width + 128), BF16),
            jax.ShapeDtypeStruct((rows, query_columns + head), F32),
            jax.ShapeDtypeStruct((rows, width), BF16),
            jax.ShapeDtypeStruct((rows, query_columns), BF16),
            jax.ShapeDtypeStruct((8 * rows, 2 * head), BF16),
            jax.ShapeDtypeStruct((rows, query_columns), BF16),
            jax.ShapeDtypeStruct((rows, width), F32),
            jax.ShapeDtypeStruct((rows, width + 128), BF16),
            jax.ShapeDtypeStruct((rows, 128), F32),
            jax.ShapeDtypeStruct((8, width), F32),
        ],
        in_specs=[vmem] * 10 + [hbm] * 2 + [vmem] * 2,
        out_specs=[hbm, hbm] + [vmem] * 9,
        scratch_shapes=[
            pltpu.VMEM((shard, columns), BF16),
            pltpu.VMEM((rows, width + 128), BF16),
            pltpu.VMEM((32 * shard, columns), BF16),
            pltpu.VMEM((rows, width), F32),
            pltpu.VMEM((rows, width), BF16),
            pltpu.VMEM((rows * 3 // 4, width), BF16),
            pltpu.VMEM((rows, width), BF16),
            pltpu.VMEM((rows, 2 * head), BF16),
            pltpu.VMEM((rows, head), F32),
            pltpu.VMEM((rows, head), F32),
            pltpu.SemaphoreType.DMA((copies,)),
            pltpu.SemaphoreType.DMA((copies,)),
            pltpu.SemaphoreType.DMA((6,)),
        ],
        compiler_params=pltpu.CompilerParams(
            collective_id=collective_id, has_side_effects=True, vmem_limit_bytes=56 * MIB
        ),
    )(*matrices, cotangent, routes, tokens, cosines, sines, query_gain, key_gain)


def back_body(
    head, part_ref, weights_ref, mixed_ref, query_ref, both_ref, raw_ref, cos_ref, sin_ref, qg_ref, kg_ref,
    out_ref, grad_out, normed_out,
    held, near, landed, own_sem,
    weights, stacked, grads, chances, slopes, key_terms, key_came, normed, normed_low, normed_came,
    cosines, sines, send_sem, recv_sem, load_sem,
):
    rows, width = mixed_ref.shape
    query_columns = query_ref.shape[1]
    heads = query_columns // head
    scale = head ** (-0.5)
    position = lax.axis_index("context")

    def context_device(step):
        return {"context": (position + step) % 8}

    table_rows = pl.ds(pl.multiple_of(position * rows, rows), rows)
    loads = [
        pltpu.make_async_copy(weights_ref, weights, load_sem.at[0]),
        pltpu.make_async_copy(cos_ref.at[table_rows], cosines, load_sem.at[1]),
        pltpu.make_async_copy(sin_ref.at[table_rows], sines, load_sem.at[2]),
    ]
    for copy in loads:
        copy.start()
    greet_all(True)
    links = Links(send_sem, recv_sem)
    parts = Parts(rows, part_ref, held, own_sem)
    sums = scatter_steps(links, parts, out_ref, near, landed)
    next(sums, None)
    for copy in loads:
        copy.wait()
    matrix = slice(query_columns + 2 * head, 2 * query_columns + 2 * head)
    attended = dot(mixed_ref[...], weights[:, matrix], ((1,), (0,))).astype(BF16)
    for h in range(heads):
        columns, here = slice(h * head, (h + 1) * head), slice(h * rows, (h + 1) * rows)
        stacked[here] = query_ref[:, columns]
        grads[here] = attended[:, columns]
    next(sums, None)
    length = 8 * rows
    key_positions = lax.broadcasted_iota(jnp.int32, (rows, length), 1)
    query_positions = lax.broadcasted_iota(jnp.int32, (rows, length), 0) + position * rows
    allowed = key_positions <= query_positions
    for h in range(heads):
        here = slice(h * rows, (h + 1) * rows)
        scores = dot(stacked[here], both_ref[:, :head], ((1,), (1,))) * scale
        scores = jnp.where(allowed, scores, -1e30)
        terms = jnp.exp(scores - jnp.max(scores, axis=-1, keepdims=True))
        probabilities = terms * (1.0 / jnp.sum(terms, axis=-1, keepdims=True))
        chances[here] = probabilities.astype(BF16)
        grad = dot(grads[here], both_ref[:, head:], ((1,), (1,)))
        delta = jnp.sum(probabilities * grad, axis=-1, keepdims=True)
        slopes[here] = (scale * probabilities * (grad - delta)).astype(BF16)
    key_terms[:, :head] = dot(slopes[...], stacked[...], ((0,), (0,))).astype(BF16)
    key_terms[:, head:] = dot(chances[...], grads[...], ((0,), (0,))).astype(BF16)
    got = []
    for step in range(1, 8):
        source = functools.partial(
            rows_at, key_terms, pl.multiple_of(((position + step) % 8) * rows, 16), rows
        )
        target = functools.partial(rows_at, key_came, (step - 1) * rows, rows)
        got.append(links.send(source, target, context_device(step), target))
    next(sums, None)

    def turn_back(values, grad, gain_row):
        grad = rotate(grad, cosines[...], -sines[...])
        inverse = lax.rsqrt(jnp.mean(values * values, axis=-1, keepdims=True) + EPSILON)
        scaled = grad * gain_row
        mean = jnp.mean(scaled * values, axis=-1, keepdims=True)
        grad_gain = jnp.sum(grad * values * inverse, axis=0, keepdims=True)
        return inverse * scaled - values * (inverse * inverse * inverse) * mean, grad_gain

    query_gain = jnp.zeros((1, head), F32)
    for h in range(heads):
        columns, here = slice(h * head, (h + 1) * head), slice(h * rows, (h + 1) * rows)
        grad = dot(slopes[here], both_ref[:, :head], ((1,), (0,)))
        grad, gain = turn_back(raw_ref[:, columns], grad, qg_ref[...].astype(F32))
        grad_out[:, columns] = grad.astype(BF16)
        query_gain = query_gain + gain
    for copy in got:
        copy.wait_recv()
    mine = key_terms[pl.ds(pl.multiple_of(position * rows, 16), rows)].astype(F32)
    for k in range(7):
        mine = mine + key_came[k * rows : (k + 1) * rows].astype(F32)
    grad, key_gain = turn_back(raw_ref[:, query_columns:], mine[:, :head], kg_ref[...].astype(F32))
    grad_out[:, query_columns : query_columns + head] = grad.astype(BF16)
    grad_out[:, query_columns + head :] = mine[:, head:].astype(BF16)
    next(sums, None)
    for block in range(4):
        columns = slice(block * width // 4, (block + 1) * width // 4)
        product = dot(grad_out[...], weights[columns, : query_columns + 2 * head], ((1,), (1,)))
        normed[:, columns] = product
        normed_low[:, columns] = product.astype(BF16)
    row = lax.broadcasted_iota(jnp.int32, (rows, head), 0)
    gains = jnp.where(row == 0, query_gain, jnp.where(row == 1, key_gain, 0.0))
    normed[:, width:] = gains
    normed_low[:, width:] = gains.astype(BF16)
    total = TensorSum(links, normed_low, normed_came, normed_out)
    total.send()
    next(sums, None)
    total.add(normed)
    for _ in sums:
        pass
    total.wait()
    links.finish()


def back(part, weights, mixed, query_low, both, raw, cosines, sines, query_gain, key_gain, collective_id):
    rows, width = mixed.shape
    head = query_gain.shape[1]
    query_columns = query_low.shape[1]
    stacked = rows * (query_columns // head)
    copies = SCATTER_COPIES + TENSOR_COPIES + 7
    vmem = pl.BlockSpec(memory_space=pltpu.VMEM)
    hbm = pl.BlockSpec(memory_space=pl.ANY)
    return pl.pallas_call(
        functools.partial(back_body, head),
        out_shape=[
            jax.ShapeDtypeStruct((rows, width), F32),
            jax.ShapeDtypeStruct((rows, query_columns + 2 * head), BF16),
            jax.ShapeDtypeStruct((rows, width + head), BF16),
        ],
        in_specs=[hbm, hbm] + [vmem] * 4 + [hbm] * 2 + [vmem] * 2,
        out_specs=[vmem] * 3,
        scratch_shapes=scatter_scratch(rows, width)
        + [
            pltpu.VMEM(weights.shape, BF16),
            pltpu.VMEM((stacked, head), BF16),
            pltpu.VMEM((stacked, head), BF16),
            pltpu.VMEM((stacked, 8 * rows), BF16),
            pltpu.VMEM((stacked, 8 * rows), BF16),
            pltpu.VMEM((8 * rows, 2 * head), BF16),
            pltpu.VMEM((7 * rows, 2 * head), BF16),
            pltpu.VMEM((rows, width + head), F32),
        ]
        + tensor_scratch(rows, width + head)
        + [
            pltpu.VMEM((rows, head), F32),
            pltpu.VMEM((rows, head), F32),
            pltpu.SemaphoreType.DMA((copies,)),
            pltpu.SemaphoreType.DMA((copies,)),
            pltpu.SemaphoreType.DMA((3,)),
        ],
        compiler_params=pltpu.CompilerParams(
            collective_id=collective_id, has_side_effects=True, vmem_limit_bytes=60 * MIB
        ),
    )(part, weights, mixed, query_low, both, raw, cosines, sines, query_gain, key_gain)


class Terms:
    early = 7

    def __init__(self, rows, held, work):
        self.rows, self.held, self.work = rows, held, work
        self.index = {place: k for k, place in enumerate(SLOTS)}
        self.core = lax.rem(lax.axis_index("context"), 2)
        self.slot = plane_place()[1]

    def base(self, place):
        return pl.multiple_of((self.index[place] * 2 + self.core) * self.rows, self.rows)

    def other(self, place):
        start = (self.index[place] * 2 + 1 - self.core) * self.rows
        return rows_at(self.held, pl.multiple_of(start, self.rows), self.rows)

    def start(self, place):
        first = pl.multiple_of((self.slot(place) - self.core) * self.rows, 2 * self.rows)
        self.work(pl.ds(first, 2 * self.rows), self.index[place] * 2 * self.rows)

    def wait(self, place):
        pass


def tail_body(
    head, normed_ref, grad_ref, mixed_ref, attended_ref, few_ref, total_ref, hidden_ref, x_ref, gains_ref,
    sum_ref,
    out, tokens_out, summed, held, near, landed, few, low, came, send_sem, recv_sem,
):
    rows, width = x_ref.shape
    shard = out.shape[0]
    greet_all(False)
    links = Links(send_sem, recv_sem)
    low[...] = sum_ref[...].astype(BF16)
    terms = TensorSum(links, low, came, summed)
    terms.send()
    values = x_ref[...].astype(F32)
    inverse = lax.rsqrt(jnp.mean(values * values, axis=-1, keepdims=True) + EPSILON)
    grad = total_ref[:, :width].astype(F32)
    scaled = grad * gains_ref[0:1]
    mean = jnp.mean(scaled * values, axis=-1, keepdims=True)
    change = inverse * scaled - values * (inverse * inverse * inverse) * mean
    tokens_out[...] = hidden_ref[...] + change
    gain = jnp.sum(grad * values * inverse, axis=0, keepdims=True)
    entry = lax.broadcasted_iota(jnp.int32, (head, width), 0)
    column = lax.broadcasted_iota(jnp.int32, (head, width), 1)
    each = head * shard // width
    inside = lax.rem(column, shard)
    wanted = jnp.where(inside < each, (column // shard) * each + inside, -1)
    spread = jnp.where(entry == wanted, 1.0, 0.0).astype(BF16)
    heads = dot(total_ref[0:16, width:], spread, ((1,), (0,)))
    at = lax.broadcasted_iota(jnp.int32, (16, width), 0)
    some = few_ref[64:80].astype(F32)
    some = jnp.where(at == 0, gain, some)
    some = jnp.where(at == 2, heads[0:1], jnp.where(at == 3, heads[1:2], some))
    few[...] = few_ref[...]
    few[64:80] = some.astype(BF16)
    first, second = grad_ref.shape[1], attended_ref.shape[1]

    def work(columns, start):
        here = pl.ds(start, 2 * shard)
        held[here, :first] = dot(normed_ref[:, columns].T, grad_ref[...], ((1,), (0,))).astype(BF16)
        held[here, first : first + second] = dot(
            mixed_ref[:, columns].T, attended_ref[...], ((1,), (0,))
        ).astype(BF16)
        held[here, first + second :] = few[:, columns].T

    sums = scatter_steps(links, Terms(shard, held, work), out, near, landed)
    next(sums)
    next(sums)
    terms.add(sum_ref)
    for _ in sums:
        pass
    terms.wait()
    links.finish()


def tail(
    normed, grad, mixed, attended, few, total, hidden, tokens, gains, sums, head, shard, collective_id
):
    rows, width = tokens.shape
    columns = grad.shape[1] + attended.shape[1] + few.shape[0]
    vmem = pl.BlockSpec(memory_space=pltpu.VMEM)
    return pl.pallas_call(
        functools.partial(tail_body, head),
        out_shape=[
            jax.ShapeDtypeStruct((shard, columns), F32),
            jax.ShapeDtypeStruct((rows, width), F32),
            jax.ShapeDtypeStruct((rows, width), BF16),
        ],
        in_specs=[vmem] * 10,
        out_specs=[vmem] * 3,
        scratch_shapes=[
            pltpu.VMEM((32 * shard, columns), BF16),
            pltpu.VMEM((16 * shard, columns), BF16),
            pltpu.VMEM((15 * shard, columns), BF16),
            pltpu.VMEM(few.shape, BF16),
        ]
        + tensor_scratch(rows, width)
        + [
            pltpu.SemaphoreType.DMA((SCATTER_COPIES + TENSOR_COPIES,)),
            pltpu.SemaphoreType.DMA((SCATTER_COPIES + TENSOR_COPIES,)),
        ],
        compiler_params=pltpu.CompilerParams(
            collective_id=collective_id, has_side_effects=True, vmem_limit_bytes=56 * MIB
        ),
    )(normed, grad, mixed, attended, few, total, hidden, tokens, gains, sums)


def unpack_body(
    sizes, total_ref, gg_ref, gu_ref, gd_ref, state_ref, sum_ref, grad_ref, q_ref, k_ref, v_ref, o_ref, r_ref, *rest
):
    ag_ref, eg_ref, qg_ref, kg_ref, gg_out, gu_out, gd_out, output, tokens_out = rest
    output[...] = state_ref[...] + sum_ref[...].astype(F32)
    tokens_out[...] = grad_ref[...]
    gg_out[...] = gg_ref[...].astype(F32)
    gu_out[...] = gu_ref[...].astype(F32)
    gd_out[...] = gd_ref[...].astype(F32)

    @pl.when(pl.program_id(0) == 0)
    def _():
        query, key, experts, few = sizes
        q_ref[...] = total_ref[:, :query]
        k_ref[...] = total_ref[:, query : query + key]
        v_ref[...] = total_ref[:, query + key : query + 2 * key]
        last = 2 * query + 2 * key
        o_ref[...] = total_ref[:, query + 2 * key : last]
        block = total_ref[:, last : last + 128]
        r_ref[...] = block[:, :experts]
        turned = block.T
        ag_ref[...] = turned[experts : experts + 1].reshape(ag_ref.shape)
        eg_ref[...] = turned[experts + 1 : experts + 2].reshape(eg_ref.shape)
        qg_ref[...] = turned[experts + 2 : experts + 3, :few].reshape(qg_ref.shape)
        kg_ref[...] = turned[experts + 3 : experts + 4, :few].reshape(kg_ref.shape)


def unpack(total, grads, state, summed, tokens_grad, query, key, experts, few):
    shard = total.shape[0]
    local, units, width = grads[0].shape
    steps = 4

    def whole(*shape):
        return pl.BlockSpec(shape, lambda i: (0,) * len(shape))

    part = pl.BlockSpec((local, units, width // steps), lambda i: (0, 0, i))
    tokens = pl.BlockSpec((state.shape[0], width // steps), lambda i: (0, i))
    shapes = [
        (shard, query), (shard, key), (shard, key), (shard, query), (shard, experts),
        (1, shard), (1, shard), (1, few), (1, few),
    ]
    return pl.pallas_call(
        functools.partial(unpack_body, (query, key, experts, few)),
        grid=(steps,),
        out_shape=[jax.ShapeDtypeStruct(shape, F32) for shape in shapes]
        + [jax.ShapeDtypeStruct(grad.shape, F32) for grad in grads]
        + [jax.ShapeDtypeStruct(state.shape, F32)] * 2,
        in_specs=[whole(*total.shape)] + [part] * 3 + [tokens] * 3,
        out_specs=[whole(*shape) for shape in shapes] + [part] * 3 + [tokens] * 2,
        compiler_params=pltpu.CompilerParams(vmem_limit_bytes=32 * MIB),
    )(total, *grads, state, summed, tokens_grad)


WORK = (
    (0, 0), (1, 0), (-1, 0), (0, 1), (0, -1), (1, 1), (1, -1), (-1, 1),
    (-1, -1), (0, 2), (2, 0), (1, 2), (2, 1), (-1, 2), (2, -1), (2, 2),
)
PUMP = ((2, 0, 1), (0, 0, 1), (1, 0, 1), (0, 1, 0), (1, 0, 1), (1, 0, 0), (1, 0, 0), (0, 0, 0))


def pack_work(axis, which):
    code = 0
    for step in range(len(WORK) // 2):
        code += (WORK[2 * step + which][axis] % 4) * 4**step
    return code


def middle_body(
    mine_ref, grads_ref, wg_ref, wu_ref, wd_ref,
    out_ref, back_ref, rows_ref, given_out, inner_out, slope_g_out, slope_u_out,
    whole, fetched, out_held, back_held, rows, given, turned_g, turned_u, raw_grads,
    picks, spots, inner, slope_g, slope_u,
    send_sem, recv_sem, own_sem, load_sem, store_sem, keep_sem,
):
    local, units, width = wg_ref.shape
    per_pair = 2 * CAPACITY
    steps = len(WORK) // 2
    device, slot, sibling = plane_place()
    y = lax.axis_index("dp")
    z = lax.axis_index("context") // 2
    greet([device(step) for step in NEAR] + [sibling])
    links = Links(send_sem, recv_sem)
    gather = Gather(links, mine_ref, whole, own_sem)
    stages = links.plan(gather.steps())
    for action in stages[0]:
        action()

    def pump(at, point):
        begin = 1 + sum(sum(counts) for counts in PUMP[:at]) + sum(PUMP[at][:point])
        for stage in stages[begin : begin + PUMP[at][point]]:
            for action in stage:
                action()

    def fetch(place, buffer):
        return pltpu.make_async_copy(
            grads_ref.at[pl.ds(pl.multiple_of(place * PAIR, PAIR), PAIR)],
            fetched.at[buffer],
            load_sem.at[buffer],
        )

    fetch(0, 0).start()
    first_expert = (y * 8 + lax.axis_index("context")) * local
    lane = lax.broadcasted_iota(jnp.int32, (1, 128), 1)
    high_lanes = [jnp.where(lane == first_expert + e, 1.0, 0.0) for e in range(local)]
    low_lanes = [jnp.where(lane == first_expert + 64 + e, 1.0, 0.0) for e in range(local)]
    names = lax.broadcasted_iota(jnp.int32, (8, 128), 0)
    names = jnp.where(names < local, names + first_expert, -1)
    marked = jnp.where(lax.broadcasted_iota(jnp.int32, (8, 128), 1) == names, 1.0, 0.0).astype(BF16)
    row = lax.broadcasted_iota(jnp.int32, (128, 128), 0)
    column = lax.broadcasted_iota(jnp.int32, (128, 128), 1)
    before = jnp.where(column < row, 1.0, 0.0).astype(BF16)
    after = jnp.where(row < column, 1.0, 0.0).astype(BF16)
    slots = lax.broadcasted_iota(jnp.int32, (per_pair, PAIR), 0).astype(F32)
    lane_slots = lax.broadcasted_iota(jnp.int32, (PAIR, per_pair), 1).astype(F32)

    def prepare(place, carry):
        buffer = lax.rem(place, 2)

        @pl.when(place < 15)
        def _():
            fetch(place + 1, 1 - buffer).start()

        fetch(place, buffer).wait()
        marks = fetched[buffer, :, width:]
        named = dot(marked, marks, ((1,), (1,)))
        across, down = [], []
        for k in range(2):
            tokens = slice(k * 128, (k + 1) * 128)
            across.append(dot(named[:, tokens].astype(BF16), after, ((1,), (0,))) + float(CAPACITY * k))
            down.append(dot(before, marks[tokens], ((1,), (0,))) + float(CAPACITY * k))
        across = jnp.where(named > 0.5, jnp.concatenate(across, axis=1), -1.0)
        down = jnp.where(marks.astype(F32) > 0.5, jnp.concatenate(down, axis=0), -1.0)
        for e in range(local):
            mine = slice(e * per_pair, (e + 1) * per_pair)
            picks[place, mine] = jnp.where(slots == across[e : e + 1], 1.0, 0.0).astype(BF16)
            wanted = jnp.where(high_lanes[e] > 0.5, down, 0.0)
            spot = jnp.sum(wanted, axis=1, keepdims=True)
            spots[place, :, mine] = jnp.where(lane_slots == spot, 1.0, 0.0).astype(BF16)
        taken = dot(picks[place], fetched[buffer, :, :width], ((1,), (0,))).astype(BF16)
        at = pl.ds(pl.multiple_of(place * per_pair, per_pair), per_pair)
        for e in range(local):
            given[e, at] = taken[e * per_pair : (e + 1) * per_pair]
        return carry

    lax.fori_loop(0, 16, prepare, 0)
    keep = pltpu.make_async_copy(given, given_out, keep_sem.at[0])
    keep.start()
    for e in range(local):
        turned_g[e] = wg_ref[e].T
        turned_u[e] = wu_ref[e].T
        raw_grads[e] = dot(given[e], wd_ref[e], ((1,), (1,)))

    def store(places, which):
        copies = []
        for k, place in enumerate(places):
            here = pl.ds(k * PAIR, PAIR)
            there = pl.ds(pl.multiple_of(place * PAIR, PAIR), PAIR)
            few = pl.ds(pl.multiple_of(place * per_pair, per_pair), per_pair)
            if which == 0:
                copies += [
                    pltpu.make_async_copy(
                        rows.at[:, pl.ds(k * per_pair, per_pair)],
                        rows_ref.at[:, few],
                        store_sem.at[4 + k],
                    ),
                ]
            else:
                copies += [
                    pltpu.make_async_copy(out_held.at[here], out_ref.at[there], store_sem.at[k]),
                    pltpu.make_async_copy(back_held.at[here], back_ref.at[there], store_sem.at[2 + k]),
                ]
        return copies

    def pump_at(step, point):
        for at in range(steps):
            if PUMP[at][point]:

                @pl.when(step == at)
                def _():
                    pump(at, point)

    def work(step, carry):
        codes = [(carry[0], carry[1]), (carry[2], carry[3])]
        places = [
            lax.rem(y + lax.rem(code[0], 4), 4) * 4 + lax.rem(z + lax.rem(code[1], 4), 4)
            for code in codes
        ]
        pump_at(step, 0)
        for at in range(steps):

            @pl.when(step == at)
            def _():
                gather.wait_beside(WORK[2 * at : 2 * at + 2])
                if at == 0:
                    gather.own().wait()

        @pl.when(step > 0)
        def _():
            for copy in store(places, 0):
                copy.wait()

        weights = [[], []]
        for p, place in enumerate(places):
            here = pl.ds(pl.multiple_of(place * PAIR, PAIR), PAIR)
            pick = picks[place]
            gates = dot(pick, whole[here, width:], ((1,), (0,)))
            taken = dot(pick, whole[here, :width], ((1,), (0,))).astype(BF16)
            for e in range(local):
                mine = slice(e * per_pair, (e + 1) * per_pair)
                lanes = high_lanes[e] + low_lanes[e]
                weights[e].append(jnp.sum(gates[mine] * lanes, axis=1, keepdims=True))
                rows[e, p * per_pair : (p + 1) * per_pair] = taken[mine]
        for copy in store(places, 0):
            copy.start()
        pump_at(step, 1)
        sent, returned = [], []
        few = [pl.ds(pl.multiple_of(place * per_pair, per_pair), per_pair) for place in places]
        for e in range(local):
            weight = jnp.concatenate(weights[e], axis=0)
            gate = dot(rows[e], turned_g[e], ((1,), (0,)))
            up = dot(rows[e], turned_u[e], ((1,), (0,)))
            raw = jnp.concatenate([raw_grads[e, at] for at in few], axis=0)
            sigmoid = jax.nn.sigmoid(gate)
            active = gate * sigmoid
            hidden = (active * up * weight).astype(BF16)
            share = jnp.sum(hidden.astype(F32) * raw, axis=1, keepdims=True)
            raw = raw * weight
            grad_gate = (raw * up * sigmoid * (1.0 + gate * (1.0 - sigmoid))).astype(BF16)
            grad_up = (raw * active).astype(BF16)
            for p, at in enumerate(few):
                part = slice(p * per_pair, (p + 1) * per_pair)
                inner[e, at] = hidden[part]
                slope_g[e, at] = grad_gate[part]
                slope_u[e, at] = grad_up[part]
            sent.append(dot(hidden, wd_ref[e], ((1,), (0,))).astype(BF16))
            grad = dot(grad_gate, wg_ref[e], ((1,), (0,)))
            grad = grad + dot(grad_up, wu_ref[e], ((1,), (0,)))
            high = share.astype(BF16).astype(F32)
            lanes = high * high_lanes[e] + (share - high) * low_lanes[e]
            returned.append((grad.astype(BF16), lanes.astype(BF16)))
        pump_at(step, 2)

        @pl.when(step > 0)
        def _():
            for copy in store(places, 1):
                copy.wait()

        for p, place in enumerate(places):
            tokens = slice(p * PAIR, (p + 1) * PAIR)
            mine = slice(p * per_pair, (p + 1) * per_pair)
            spot = spots[place]
            out_rows = jnp.concatenate([s[mine] for s in sent], axis=0)
            out_held[tokens] = dot(spot, out_rows, ((1,), (0,))).astype(BF16)
            back_rows = jnp.concatenate([r[0][mine] for r in returned], axis=0)
            back_held[tokens, :width] = dot(spot, back_rows, ((1,), (0,))).astype(BF16)
            lane_rows = jnp.concatenate([r[1][mine] for r in returned], axis=0)
            back_held[tokens, width:] = dot(spot, lane_rows, ((1,), (0,))).astype(BF16)
        for copy in store(places, 1):
            copy.start()
        return tuple(part // 4 for code in codes for part in code)

    codes = [pack_work(axis, which) for which in range(2) for axis in range(2)]
    lax.fori_loop(0, steps, work, tuple(codes))
    keeps = [
        pltpu.make_async_copy(inner, inner_out, keep_sem.at[1]),
        pltpu.make_async_copy(slope_g, slope_g_out, keep_sem.at[2]),
        pltpu.make_async_copy(slope_u, slope_u_out, keep_sem.at[3]),
    ]
    for copy in keeps:
        copy.start()
    for copy in store([0, 1], 0) + store([0, 1], 1):
        copy.wait()
    for copy in keeps:
        copy.wait()
    keep.wait()
    gather.wait_beside()
    links.finish()


def middle(mine, grads, wg, wu, wd, collective_id):
    local, units, width = wg.shape
    count = grads.shape[0]
    slots = count // 128 * CAPACITY
    step = 2 * PAIR
    vmem = pl.BlockSpec(memory_space=pltpu.VMEM)
    hbm = pl.BlockSpec(memory_space=pl.ANY)
    return pl.pallas_call(
        middle_body,
        out_shape=[
            jax.ShapeDtypeStruct((count, width), BF16),
            jax.ShapeDtypeStruct((count, width + 128), BF16),
        ]
        + [jax.ShapeDtypeStruct((local, slots, width), BF16)] * 2
        + [jax.ShapeDtypeStruct((local, slots, units), BF16)] * 3,
        in_specs=[hbm, hbm] + [vmem] * 3,
        out_specs=[hbm] * 7,
        scratch_shapes=[
            pltpu.VMEM((count, width + 128), BF16),
            pltpu.VMEM((2, PAIR, width + 128), BF16),
            pltpu.VMEM((step, width), BF16),
            pltpu.VMEM((step, width + 128), BF16),
            pltpu.VMEM((local, 4 * CAPACITY, width), BF16),
            pltpu.VMEM((local, slots, width), BF16),
            pltpu.VMEM((local, width, units), BF16),
            pltpu.VMEM((local, width, units), BF16),
            pltpu.VMEM((local, slots, units), F32),
            pltpu.VMEM((count // PAIR, 4 * CAPACITY, PAIR), BF16),
            pltpu.VMEM((count // PAIR, PAIR, 4 * CAPACITY), BF16),
            pltpu.VMEM((local, slots, units), BF16),
            pltpu.VMEM((local, slots, units), BF16),
            pltpu.VMEM((local, slots, units), BF16),
            pltpu.SemaphoreType.DMA((GATHER_COPIES,)),
            pltpu.SemaphoreType.DMA((GATHER_COPIES,)),
            pltpu.SemaphoreType.DMA,
            pltpu.SemaphoreType.DMA((2,)),
            pltpu.SemaphoreType.DMA((6,)),
            pltpu.SemaphoreType.DMA((4,)),
        ],
        compiler_params=pltpu.CompilerParams(
            collective_id=collective_id, has_side_effects=True, vmem_limit_bytes=63 * MIB
        ),
    )(mine, grads, wg, wu, wd)


CROSS_COLUMNS = 640
CROSS_PUMP = (0, 0, 0, 0, 1, 2)


def scatter_sum_body(
    part_ref, rows_ref, given_ref, inner_ref, slope_g_ref, slope_u_ref, weights_ref,
    cot_ref, hidden_ref, sent_ref, gates_ref, gains_ref,
    gg_ref, gu_ref, gd_ref, hidden_out, mixed_out, few_out,
    held, near, landed, own_sem, exact, low, came,
    cross_held, cross_near, cross_landed, cross_sem, cross_came, crossed, cross_exact,
    out, taken, given, inner, slope_g, slope_u, router,
    send_sem, recv_sem, load_sem,
):
    rows = cot_ref.shape[0]
    local, units, width = gg_ref.shape
    greet_all(False)
    links = Links(send_sem, recv_sem)
    split = exact.shape[1]
    parts = Parts(rows, part_ref, held, own_sem, pl.ds(0, split))
    sums = scatter_steps(links, parts, exact, near, landed)
    next(sums)
    parts = Parts(rows, part_ref, cross_held, cross_sem, pl.ds(split, width + 128 - split))
    cross = CrossParts(links, parts, cross_near, cross_came, crossed)
    cross.begin()
    cross_sums = scatter_steps(links, cross, cross_exact, None, cross_landed)
    loads = [
        pltpu.make_async_copy(ref, to, load_sem.at[k])
        for k, (ref, to) in enumerate(
            (
                (inner_ref, inner), (given_ref, given), (slope_g_ref, slope_g), (slope_u_ref, slope_u),
                (rows_ref, taken), (weights_ref.at[:, pl.ds(weights_ref.shape[1] - 128, 128)], router),
            )
        )
    ]
    for copy in loads:
        copy.start()
    next(sums)
    cross.cross(SLOTS[:8])
    next(cross_sums)
    for copy in loads:
        copy.wait()
    jobs = [
        (ref, left, right, e)
        for ref, left, right in ((gd_ref, inner, given), (gg_ref, slope_g, taken), (gu_ref, slope_u, taken))
        for e in range(local)
    ]
    for job, (ref, left, right, e) in enumerate(jobs):
        turned = left[e].T
        for block in range(4):
            columns = slice(block * width // 4, (block + 1) * width // 4)
            ref[e, :, columns] = dot(turned, right[e, :, columns], ((1,), (0,))).astype(BF16)
        next(sums, None)
        if job == 0:
            cross.cross(SLOTS[8:])
        for _ in range(CROSS_PUMP[job]):
            next(cross_sums, None)
    for _ in sums:
        pass
    total = TensorSum(links, low, came, out)
    low[...] = exact[...].astype(BF16)
    total.send()
    for _ in cross_sums:
        pass
    total.add(exact, cross_exact)
    total.wait()
    lane = lax.broadcasted_iota(jnp.int32, (rows, 128), 1)
    shares = out[:, width:].astype(F32)
    shares = jnp.where(lane < 64, shares + pltpu.roll(shares, 64, 1), 0.0)
    shares = shares - gates_ref[...] * jnp.sum(shares, axis=-1, keepdims=True)
    shares = shares.astype(BF16)
    grad = out[:, :width].astype(F32) + dot(shares, router[...], ((1,), (1,)))
    hidden = hidden_ref[...]
    inverse = lax.rsqrt(jnp.mean(hidden * hidden, axis=-1, keepdims=True) + EPSILON)
    scaled = grad * gains_ref[1:2]
    mean = jnp.mean(scaled * hidden, axis=-1, keepdims=True)
    change = inverse * scaled - hidden * (inverse * inverse * inverse) * mean
    result = cot_ref[...].astype(F32) + change
    hidden_out[...] = result
    mixed_out[...] = result.astype(BF16)
    gain = jnp.sum(grad * hidden * inverse, axis=0, keepdims=True)
    few = dot(shares.astype(F32).T.astype(BF16), sent_ref[:, :width], ((1,), (0,)))
    at = lax.broadcasted_iota(jnp.int32, (128, width), 0)
    few_out[...] = jnp.where(at == 65, gain, few).astype(BF16)
    links.finish()


def scatter_sum(
    part, rows_kept, given, inner, slope_g, slope_u, weights, cot, hidden, sent, gates, gains, collective_id
):
    rows, columns = part.shape[0] // 32, part.shape[1]
    local, slots, width = rows_kept.shape
    units = inner.shape[2]
    copies = SCATTER_COPIES + TENSOR_COPIES + CROSS_COPIES
    split = columns - CROSS_COLUMNS
    vmem = pl.BlockSpec(memory_space=pltpu.VMEM)
    hbm = pl.BlockSpec(memory_space=pl.ANY)
    return pl.pallas_call(
        scatter_sum_body,
        out_shape=[jax.ShapeDtypeStruct((local, units, width), BF16)] * 3
        + [
            jax.ShapeDtypeStruct((rows, width), F32),
            jax.ShapeDtypeStruct((rows, width), BF16),
            jax.ShapeDtypeStruct((128, width), BF16),
        ],
        in_specs=[hbm] * 7 + [vmem] * 5,
        out_specs=[vmem] * 6,
        scratch_shapes=scatter_scratch(rows, split)
        + [pltpu.VMEM((rows, split), F32)]
        + tensor_scratch(rows, split)
        + [
            pltpu.VMEM((16 * rows, CROSS_COLUMNS), BF16),
            pltpu.VMEM((16 * rows, CROSS_COLUMNS), BF16),
            pltpu.VMEM((15 * rows // 4, CROSS_COLUMNS), BF16),
            pltpu.SemaphoreType.DMA((16,)),
            pltpu.VMEM((16 * 3 * rows // 4, CROSS_COLUMNS), BF16),
            pltpu.VMEM((16 * rows // 4, CROSS_COLUMNS), BF16),
            pltpu.VMEM((rows // 4, CROSS_COLUMNS), F32),
        ]
        + [pltpu.VMEM((rows, columns), BF16)]
        + [pltpu.VMEM((local, slots, width), BF16)] * 2
        + [pltpu.VMEM((local, slots, units), BF16)] * 3
        + [pltpu.VMEM((width, 128), BF16)]
        + [
            pltpu.SemaphoreType.DMA((copies,)),
            pltpu.SemaphoreType.DMA((copies,)),
            pltpu.SemaphoreType.DMA((6,)),
        ],
        compiler_params=pltpu.CompilerParams(
            collective_id=collective_id, has_side_effects=True, vmem_limit_bytes=63 * MIB
        ),
    )(part, rows_kept, given, inner, slope_g, slope_u, weights, cot, hidden, sent, gates, gains)


def rotary_tables(length, head_size):
    half_size = head_size // 2
    steps = np.arange(half_size, dtype=np.float32) * np.float32(-2.0 * math.log(THETA) / head_size)
    angles = np.arange(length, dtype=np.float32)[:, None] * np.exp(steps)[None, :]
    cosines, sines = np.cos(angles.astype(np.float64)), np.sin(angles.astype(np.float64))
    cosines = np.concatenate([cosines, cosines], axis=1).astype(np.float32)
    return cosines, np.concatenate([-sines, sines], axis=1).astype(np.float32)


def per_device(
    tokens, routes, attention_gain, query_matrix, key_matrix, value_matrix, query_gain, key_gain,
    output_matrix, experts_gain, router_matrix, gate_weight, up_weight, down_weight, cotangent,
):
    tokens, routes, cotangent = tokens[0], routes[0], cotangent[0]
    rows, width = tokens.shape
    expert_count = router_matrix.shape[1]
    local = gate_weight.shape[0]
    head = query_gain.shape[0]
    query_columns, key_columns = query_matrix.shape[1], key_matrix.shape[1]
    shard = query_matrix.shape[0]
    cosines, sines = rotary_tables(8 * rows, head)
    matrices = (
        query_matrix, key_matrix, value_matrix, output_matrix.T, router_matrix,
        attention_gain[None], experts_gain[None],
    )
    weights, all_grads, raw, normed_low, query_flat, both, attended_low, hidden, sent, gates, gains = front(
        matrices, cotangent, routes, tokens, cosines, sines, query_gain[None], key_gain[None], 0
    )
    out_terms, back_terms, *kept = middle(
        sent, all_grads, gate_weight, up_weight, down_weight, 1
    )
    *expert_grads, grad_hidden, grad_mixed, few = scatter_sum(
        back_terms, *kept, weights, cotangent, hidden, sent, gates, gains, 2
    )
    out_sum, grad_qkv, normed_total = back(
        out_terms, weights, grad_mixed, query_flat, both, raw, cosines, sines,
        query_gain[None], key_gain[None], 3,
    )
    total, tokens_part, summed = tail(
        normed_low, grad_qkv, grad_mixed, attended_low, few, normed_total, grad_hidden, tokens, gains,
        out_sum, head, shard, 4,
    )
    (
        query_grad, key_grad, value_grad, output_grad, router_grad, first_gain, second_gain,
        query_gain_grad, key_gain_grad, gate_grad, up_grad, down_grad, output, tokens_grad,
    ) = unpack(
        total, expert_grads, hidden, summed, tokens_part,
        query_columns, key_columns, expert_count, head * shard // width,
    )
    return (
        output[None],
        tokens_grad[None],
        first_gain[0],
        query_grad,
        key_grad,
        value_grad,
        query_gain_grad[0],
        key_gain_grad[0],
        output_grad.T,
        second_gain[0],
        router_grad,
        gate_grad,
        up_grad,
        down_grad,
    )


def solution(mesh):
    plane_rows = P(PLANE)
    both = P(PLANE, "tensor")
    tokens = P("dp", "context", None)
    expert_rows = P(PLANE, "tensor", None)
    router = P(PLANE, None)
    output_matrix = P("tensor", PLANE)
    return jax.shard_map(
        per_device,
        mesh=mesh,
        in_specs=(
            tokens, tokens, plane_rows, both, both, both, P(), P(), output_matrix, plane_rows,
            router, expert_rows, expert_rows, expert_rows, tokens,
        ),
        out_specs=(
            tokens, tokens, plane_rows, both, both, both, plane_rows, plane_rows, output_matrix,
            plane_rows, router, expert_rows, expert_rows, expert_rows,
        ),
        check_vma=False,
    )
```
